32 devices in a mesh: section: 4 (over z), expert: 4 (over y, x), dp: 2 (over core).
Axes of the slice: x: 2, y: 2, z: 4, core: 2. Of those that a mesh axis runs over, the one named last changes fastest.
Arguments:
- x_fwd: bfloat16 [4, 512, 3584], P('section', ('expert', 'dp')), may hold values from -6 to 6
- ids_fwd: int32 [4, 512, 2], P('section', ('expert', 'dp')), may hold values from 0 to 3, all different within a row; in each aligned block of 64 rows (0 to 63, 64 to 127, ..., all dimensions but the last counted through in order) at most 40 rows name the same one
- route_fwd: float32 [4, 512, 2], P('section', ('expert', 'dp')), may hold values from 0.1 to 1
- x_bwd: bfloat16 [4, 512, 3584], P('section', ('expert', 'dp')), may hold values from -6 to 6
- ids_bwd: int32 [4, 512, 2], P('section', ('expert', 'dp')), may hold values from 0 to 3, all different within a row; in each aligned block of 64 rows (0 to 63, 64 to 127, ..., all dimensions but the last counted through in order) at most 40 rows name the same one
- route_bwd: float32 [4, 512, 2], P('section', ('expert', 'dp')), may hold values from 0.1 to 1
- dy_bwd: bfloat16 [4, 512, 3584], P('section', ('expert', 'dp')), may hold values from -3 to 3
- w_gate: bfloat16 [4, 4, 3584, 1024], P('section', 'expert', 'dp'), may hold values from -0.09375 to 0.09375
- w_up: bfloat16 [4, 4, 3584, 1024], P('section', 'expert', 'dp'), may hold values from -0.09375 to 0.09375
- w_down: bfloat16 [4, 4, 1024, 3584], P('section', 'expert', None, 'dp'), may hold values from -0.1875 to 0.1875
Outputs:
- y_next: bfloat16 [4, 512, 3584], P('section', ('expert', 'dp'))
- dx_next: bfloat16 [4, 512, 3584], P('section', ('expert', 'dp'))
- grad_gate: bfloat16 [4, 4, 3584, 1024], P('section', 'expert', 'dp')
- grad_up: bfloat16 [4, 4, 3584, 1024], P('section', 'expert', 'dp')
- grad_down: bfloat16 [4, 4, 1024, 3584], P('section', 'expert', None, 'dp')
The draws below stay inside these ranges and needn't reach their ends.
Inputs may be any that keep to these rules, and one draw needn't show every extreme that they name: `ids_fwd`: each row names 2 different experts. In each aligned block of 64 rows of a section (the rows of one device) no expert is named by more than 40 rows, and in some block one expert is named by exactly 40 rows. `ids_bwd`: each row names 2 different experts. In each aligned block of 64 rows of a section (the rows of one device) no expert is named by more than 40 rows, and in some block one expert is named by exactly 40 rows.
All inputs are finite; a program needn't handle non-finite values.
Results may differ from the reference program's by a relative error of at most 0.0065.
Values may be sent and summed in bfloat16 or wider, within the bound.
No kernel may reach another device: no remote copies, remote signals or barrier semaphores. Data moves between devices by JAX's collectives and lax.ppermute only.
A program may use at most 128 MiB of HBM per device.

```python
import math
import jax
import jax.numpy as jnp
import numpy as np
from jax import lax

D = 3584
FF = 1024
TOP = 2
TOK_DEV = 64
SECTIONS = 4
GROUP = 1
EXPERTS = 4
FS = 1024
CAP = 40
MB = 512
N_EXPERT = 4
N_DP = 2


def block_scale(own_key, extent, cuts, least, top_value):
    def one(dim, parts):
        draws = jax.random.uniform(jax.random.fold_in(jax.random.fold_in(own_key, 6), dim), (parts,), jnp.float32, least / len(cuts), top_value / len(cuts))
        return jnp.repeat(jnp.exp(draws), extent[dim] // parts).reshape((-1,) + (1,) * (len(extent) - dim - 1))

    level = one(*cuts[0])
    for cut in cuts[1:]:
        level = level * one(*cut)
    return level


def shared_out(key, own, number, rows, count, top, limit, lean):
    sequence = jax.random.permutation(key, count)
    heavy_load, usual = shares(count, rows * top, limit, lean, True), shares(count, rows * top, limit, lean, False)
    places = jnp.arange(count)

    def named(lengths, offset_by):
        used = int((lengths > 0).sum())
        fixed = max(1, used // 4)
        passed = fixed + (places - fixed + offset_by * (used - fixed)) % max(1, count - fixed)
        return jnp.zeros((count,), jnp.int32).at[sequence[jnp.where(places < fixed, places, passed)]].set(jnp.asarray(lengths, jnp.int32))

    lengths = jnp.where(number % 4 == 0, named(heavy_load, number // 4), named(usual, number - number // 4 - 1))
    mixed = jax.random.permutation(jax.random.fold_in(own, 3), count)
    source_of, taker = mixed[0:count // 2 * 2:2], mixed[1:count // 2 * 2:2]
    room = jnp.minimum(lengths[source_of] - 1, limit - lengths[taker]) // 2
    room = jnp.where((source_of == sequence[0]) | (taker == sequence[0]) | (lengths[taker] == 0), 0, jnp.maximum(room, 0))
    passed = jax.random.randint(jax.random.fold_in(own, 4), (count // 2,), 0, 1 << 20) % (room + 1)
    lengths = lengths.at[source_of].add(-passed).at[taker].add(passed)
    items = jnp.searchsorted(jnp.cumsum(lengths), jnp.arange(rows * top), side="right").astype(jnp.int32)
    listing = items.reshape(top, rows).T
    listing = listing[jax.random.permutation(jax.random.fold_in(own, 1), rows)]
    offset_by = jax.random.randint(jax.random.fold_in(own, 2), (rows, 1), 0, top)
    return jnp.take_along_axis(listing, (jnp.arange(top)[None, :] + offset_by) % top, axis=1)


def shares(count, total, reach, slope, full):
    loads = [(1 << 20) // math.isqrt(grade ** slope) + 1 for grade in range(1, count + 1)]
    largest = reach if full else min(reach, max(-(-total // count), total * loads[0] // sum(loads)))
    least = 1 if total - largest >= count - 1 else 0
    holding, spare = [largest] + [least] * (count - 1), total - largest - least * (count - 1)
    while spare > 0:
        free = [i for i in range(1, count) if holding[i] < largest] or [i for i in range(1, count) if holding[i] < reach]
        mass, remaining = sum([loads[i] for i in free]), spare
        for i in free:
            extra = min(reach - holding[i], max(1, remaining * loads[i] // mass), spare)
            holding[i] = holding[i] + extra
            spare = spare - extra
    return np.array(holding)


def centred(key, shape, deviation, bound, cuts=(), held_as=jnp.bfloat16):
    result = jax.random.normal(key, shape, jnp.float32) * deviation
    if len(cuts) > 0:
        result = block_scale(key, shape, cuts, -0.22, 0.18) * result
    return jnp.clip(result, min=-bound, max=bound).astype(held_as)


def setup_inputs(seed: int = 0) -> dict:
    arg_keys = jax.random.split(jax.random.key(seed), 11)
    x_fwd = centred(arg_keys[0], (SECTIONS, MB, D), 1.0, 6.0, ((0, 4), (1, 8)))
    ids_fwd_keys = jax.random.split(jax.random.fold_in(arg_keys[1], 1), SECTIONS * MB // TOK_DEV)
    ids_fwd_turns = jax.random.permutation(jax.random.fold_in(arg_keys[1], 3), SECTIONS * MB // TOK_DEV)
    ids_fwd = jax.vmap(lambda own, number: shared_out(jax.random.fold_in(arg_keys[1], 2), own, number, TOK_DEV, EXPERTS, TOP, CAP, 2))(ids_fwd_keys, ids_fwd_turns).reshape((SECTIONS, MB, TOP))
    route_fwd = jnp.clip(0.1 + 0.9 * jax.random.uniform(arg_keys[2], (SECTIONS, MB, TOP), jnp.float32) ** block_scale(arg_keys[2], (SECTIONS, MB, TOP), ((0, 4), (1, 8)), -0.2, 0.2), 0.1, 1.0)
    x_bwd = centred(arg_keys[3], (SECTIONS, MB, D), 1.0, 6.0, ((0, 4), (1, 8)))
    ids_bwd_keys = jax.random.split(jax.random.fold_in(arg_keys[4], 1), SECTIONS * MB // TOK_DEV)
    ids_bwd_turns = jax.random.permutation(jax.random.fold_in(arg_keys[4], 3), SECTIONS * MB // TOK_DEV)
    ids_bwd = jax.vmap(lambda own, number: shared_out(jax.random.fold_in(arg_keys[4], 2), own, number, TOK_DEV, EXPERTS, TOP, CAP, 2))(ids_bwd_keys, ids_bwd_turns).reshape((SECTIONS, MB, TOP))
    route_bwd = jnp.clip(0.1 + 0.9 * jax.random.uniform(arg_keys[5], (SECTIONS, MB, TOP), jnp.float32) ** block_scale(arg_keys[5], (SECTIONS, MB, TOP), ((0, 4), (1, 8)), -0.2, 0.2), 0.1, 1.0)
    dy_bwd = centred(arg_keys[6], (SECTIONS, MB, D), 0.5, 3.0, ((0, 4), (1, 8)))
    w_gate = centred(arg_keys[7], (SECTIONS, EXPERTS * GROUP, D, FS), D ** -0.5, 0.09375, ((0, 4), (1, 4), (2, 2)))
    w_up = centred(arg_keys[8], (SECTIONS, EXPERTS * GROUP, D, FS), D ** -0.5, 0.09375, ((0, 4), (1, 4), (2, 2)))
    w_down = centred(arg_keys[9], (SECTIONS, EXPERTS * GROUP, FS, D), FF ** -0.5, 0.1875, ((0, 4), (1, 4), (3, 2)))
    return dict(x_fwd=x_fwd, ids_fwd=ids_fwd, route_fwd=route_fwd, x_bwd=x_bwd, ids_bwd=ids_bwd, route_bwd=route_bwd, dy_bwd=dy_bwd, w_gate=w_gate, w_up=w_up, w_down=w_down)


def pair_positions(ids):
    blocks = ids.shape[0] // TOK_DEV
    flat = ids.reshape(blocks, TOK_DEV * TOP)
    onehot = (flat[:, :, None] == jnp.arange(EXPERTS, dtype=jnp.int32)[None, None, :]).astype(jnp.int32)
    position = jnp.sum(jnp.cumsum(onehot, axis=1) * onehot, axis=2) - 1
    block_base = (jnp.arange(blocks, dtype=jnp.int32) * CAP)[:, None]
    return (block_base + position).astype(jnp.int32).reshape(ids.shape[0], TOP)


def gather_rows(values, target, slot_total):
    buffer = jnp.zeros((slot_total + 1, values.shape[1]), values.dtype)
    return buffer.at[target].set(values)[:slot_total]


def slab_sum(products):
    total = None
    for left, right in products:
        term = jnp.einsum("rgf,gfd->grd", left.reshape(left.shape[0], GROUP, FS).astype(jnp.float32), right.astype(jnp.float32), precision=lax.Precision.HIGHEST)
        total = term if total is None else total + term
    rounded = lax.optimization_barrier(total.astype(jnp.bfloat16))
    return jnp.sum(rounded.astype(jnp.float32), axis=0)


def data_reduce(left, right):
    left_split = left.reshape(N_EXPERT, N_DP, CAP, left.shape[1]).astype(jnp.float32)
    right_split = right.reshape(N_EXPERT, N_DP, CAP, right.shape[1]).astype(jnp.float32)
    halves = jnp.einsum("sdca,sdcb->dab", left_split, right_split, precision=lax.Precision.HIGHEST)
    rounded = lax.optimization_barrier(halves.astype(jnp.bfloat16))
    return jnp.sum(rounded.astype(jnp.float32), axis=0).astype(jnp.bfloat16)


def section_forward(inputs):
    x_rows, ids, route, w_gate, w_up, w_down = inputs
    slot_total = (ids.shape[0] // TOK_DEV) * CAP
    destination = pair_positions(ids)
    pair_rows = jnp.repeat(x_rows, TOP, axis=0)
    gate_slabs = w_gate.reshape(EXPERTS, GROUP, D, FS)
    up_slabs = w_up.reshape(EXPERTS, GROUP, D, FS)
    down_slabs = w_down.reshape(EXPERTS, GROUP, FS, D)

    def one_expert(accumulated, items):
        expert_id, gate_w, up_w, down_w = items
        expert_mask = ids == expert_id
        target = jnp.where(expert_mask, destination, slot_total).reshape(-1)
        expert_rows = gather_rows(pair_rows, target, slot_total)
        gate_pre = jnp.dot(expert_rows, gate_w.transpose(1, 0, 2).reshape(D, FF), preferred_element_type=jnp.float32)
        up_proj = jnp.dot(expert_rows, up_w.transpose(1, 0, 2).reshape(D, FF), preferred_element_type=jnp.float32)
        hidden = (jax.nn.silu(gate_pre) * up_proj).astype(jnp.bfloat16)
        output = slab_sum([(hidden, down_w)])
        picked = output[jnp.minimum(target, slot_total - 1)].reshape(ids.shape[0], TOP, D)
        weighted = jnp.where(expert_mask[:, :, None], route[:, :, None] * picked, 0.0)
        return accumulated + jnp.sum(weighted, axis=1), None

    start = jnp.zeros((ids.shape[0], D), jnp.float32)
    total, _ = lax.scan(one_expert, start, (jnp.arange(EXPERTS, dtype=jnp.int32), gate_slabs, up_slabs, down_slabs))
    return total.astype(jnp.bfloat16)


def section_backward(inputs):
    x_rows, ids, route, dy_rows, w_gate, w_up, w_down = inputs
    slot_total = (ids.shape[0] // TOK_DEV) * CAP
    destination = pair_positions(ids)
    pair_rows = jnp.repeat(x_rows, TOP, axis=0)
    cotangent = (route[:, :, None] * dy_rows[:, None, :].astype(jnp.float32)).astype(jnp.bfloat16).reshape(-1, D)
    gate_slabs = w_gate.reshape(EXPERTS, GROUP, D, FS)
    up_slabs = w_up.reshape(EXPERTS, GROUP, D, FS)
    down_slabs = w_down.reshape(EXPERTS, GROUP, FS, D)

    def one_expert(accumulated, items):
        expert_id, gate_w, up_w, down_w = items
        expert_mask = ids == expert_id
        target = jnp.where(expert_mask, destination, slot_total).reshape(-1)
        expert_rows = gather_rows(pair_rows, target, slot_total)
        expert_cot = gather_rows(cotangent, target, slot_total)
        gate_pre = jnp.dot(expert_rows, gate_w.transpose(1, 0, 2).reshape(D, FF), preferred_element_type=jnp.float32)
        up_proj = jnp.dot(expert_rows, up_w.transpose(1, 0, 2).reshape(D, FF), preferred_element_type=jnp.float32)
        sigmoid_gate = jax.nn.sigmoid(gate_pre)
        activated = gate_pre * sigmoid_gate
        hidden = (activated * up_proj).astype(jnp.bfloat16)
        d_hidden = jnp.dot(expert_cot, down_w.reshape(FF, D).T, preferred_element_type=jnp.float32)
        d_up = (d_hidden * activated).astype(jnp.bfloat16)
        d_gate = (d_hidden * up_proj * sigmoid_gate * (1.0 + gate_pre * (1.0 - sigmoid_gate))).astype(jnp.bfloat16)
        back = slab_sum([(d_gate, gate_w.transpose(0, 2, 1)), (d_up, up_w.transpose(0, 2, 1))])
        picked = back[jnp.minimum(target, slot_total - 1)].reshape(ids.shape[0], TOP, D)
        summed = jnp.sum(jnp.where(expert_mask[:, :, None], picked, 0.0), axis=1)
        grad_g = data_reduce(expert_rows, d_gate).reshape(D, GROUP, FS).transpose(1, 0, 2)
        grad_u = data_reduce(expert_rows, d_up).reshape(D, GROUP, FS).transpose(1, 0, 2)
        grad_d = data_reduce(hidden, expert_cot).reshape(GROUP, FS, D)
        return accumulated + summed, (grad_g, grad_u, grad_d)

    start = jnp.zeros((ids.shape[0], D), jnp.float32)
    total, grads = lax.scan(one_expert, start, (jnp.arange(EXPERTS, dtype=jnp.int32), gate_slabs, up_slabs, down_slabs))
    grad_g = grads[0].reshape(EXPERTS * GROUP, D, FS)
    grad_u = grads[1].reshape(EXPERTS * GROUP, D, FS)
    grad_d = grads[2].reshape(EXPERTS * GROUP, FS, D)
    return total.astype(jnp.bfloat16), grad_g, grad_u, grad_d


def reference(x_fwd, ids_fwd, route_fwd, x_bwd, ids_bwd, route_bwd, dy_bwd, w_gate, w_up, w_down):
    outputs = lax.map(section_forward, (x_fwd, ids_fwd, route_fwd, w_gate, w_up, w_down))
    back, grad_gate, grad_up, grad_down = lax.map(section_backward, (x_bwd, ids_bwd, route_bwd, dy_bwd, w_gate, w_up, w_down))
    y_next = jnp.roll(outputs, 1, axis=0)
    dx_next = jnp.roll(back, 1, axis=0)
    return y_next, dx_next, grad_gate, grad_up, grad_down
```

```python
import functools

import jax
import jax.numpy as jnp
from jax import lax
from jax.experimental import pallas as pl
from jax.experimental.pallas import tpu as pltpu
from jax.sharding import PartitionSpec as P

FF = 1024
TOP = 2
TILE = 256
VMEM_LIMIT = 32 * 1024 * 1024
F32 = jnp.float32
BF16 = jnp.bfloat16


def exchange(value, axis, mask):
    count = lax.axis_size(axis)
    return lax.ppermute(value, axis, [(source, source ^ mask) for source in range(count)])


def section_shift(value, flip):
    sections, cores = lax.axis_size("section"), lax.axis_size("dp")
    pairs = []
    for section in range(sections):
        for core in range(cores):
            target = ((section + 1) % sections) * cores + (core ^ flip)
            pairs.append((section * cores + core, target))
    return lax.ppermute(value, ("section", "dp"), pairs)


def dot(left, right, left_dim, right_dim):
    return lax.dot_general(
        left, right, (((left_dim,), (right_dim,)), ((), ())), preferred_element_type=F32
    )


def call(kernel, out_shape, grid, in_specs, out_specs, scratch, flops, moved):
    return pl.pallas_call(
        kernel,
        out_shape=out_shape,
        grid=grid,
        in_specs=in_specs,
        out_specs=out_specs,
        scratch_shapes=scratch,
        compiler_params=pltpu.CompilerParams(vmem_limit_bytes=VMEM_LIMIT),
        cost_estimate=pl.CostEstimate(flops=flops, bytes_accessed=moved, transcendentals=0),
    )


def whole(shape):
    return pl.BlockSpec(shape, lambda *_: (0,) * len(shape))


SCALARS = pl.BlockSpec(memory_space=pltpu.SMEM)


def slot_rows(place_ref, ids_ref, blocks, group, capacity, tokens):
    lanes = 2 * tokens
    padded = max(8, blocks)
    me, core = place_ref[0], place_ref[1]
    first, second = ids_ref[0:1, :], ids_ref[1:2, :]
    row = lax.broadcasted_iota(jnp.int32, (padded, lanes), 0)
    expert = ((row ^ me) // group).astype(F32)
    is_first, is_second = expert == first, expert == second
    named = jnp.where(is_first | is_second, 1.0, 0.0)
    before = lax.broadcasted_iota(jnp.int32, (lanes, lanes), 0)
    after = lax.broadcasted_iota(jnp.int32, (lanes, lanes), 1)
    earlier = (before < after) & ((before < tokens) == (after < tokens))
    position = dot(named.astype(BF16), jnp.where(earlier, 1.0, 0.0).astype(BF16), 1, 0)
    lane = lax.broadcasted_iota(jnp.int32, (padded, lanes), 1)
    half = jnp.where(lane < tokens, core, 1 - core).astype(F32)
    slot = jnp.where(named > 0.5, position + half * capacity, -1.0)
    return slot, is_first


def slot_table(slot, block, rows):
    lanes = slot.shape[1]
    index = lax.broadcasted_iota(jnp.int32, (rows, lanes), 0).astype(F32)
    return jnp.where(index == slot[block : block + 1, :], 1.0, 0.0)


def dispatch_kernel(
    place_ref, meta_ref, own_ref, other_ref, *refs, blocks, group, capacity, tokens, weighted
):
    outs, all_ref = refs[:blocks], refs[blocks]
    rows, width = outs[0].shape
    core = place_ref[1]
    own = own_ref[:, pl.ds(pl.multiple_of(core * width, 128), width)]
    all_ref[0:tokens, :] = own
    all_ref[tokens : 2 * tokens, :] = other_ref[...]
    slot, is_first = slot_rows(place_ref, meta_ref, blocks, group, capacity, tokens)
    for block in range(blocks):
        table = slot_table(slot, block, rows)
        if weighted:
            route = jnp.where(
                is_first[block : block + 1, :], meta_ref[2:3, :], meta_ref[3:4, :]
            )
            scale = jnp.sum(table * route, axis=1, keepdims=True)
        table = table.astype(BF16)
        for start in range(0, width, TILE):
            picked = dot(table, all_ref[:, start : start + TILE], 1, 0)
            if weighted:
                picked = picked * scale
            outs[block][:, start : start + TILE] = picked.astype(BF16)


def dispatch(place, meta, own, other, shape, weighted):
    blocks, rows, group, capacity = shape
    tokens, width = other.shape
    kernel = functools.partial(
        dispatch_kernel,
        blocks=blocks,
        group=group,
        capacity=capacity,
        tokens=tokens,
        weighted=weighted,
    )
    return call(
        kernel,
        [jax.ShapeDtypeStruct((rows, width), BF16)] * blocks,
        (1,),
        [SCALARS, whole(meta.shape), whole(own.shape), whole(other.shape)],
        [whole((rows, width))] * blocks,
        [pltpu.VMEM((2 * tokens, width), BF16)],
        2 * blocks * rows * 2 * tokens * width,
        2 * width * (3 * tokens + blocks * rows),
    )(place, meta, own, other)


def combine_kernel(place_ref, meta_ref, *refs, blocks, group, capacity, tokens, weighted):
    returned, (own_ref, other_ref) = refs[:blocks], refs[blocks:]
    rows, width = returned[0].shape
    slot, is_first = slot_rows(place_ref, meta_ref, blocks, group, capacity, tokens)
    high, low = [], []
    for block in range(blocks):
        table = slot_table(slot, block, rows)
        if weighted:
            route = jnp.where(
                is_first[block : block + 1, :], meta_ref[2:3, :], meta_ref[3:4, :]
            )
            table = table * route
        top = table.astype(BF16)
        high.append(top)
        low.append((table - top.astype(F32)).astype(BF16))
    for start in range(0, width, TILE):
        total = jnp.zeros((2 * tokens, TILE), F32)
        for block in range(blocks):
            values = returned[block][:, start : start + TILE]
            total += dot(high[block], values, 0, 0)
            if weighted:
                total += dot(low[block], values, 0, 0)
        total = total.astype(BF16)
        own_ref[:, start : start + TILE] = total[:tokens]
        other_ref[:, start : start + TILE] = total[tokens:]


def combine(place, meta, returned, shape, tokens, weighted):
    blocks, rows, group, capacity = shape
    width = returned[0].shape[1]
    kernel = functools.partial(
        combine_kernel,
        blocks=blocks,
        group=group,
        capacity=capacity,
        tokens=tokens,
        weighted=weighted,
    )
    return call(
        kernel,
        [jax.ShapeDtypeStruct((tokens, width), BF16)] * 2,
        (1,),
        [SCALARS, whole(meta.shape)] + [whole((rows, width))] * blocks,
        [whole((tokens, width))] * 2,
        [],
        4 * blocks * rows * 2 * tokens * width,
        2 * width * (2 * tokens + blocks * rows),
    )(place, meta, *returned)


def gather_blocks(refs, target):
    rows = refs[0].shape[0]
    for block, ref in enumerate(refs):
        target[block * rows : (block + 1) * rows, :] = ref[...]


def gate_up_kernel(*refs, blocks):
    gate_w, up_w, out, all_ref = refs[blocks:]

    @pl.when(pl.program_id(0) == 0)
    def _():
        gather_blocks(refs[:blocks], all_ref)

    out[0] = dot(all_ref[...], gate_w[...], 1, 0).astype(BF16)
    out[1] = dot(all_ref[...], up_w[...], 1, 0).astype(BF16)


def gate_up(inputs, gate_w, up_w):
    blocks, (rows, width) = len(inputs), inputs[0].shape
    units, total = gate_w.shape[1], len(inputs) * inputs[0].shape[0]
    weight = pl.BlockSpec((width, TILE), lambda i: (0, i))
    return call(
        functools.partial(gate_up_kernel, blocks=blocks),
        jax.ShapeDtypeStruct((2, total, units), BF16),
        (units // TILE,),
        [whole((rows, width))] * blocks + [weight, weight],
        pl.BlockSpec((2, total, TILE), lambda i: (0, 0, i)),
        [pltpu.VMEM((total, width), BF16)],
        4 * total * width * units,
        2 * (total * width + 2 * width * units + 2 * total * units),
    )(*inputs, gate_w, up_w)


def d_hidden_kernel(*refs, blocks):
    down_w, out, all_ref = refs[blocks:]

    @pl.when(pl.program_id(0) == 0)
    def _():
        gather_blocks(refs[:blocks], all_ref)

    out[...] = dot(all_ref[...], down_w[...], 1, 1).astype(BF16)


def d_hidden(inputs, down_w):
    blocks, (rows, width) = len(inputs), inputs[0].shape
    units, total = down_w.shape[0], len(inputs) * inputs[0].shape[0]
    return call(
        functools.partial(d_hidden_kernel, blocks=blocks),
        jax.ShapeDtypeStruct((total, units), BF16),
        (units // TILE,),
        [whole((rows, width))] * blocks + [pl.BlockSpec((TILE, width), lambda i: (i, 0))],
        pl.BlockSpec((total, TILE), lambda i: (0, i)),
        [pltpu.VMEM((total, width), BF16)],
        2 * total * width * units,
        2 * (total * width + width * units + total * units),
    )(*inputs, down_w)


def scatter_tile(value, outs):
    rows = outs[0].shape[0]
    for block, out in enumerate(outs):
        out[...] = value[block * rows : (block + 1) * rows]


def down_kernel(own_ref, other_ref, down_w, *refs):
    outs, hidden = refs[:-1], refs[-1]

    @pl.when(pl.program_id(0) == 0)
    def _():
        for start in range(0, hidden.shape[1], TILE):
            part = slice(start, start + TILE)
            gate = own_ref[0, :, part].astype(F32) + other_ref[0, :, part].astype(F32)
            up = own_ref[1, :, part].astype(F32) + other_ref[1, :, part].astype(F32)
            hidden[:, part] = (gate * jax.nn.sigmoid(gate) * up).astype(BF16)

    scatter_tile(dot(hidden[...], down_w[...], 1, 0).astype(BF16), outs)


def down(own, other, down_w, blocks):
    _, total, units = own.shape
    width, rows = down_w.shape[1], total // blocks
    return call(
        down_kernel,
        [jax.ShapeDtypeStruct((rows, width), BF16)] * blocks,
        (width // TILE,),
        [whole(own.shape)] * 2 + [pl.BlockSpec((units, TILE), lambda i: (0, i))],
        [pl.BlockSpec((rows, TILE), lambda i: (0, i))] * blocks,
        [pltpu.VMEM((total, units), BF16)],
        2 * total * width * units,
        2 * (total * width + width * units + 4 * total * units),
    )(own, other, down_w)


def back_kernel(own_ref, other_ref, own_d, other_d, gate_w, up_w, hidden, d_gate, d_up, *outs):
    @pl.when(pl.program_id(0) == 0)
    def _():
        for start in range(0, hidden.shape[1], TILE):
            part = slice(start, start + TILE)
            gate = own_ref[0, :, part].astype(F32) + other_ref[0, :, part].astype(F32)
            up = own_ref[1, :, part].astype(F32) + other_ref[1, :, part].astype(F32)
            d_hid = own_d[:, part].astype(F32) + other_d[:, part].astype(F32)
            sigmoid = jax.nn.sigmoid(gate)
            activated = gate * sigmoid
            hidden[:, part] = (activated * up).astype(BF16)
            d_up[:, part] = (d_hid * activated).astype(BF16)
            d_gate[:, part] = (
                d_hid * up * sigmoid * (1.0 + gate * (1.0 - sigmoid))
            ).astype(BF16)

    total = dot(d_gate[...], gate_w[...], 1, 1) + dot(d_up[...], up_w[...], 1, 1)
    scatter_tile(total.astype(BF16), outs)


def back(own, other, own_d, other_d, gate_w, up_w, blocks):
    _, total, units = own.shape
    width, rows = gate_w.shape[0], total // blocks
    weight = pl.BlockSpec((TILE, units), lambda i: (i, 0))
    return call(
        back_kernel,
        [jax.ShapeDtypeStruct((total, units), BF16)] * 3
        + [jax.ShapeDtypeStruct((rows, width), BF16)] * blocks,
        (width // TILE,),
        [whole(own.shape)] * 2 + [whole(own_d.shape)] * 2 + [weight, weight],
        [whole((total, units))] * 3 + [pl.BlockSpec((rows, TILE), lambda i: (0, i))] * blocks,
        [],
        4 * total * width * units,
        2 * (total * width + 2 * width * units + 9 * total * units),
    )(own, other, own_d, other_d, gate_w, up_w)


def grad_kernel(hidden, d_gate, d_up, *refs, blocks):
    inputs, cots = refs[:blocks], refs[blocks : 2 * blocks]
    grad_gate, grad_up, grad_down, in_all, cot_all = refs[2 * blocks :]
    gather_blocks(inputs, in_all)
    gather_blocks(cots, cot_all)
    grad_gate[...] = dot(in_all[...], d_gate[...], 0, 0).astype(BF16)
    grad_up[...] = dot(in_all[...], d_up[...], 0, 0).astype(BF16)
    grad_down[...] = dot(hidden[...], cot_all[...], 0, 0).astype(BF16)


def grads(hidden, d_gate, d_up, inputs, cots):
    blocks, (rows, width) = len(inputs), inputs[0].shape
    total, units = hidden.shape
    piece = pl.BlockSpec((rows, TILE), lambda i: (0, i))
    return call(
        functools.partial(grad_kernel, blocks=blocks),
        [
            jax.ShapeDtypeStruct((width, units), BF16),
            jax.ShapeDtypeStruct((width, units), BF16),
            jax.ShapeDtypeStruct((units, width), BF16),
        ],
        (width // TILE,),
        [whole((total, units))] * 3 + [piece] * (2 * blocks),
        [
            pl.BlockSpec((TILE, units), lambda i: (i, 0)),
            pl.BlockSpec((TILE, units), lambda i: (i, 0)),
            pl.BlockSpec((units, TILE), lambda i: (0, i)),
        ],
        [pltpu.VMEM((total, TILE), BF16)] * 2,
        6 * total * width * units,
        2 * (2 * total * width + 3 * width * units + 3 * total * units),
    )(hidden, d_gate, d_up, *inputs, *cots)


def to_experts(blocks):
    return [blocks[0]] + [
        exchange(block, "expert", mask) for mask, block in enumerate(blocks) if mask > 0
    ]


def next_section(own, other, core):
    mine, rest = section_shift(own, 0), section_shift(other, 1)
    first = jnp.where(core == 0, mine, rest)
    second = jnp.where(core == 0, rest, mine)
    return jnp.concatenate([first, second], axis=1)


def local(x_fwd, ids_fwd, route_fwd, x_bwd, ids_bwd, route_bwd, dy_bwd, w_gate, w_up, w_down):
    n_expert = lax.axis_size("expert")
    slab_width = w_gate.shape[-1]
    group = FF // slab_width
    experts = n_expert // group
    tokens = x_fwd.shape[1]
    width = w_gate.shape[2]
    spread = 4 * experts * group
    capacity = group * ((5 * tokens * TOP + spread - 1) // spread)
    rows = (2 * capacity + 15) // 16 * 16
    shape = (n_expert, rows, group, capacity)
    core = lax.axis_index("dp")
    place = jnp.stack([lax.axis_index("expert"), core]).astype(jnp.int32)
    gate_w, up_w, down_w = w_gate[0, 0], w_up[0, 0], w_down[0, 0]

    def other_half(value):
        return lax.dynamic_slice_in_dim(value, (1 - core) * width, width, axis=1)

    meta = jnp.concatenate(
        [
            ids_bwd[0].T.astype(F32),
            route_bwd[0].T,
            ids_fwd[0].T.astype(F32),
            route_fwd[0].T,
        ],
        axis=0,
    )
    meta = jnp.concatenate([meta, exchange(meta, "dp", 1)], axis=1)
    meta_b, meta_f = meta[0:4], meta[4:8]
    other_x = exchange(other_half(x_bwd[0]), "dp", 1)
    other_dy = exchange(other_half(dy_bwd[0]), "dp", 1)
    other_f = exchange(other_half(x_fwd[0]), "dp", 1)

    rows_b = to_experts(dispatch(place, meta_b, x_bwd[0], other_x, shape, False))
    cots_b = to_experts(dispatch(place, meta_b, dy_bwd[0], other_dy, shape, True))
    rows_f = to_experts(dispatch(place, meta_f, x_fwd[0], other_f, shape, False))

    part_b = gate_up(rows_b, gate_w, up_w)
    part_b_other = exchange(part_b, "dp", 1)
    part_d = d_hidden(cots_b, down_w)
    part_d_other = exchange(part_d, "dp", 1)
    hidden, d_gate, d_up, *back_blocks = back(
        part_b, part_b_other, part_d, part_d_other, gate_w, up_w, n_expert
    )
    returned_b = to_experts(back_blocks)

    part_f = gate_up(rows_f, gate_w, up_w)
    part_f_other = exchange(part_f, "dp", 1)
    returned_f = to_experts(down(part_f, part_f_other, down_w, n_expert))

    grad_gate, grad_up, grad_down = grads(hidden, d_gate, d_up, rows_b, cots_b)

    dx_next = next_section(*combine(place, meta_b, returned_b, shape, tokens, False), core)
    y_next = next_section(*combine(place, meta_f, returned_f, shape, tokens, True), core)
    return (
        y_next[None],
        dx_next[None],
        grad_gate[None, None],
        grad_up[None, None],
        grad_down[None, None],
    )


def solution(mesh):
    rows = P("section", ("expert", "dp"), None)
    by_feature = P("section", "expert", "dp", None)
    down_spec = P("section", "expert", None, "dp")
    return jax.shard_map(
        local,
        mesh=mesh,
        in_specs=(rows,) * 7 + (by_feature, by_feature, down_spec),
        out_specs=(rows, rows, by_feature, by_feature, down_spec),
        check_vma=False,
    )
```

```python
import functools

import jax
import jax.numpy as jnp
from jax import lax
from jax.experimental import pallas as pl
from jax.experimental.pallas import tpu as pltpu
from jax.sharding import PartitionSpec as P

FF = 1024
TOP = 2
TILE = 256
VMEM_LIMIT = 20 * 1024 * 1024
META = 16
COST_SHARE = 1024
F32 = jnp.float32
BF16 = jnp.bfloat16


def exchange(value, axis, mask):
    count = lax.axis_size(axis)
    return lax.ppermute(value, axis, [(source, source ^ mask) for source in range(count)])


def section_shift(value, flip):
    sections, cores = lax.axis_size("section"), lax.axis_size("dp")
    pairs = []
    for section in range(sections):
        for core in range(cores):
            target = ((section + 1) % sections) * cores + (core ^ flip)
            pairs.append((section * cores + core, target))
    return lax.ppermute(value, ("section", "dp"), pairs)


def dot(left, right, left_dim, right_dim):
    return lax.dot_general(
        left, right, (((left_dim,), (right_dim,)), ((), ())), preferred_element_type=F32
    )


VMEM = pl.BlockSpec(memory_space=pltpu.VMEM)
HBM = pl.BlockSpec(memory_space=pltpu.HBM)
AFTER = pl.BlockSpec(memory_space=pl.ANY)


def call(kernel, out_shape, in_specs, out_specs, scratch, flops, moved, grid=()):
    return pl.pallas_call(
        kernel,
        out_shape=out_shape,
        grid=grid,
        in_specs=in_specs,
        out_specs=out_specs,
        scratch_shapes=scratch,
        compiler_params=pltpu.CompilerParams(vmem_limit_bytes=VMEM_LIMIT),
        cost_estimate=pl.CostEstimate(
            flops=flops // COST_SHARE, bytes_accessed=moved // COST_SHARE, transcendentals=0
        ),
    )


def array(*shape):
    return jax.ShapeDtypeStruct(shape, BF16)


def in_hbm(value):
    return pltpu.with_memory_space_constraint(value, pltpu.HBM)


def halves(value_ref, own_ref, other_ref, sems, first):
    tokens, width = value_ref.shape[0], value_ref.shape[1] // 2
    core = lax.axis_index("dp")
    copies = []
    for place, (half, target) in enumerate(((core, own_ref), (1 - core, other_ref))):
        columns = pl.ds(pl.multiple_of(half * width, 128), width)
        copies.append(
            pltpu.make_async_copy(
                value_ref.at[:, columns], target.at[0:tokens], sems.at[first + place]
            )
        )
    for copy in copies:
        copy.start()
    return copies


def pack_kernel(x_ref, *refs):
    sources, (own_ref, other_ref, packed, sems), held = refs[:4], refs[4:8], refs[8:]
    copies = halves(x_ref, own_ref, other_ref, sems, 0)
    tokens = x_ref.shape[0]
    small = [
        pltpu.make_async_copy(source, target, sems.at[2 + place])
        for place, (source, target) in enumerate(zip(sources, held))
    ]
    for copy in small:
        copy.start()
    packed[...] = jnp.zeros_like(packed)
    for copy in small:
        copy.wait()
    ids_b, route_b, ids_f, route_f = held
    for start, ids, route in ((0, ids_b, route_b), (META // 2, ids_f, route_f)):
        packed[start : start + 2, 0:tokens] = ids[...].astype(F32)
        rest = route[...]
        for piece in range(3):
            top = rest.astype(BF16).astype(F32)
            row = start + 2 + 2 * piece
            packed[row : row + 2, 0:tokens] = top
            rest = rest - top
    mine = packed[...]
    lanes = packed.shape[1]
    own_ref[tokens : tokens + META, 0:lanes] = mine.astype(BF16)
    other_ref[tokens : tokens + META, 0:lanes] = pltpu.roll(mine, tokens, 1).astype(BF16)
    for copy in copies:
        copy.wait()


def pack(x, ids_b, route_b, ids_f, route_f):
    tokens, width = x.shape[0], x.shape[1] // 2
    out = array(tokens + META, width)
    return call(
        pack_kernel,
        [out, out],
        [HBM] * 5,
        [VMEM, VMEM],
        [pltpu.VMEM((META, 2 * tokens), F32), pltpu.SemaphoreType.DMA((6,))]
        + [pltpu.VMEM(value.shape, value.dtype) for value in (ids_b, route_b, ids_f, route_f)],
        0,
        8 * x.size,
    )(x, ids_b, route_b, ids_f, route_f)


def cut_kernel(x_ref, dy_ref, own_x, other_x, own_dy, other_dy, sems):
    copies = halves(x_ref, own_x, other_x, sems, 0)
    copies += halves(dy_ref, own_dy, other_dy, sems, 2)
    for copy in copies:
        copy.wait()


def cut(x, dy):
    tokens, width = x.shape[0], x.shape[1] // 2
    return call(
        cut_kernel,
        [array(tokens, width)] * 4,
        [HBM, HBM],
        [VMEM] * 4,
        [pltpu.SemaphoreType.DMA((4,))],
        0,
        16 * x.size,
    )(x, dy)


class Plan:
    def __init__(self, blocks, rows, group, capacity, tokens, relative):
        self.blocks, self.rows, self.group = blocks, rows, group
        self.capacity, self.tokens, self.relative = capacity, tokens, relative


def slot_rows(own_meta, other_meta, plan, first_row):
    lanes = 2 * plan.tokens
    padded = max(8, plan.blocks)
    me = lax.axis_index("expert") if plan.relative else 0
    core = lax.axis_index("dp")
    meta = own_meta[plan.tokens : plan.tokens + META, 0:lanes].astype(F32)
    meta = meta + other_meta[plan.tokens : plan.tokens + META, 0:lanes].astype(F32)
    meta = meta[first_row : first_row + META // 2]
    first, second = meta[0:1], meta[1:2]
    route = meta[2:4] + meta[4:6] + meta[6:8]
    row = lax.broadcasted_iota(jnp.int32, (padded, lanes), 0)
    expert = ((row ^ me) // plan.group).astype(F32)
    is_first, is_second = expert == first, expert == second
    named = jnp.where(is_first | is_second, 1.0, 0.0)
    before = lax.broadcasted_iota(jnp.int32, (lanes, lanes), 0)
    after = lax.broadcasted_iota(jnp.int32, (lanes, lanes), 1)
    earlier = (before < after) & ((before < plan.tokens) == (after < plan.tokens))
    position = dot(named.astype(BF16), jnp.where(earlier, 1.0, 0.0).astype(BF16), 1, 0)
    lane = lax.broadcasted_iota(jnp.int32, (padded, lanes), 1)
    half = jnp.where(lane < plan.tokens, core, 1 - core).astype(F32)
    slot = jnp.where(named > 0.5, position + half * plan.capacity, -1.0)
    return slot, jnp.where(is_first, route[0:1], route[1:2])


def slot_table(slot, block, rows):
    index = lax.broadcasted_iota(jnp.int32, (rows, slot.shape[1]), 0).astype(F32)
    return jnp.where(index == slot[block : block + 1, :], 1.0, 0.0)


def dispatch_kernel(own_meta, other_meta, own_ref, other_ref, *refs, plan, first_row, weighted):
    outs = refs[-plan.blocks :]
    width, tokens = outs[0].shape[1], plan.tokens
    slot, route = slot_rows(own_meta, other_meta, plan, first_row)
    values = jnp.concatenate([own_ref[0:tokens, :], other_ref[0:tokens, :]], axis=0)
    for block in range(plan.blocks):
        table = slot_table(slot, block, plan.rows)
        if weighted:
            scale = jnp.sum(table * route[block : block + 1, :], axis=1, keepdims=True)
        table = table.astype(BF16)
        for start in range(0, width, TILE):
            picked = dot(table, values[:, start : start + TILE], 1, 0)
            if weighted:
                picked = picked * scale
            outs[block][:, start : start + TILE] = picked.astype(BF16)


def dispatch(metas, own, other, plan, first_row, weighted, after=()):
    width = own.shape[1]
    return call(
        functools.partial(
            dispatch_kernel, plan=plan, first_row=first_row, weighted=weighted
        ),
        [array(plan.rows, width)] * plan.blocks,
        [VMEM] * 4 + [AFTER] * len(after),
        [VMEM] * plan.blocks,
        [],
        4 * plan.blocks * plan.rows * plan.tokens * width,
        2 * width * (3 * plan.tokens + plan.blocks * plan.rows),
    )(*metas, own, other, *after)


def combine_kernel(own_meta, other_meta, *refs, plan, first_row, weighted):
    returned = refs[: plan.blocks]
    own_ref, other_ref = refs[-2:]
    width, tokens = returned[0].shape[1], plan.tokens
    slot, route = slot_rows(own_meta, other_meta, plan, first_row)
    high, low = [], []
    for block in range(plan.blocks):
        table = slot_table(slot, block, plan.rows)
        if weighted:
            table = table * route[block : block + 1, :]
        top = table.astype(BF16)
        high.append(top)
        low.append((table - top.astype(F32)).astype(BF16))
    high = jnp.concatenate(high, axis=0)
    low = jnp.concatenate(low, axis=0)
    for start in range(0, width, TILE):
        values = jnp.concatenate([ref[:, start : start + TILE] for ref in returned], axis=0)
        total = dot(high, values, 0, 0)
        if weighted:
            total += dot(low, values, 0, 0)
        total = total.astype(BF16)
        own_ref[:, start : start + TILE] = total[:tokens]
        other_ref[:, start : start + TILE] = total[tokens:]


def combine(metas, returned, plan, first_row, weighted, after=()):
    width = returned[0].shape[1]
    return call(
        functools.partial(combine_kernel, plan=plan, first_row=first_row, weighted=weighted),
        [array(plan.tokens, width)] * 2,
        [VMEM] * (2 + plan.blocks) + [AFTER] * len(after),
        [VMEM] * 2,
        [],
        8 * plan.blocks * plan.rows * plan.tokens * width,
        2 * width * (2 * plan.tokens + plan.blocks * plan.rows),
    )(*metas, *returned, *after)


def stream(weight_ref, held, sems, axis):
    copies = []
    for tile in range(weight_ref.shape[axis] // TILE):
        part = pl.ds(tile * TILE, TILE)
        part = (part, slice(None)) if axis == 0 else (slice(None), part)
        copy = pltpu.make_async_copy(weight_ref.at[part], held.at[part], sems.at[tile])
        copy.start()
        copies.append(copy)
    return copies


def held_weight(shape, axis):
    return [pltpu.VMEM(shape, BF16), pltpu.SemaphoreType.DMA((shape[axis] // TILE,))]


def joined(refs):
    return jnp.concatenate([ref[...] for ref in refs], axis=0)


def gate_up_kernel(*refs, blocks):
    gate_w, up_w = refs[blocks : blocks + 2]
    out, gate_held, gate_sems, up_held, up_sems, rows = refs[-6:]
    gate_copies = stream(gate_w, gate_held, gate_sems, 1)
    up_copies = stream(up_w, up_held, up_sems, 1)
    rows[...] = joined(refs[:blocks])
    for tile in range(len(gate_copies)):
        part = slice(tile * TILE, (tile + 1) * TILE)
        gate_copies[tile].wait()
        out[0, :, part] = dot(rows[...], gate_held[:, part], 1, 0).astype(BF16)
        up_copies[tile].wait()
        out[1, :, part] = dot(rows[...], up_held[:, part], 1, 0).astype(BF16)


def gate_up(inputs, gate_w, up_w, after=()):
    blocks, (rows, width) = len(inputs), inputs[0].shape
    units, total = gate_w.shape[1], blocks * rows
    return call(
        functools.partial(gate_up_kernel, blocks=blocks),
        array(2, total, units),
        [VMEM] * blocks + [HBM, HBM] + [AFTER] * len(after),
        VMEM,
        held_weight(gate_w.shape, 1) * 2 + [pltpu.VMEM((total, width), BF16)],
        4 * total * width * units,
        2 * (total * width + 2 * width * units + 2 * total * units),
    )(*inputs, gate_w, up_w, *after)


def d_hidden_kernel(*refs, blocks):
    down_w = refs[blocks]
    out, held, sems, rows = refs[-4:]
    copies = stream(down_w, held, sems, 0)
    rows[...] = joined(refs[:blocks])
    for tile, copy in enumerate(copies):
        part = slice(tile * TILE, (tile + 1) * TILE)
        copy.wait()
        out[:, part] = dot(rows[...], held[part, :], 1, 1).astype(BF16)


def d_hidden(inputs, down_w, after=()):
    blocks, (rows, width) = len(inputs), inputs[0].shape
    units, total = down_w.shape[0], blocks * rows
    return call(
        functools.partial(d_hidden_kernel, blocks=blocks),
        array(total, units),
        [VMEM] * blocks + [HBM] + [AFTER] * len(after),
        VMEM,
        held_weight(down_w.shape, 0) + [pltpu.VMEM((total, width), BF16)],
        2 * total * width * units,
        2 * (total * width + width * units + total * units),
    )(*inputs, down_w, *after)


def scatter_tile(value, outs, part):
    rows = outs[0].shape[0]
    for block, out in enumerate(outs):
        out[:, part] = value[block * rows : (block + 1) * rows]


def gate_and_up(own_ref, other_ref, part):
    gate = own_ref[0, :, part].astype(F32) + other_ref[0, :, part].astype(F32)
    up = own_ref[1, :, part].astype(F32) + other_ref[1, :, part].astype(F32)
    return gate, up


def down_kernel(own_ref, other_ref, down_w, *refs):
    outs, (held, sems, hidden) = refs[:-3], refs[-3:]
    copies = stream(down_w, held, sems, 1)
    for start in range(0, hidden.shape[1], TILE):
        part = slice(start, start + TILE)
        gate, up = gate_and_up(own_ref, other_ref, part)
        hidden[:, part] = (gate * jax.nn.sigmoid(gate) * up).astype(BF16)
    for tile, copy in enumerate(copies):
        part = slice(tile * TILE, (tile + 1) * TILE)
        copy.wait()
        scatter_tile(dot(hidden[...], held[:, part], 1, 0).astype(BF16), outs, part)


def down(own, other, down_w, blocks):
    _, total, units = own.shape
    width, rows = down_w.shape[1], total // blocks
    return call(
        down_kernel,
        [array(rows, width)] * blocks,
        [VMEM, VMEM, HBM],
        [VMEM] * blocks,
        held_weight(down_w.shape, 1) + [pltpu.VMEM((total, units), BF16)],
        2 * total * width * units,
        2 * (total * width + width * units + 4 * total * units),
    )(own, other, down_w)


def back_kernel(own_ref, other_ref, own_d, other_d, gate_w, up_w, hidden, d_gate, d_up, *refs):
    outs, (gate_held, gate_sems, up_held, up_sems) = refs[:-4], refs[-4:]
    gate_copies = stream(gate_w, gate_held, gate_sems, 0)
    up_copies = stream(up_w, up_held, up_sems, 0)
    for start in range(0, hidden.shape[1], TILE):
        part = slice(start, start + TILE)
        gate, up = gate_and_up(own_ref, other_ref, part)
        d_hid = own_d[:, part].astype(F32) + other_d[:, part].astype(F32)
        sigmoid = jax.nn.sigmoid(gate)
        activated = gate * sigmoid
        hidden[:, part] = (activated * up).astype(BF16)
        d_up[:, part] = (d_hid * activated).astype(BF16)
        d_gate[:, part] = (d_hid * up * sigmoid * (1.0 + gate * (1.0 - sigmoid))).astype(BF16)
    for tile in range(len(gate_copies)):
        part = slice(tile * TILE, (tile + 1) * TILE)
        gate_copies[tile].wait()
        total = dot(d_gate[...], gate_held[part, :], 1, 1)
        up_copies[tile].wait()
        total += dot(d_up[...], up_held[part, :], 1, 1)
        scatter_tile(total.astype(BF16), outs, part)


def back(own, other, own_d, other_d, gate_w, up_w, blocks):
    _, total, units = own.shape
    width, rows = gate_w.shape[0], total // blocks
    return call(
        back_kernel,
        [array(total, units)] * 3 + [array(rows, width)] * blocks,
        [VMEM] * 4 + [HBM] * 2,
        [VMEM] * (3 + blocks),
        held_weight(gate_w.shape, 0) * 2,
        4 * total * width * units,
        2 * (total * width + 2 * width * units + 9 * total * units),
    )(own, other, own_d, other_d, gate_w, up_w)


def grad_kernel(hidden, d_gate, d_up, *refs, blocks):
    inputs, cots = refs[:blocks], refs[blocks : 2 * blocks]
    grad_gate, grad_up, grad_down, turned, cot_all = refs[-5:]

    @pl.when(pl.program_id(0) == 0)
    def _():
        for start in range(0, turned.shape[0], TILE):
            part = slice(start, start + TILE)
            piece = jnp.concatenate([ref[:, part] for ref in inputs], axis=0)
            turned[part, :] = piece.T
        cot_all[...] = joined(cots)

    part = pl.ds(pl.multiple_of(pl.program_id(0) * TILE, TILE), TILE)
    grad_gate[...] = dot(turned[...], d_gate[:, part], 1, 0).astype(BF16)
    grad_up[...] = dot(turned[...], d_up[:, part], 1, 0).astype(BF16)
    grad_down[...] = dot(hidden[:, part], cot_all[...], 0, 0).astype(BF16)


def grads(hidden, d_gate, d_up, inputs, cots, after=()):
    blocks, (rows, width) = len(inputs), inputs[0].shape
    total, units = hidden.shape
    by_column = pl.BlockSpec((width, TILE), lambda i: (0, i))
    return call(
        functools.partial(grad_kernel, blocks=blocks),
        [
            pltpu.HBM((width, units), BF16),
            pltpu.HBM((width, units), BF16),
            pltpu.HBM((units, width), BF16),
        ],
        [VMEM] * (3 + 2 * blocks) + [AFTER] * len(after),
        [by_column, by_column, pl.BlockSpec((TILE, width), lambda i: (i, 0))],
        [pltpu.VMEM((width, total), BF16), pltpu.VMEM((total, width), BF16)],
        6 * total * width * units,
        2 * (2 * total * width + 3 * width * units + 3 * total * units),
        grid=(units // TILE,),
    )(hidden, d_gate, d_up, *inputs, *cots, *after)


def to_experts(blocks, relative):
    if not relative:
        stacked = lax.all_to_all(jnp.stack(blocks), "expert", split_axis=0, concat_axis=0)
        return [stacked[block] for block in range(len(blocks))]
    return [blocks[0]] + [
        exchange(block, "expert", mask) for mask, block in enumerate(blocks) if mask > 0
    ]


def finish_kernel(mine_ref, rest_ref, out_ref, sems):
    width = mine_ref.shape[1]
    core = lax.axis_index("dp")
    copies = []
    for place, (half, source) in enumerate(((core, mine_ref), (1 - core, rest_ref))):
        columns = pl.ds(pl.multiple_of(half * width, 128), width)
        copies.append(
            pltpu.make_async_copy(source, out_ref.at[:, columns], sems.at[place])
        )
    for copy in copies:
        copy.start()
    for copy in copies:
        copy.wait()


def next_section(own, other):
    mine, rest = section_shift(own, 0), section_shift(other, 1)
    tokens, width = mine.shape
    return call(
        finish_kernel,
        pltpu.HBM((tokens, 2 * width), BF16),
        [VMEM, VMEM],
        HBM,
        [pltpu.SemaphoreType.DMA((2,))],
        0,
        8 * tokens * width,
    )(mine, rest)


def local(x_fwd, ids_fwd, route_fwd, x_bwd, ids_bwd, route_bwd, dy_bwd, w_gate, w_up, w_down):
    n_expert = lax.axis_size("expert")
    slab_width = w_gate.shape[-1]
    group = FF // slab_width
    experts = n_expert // group
    tokens = x_fwd.shape[1]
    spread = 4 * experts * group
    capacity = group * ((5 * tokens * TOP + spread - 1) // spread)
    rows = (2 * capacity + 15) // 16 * 16
    relative = n_expert <= 8
    plan = Plan(n_expert, rows, group, capacity, tokens, relative)
    gate_w, up_w, down_w = in_hbm(w_gate[0, 0]), in_hbm(w_up[0, 0]), in_hbm(w_down[0, 0])
    row_b, row_f = 0, META // 2

    own_x, send_x = pack(
        in_hbm(x_bwd[0]),
        *[in_hbm(value[0].T) for value in (ids_bwd, route_bwd, ids_fwd, route_fwd)],
    )
    other_x = exchange(send_x, "dp", 1)
    own_f, send_f, own_dy, send_dy = cut(in_hbm(x_fwd[0]), in_hbm(dy_bwd[0]))
    other_f = exchange(send_f, "dp", 1)
    other_dy = exchange(send_dy, "dp", 1)
    metas = (own_x, other_x)
    sent_x = dispatch(metas, own_x, other_x, plan, row_b, False, after=(own_f,))
    rows_b = to_experts(sent_x, relative)
    sent_f = dispatch(metas, own_f, other_f, plan, row_f, False, after=sent_x[:1])
    rows_f = to_experts(sent_f, relative)
    sent_dy = dispatch(metas, own_dy, other_dy, plan, row_b, True, after=sent_f[:1])
    cots_b = to_experts(sent_dy, relative)

    part_b = gate_up(rows_b, gate_w, up_w, after=sent_dy[:1])
    part_b_other = exchange(part_b, "dp", 1)

    part_f = gate_up(rows_f, gate_w, up_w, after=(part_b,))
    part_f_other = exchange(part_f, "dp", 1)
    down_blocks = down(part_f, part_f_other, down_w, n_expert)
    returned_f = to_experts(down_blocks, relative)

    part_d = d_hidden(cots_b, down_w, after=down_blocks[:1])
    part_d_other = exchange(part_d, "dp", 1)
    hidden, d_gate, d_up, *back_blocks = back(
        part_b, part_b_other, part_d, part_d_other, gate_w, up_w, n_expert
    )
    returned_b = to_experts(back_blocks, relative)

    sums_f = combine(metas, returned_f, plan, row_f, True, after=back_blocks[:1])
    y_next = next_section(*sums_f)
    grad_gate, grad_up, grad_down = grads(hidden, d_gate, d_up, rows_b, cots_b, after=sums_f[:1])
    sums_b = combine(metas, returned_b, plan, row_b, False, after=(in_hbm(grad_gate),))
    dx_next = next_section(*sums_b)
    return (
        y_next[None],
        dx_next[None],
        grad_gate[None, None],
        grad_up[None, None],
        grad_down[None, None],
    )


def solution(mesh):
    rows = P("section", ("expert", "dp"), None)
    by_feature = P("section", "expert", "dp", None)
    down_spec = P("section", "expert", None, "dp")
    return jax.shard_map(
        local,
        mesh=mesh,
        in_specs=(rows,) * 7 + (by_feature, by_feature, down_spec),
        out_specs=(rows, rows, by_feature, by_feature, down_spec),
        check_vma=False,
    )
```

```python
import functools

import jax
import jax.numpy as jnp
from jax import lax
from jax.experimental import pallas as pl
from jax.experimental.pallas import tpu as pltpu
from jax.sharding import PartitionSpec as P

FF = 1024
TOP = 2
TILE = 256
VMEM_LIMIT = 20 * 1024 * 1024
META = 16
COST = 10**7
F32 = jnp.float32
BF16 = jnp.bfloat16


def exchange(value, axis, mask):
    count = lax.axis_size(axis)
    return lax.ppermute(value, axis, [(source, source ^ mask) for source in range(count)])


def section_shift(value, flip):
    sections, cores = lax.axis_size("section"), lax.axis_size("dp")
    pairs = []
    for section in range(sections):
        for core in range(cores):
            target = ((section + 1) % sections) * cores + (core ^ flip)
            pairs.append((section * cores + core, target))
    return lax.ppermute(value, ("section", "dp"), pairs)


def dot(left, right, left_dim, right_dim):
    return lax.dot_general(
        left, right, (((left_dim,), (right_dim,)), ((), ())), preferred_element_type=F32
    )


VMEM = pl.BlockSpec(memory_space=pltpu.VMEM)
HBM = pl.BlockSpec(memory_space=pltpu.HBM)
AFTER = pl.BlockSpec(memory_space=pl.ANY)


def call(kernel, out_shape, in_specs, out_specs, scratch, grid=(), weight=1):
    return pl.pallas_call(
        kernel,
        out_shape=out_shape,
        grid=grid,
        in_specs=in_specs,
        out_specs=out_specs,
        scratch_shapes=scratch,
        compiler_params=pltpu.CompilerParams(vmem_limit_bytes=VMEM_LIMIT),
        cost_estimate=pl.CostEstimate(
            flops=weight * COST, bytes_accessed=1, transcendentals=0
        ),
    )


def array(*shape):
    return jax.ShapeDtypeStruct(shape, BF16)


def in_vmem(value):
    return pltpu.with_memory_space_constraint(value, pltpu.VMEM)


def in_hbm(value):
    return pltpu.with_memory_space_constraint(value, pltpu.HBM)


def halves(value_ref, own_ref, other_ref, sems, first):
    tokens, width = value_ref.shape[0], value_ref.shape[1] // 2
    core = lax.axis_index("dp")
    copies = []
    for place, (half, target) in enumerate(((core, own_ref), (1 - core, other_ref))):
        columns = pl.ds(pl.multiple_of(half * width, 128), width)
        copies.append(
            pltpu.make_async_copy(
                value_ref.at[:, columns], target.at[0:tokens], sems.at[first + place]
            )
        )
    for copy in copies:
        copy.start()
    return copies


def pack_kernel(x_ref, f_ref, dy_ref, *refs):
    sources, outs, (packed, sems), held = refs[:4], refs[4:9], refs[9:11], refs[11:]
    own_x, other_x, own_f, own_dy, other_rest = outs
    tokens = x_ref.shape[0]
    copies = halves(x_ref, own_x, other_x, sems, 0)
    small = [
        pltpu.make_async_copy(source, target, sems.at[6 + place])
        for place, (source, target) in enumerate(zip(sources, held))
    ]
    for copy in small:
        copy.start()
    copies += halves(f_ref, own_f, other_rest.at[0:tokens], sems, 2)
    copies += halves(dy_ref, own_dy, other_rest.at[tokens : 2 * tokens], sems, 4)
    packed[...] = jnp.zeros_like(packed)
    for copy in small:
        copy.wait()
    for start, ids, route in ((0, *held[:2]), (META // 2, *held[2:])):
        packed[start : start + 2, 0:tokens] = ids[...].astype(F32)
        rest = route[...]
        for piece in range(3):
            top = rest.astype(BF16).astype(F32)
            row = start + 2 + 2 * piece
            packed[row : row + 2, 0:tokens] = top
            rest = rest - top
    mine = packed[...]
    lanes = packed.shape[1]
    own_x[tokens : tokens + META, 0:lanes] = mine.astype(BF16)
    other_x[tokens : tokens + META, 0:lanes] = pltpu.roll(mine, tokens, 1).astype(BF16)
    for copy in copies:
        copy.wait()


def pack(x, f, dy, *small):
    tokens, width = x.shape[0], x.shape[1] // 2
    return call(
        pack_kernel,
        [array(tokens + META, width)] * 2 + [array(tokens, width)] * 2 + [array(2 * tokens, width)],
        [HBM] * 7,
        [VMEM] * 5,
        [pltpu.VMEM((META, 2 * tokens), F32), pltpu.SemaphoreType.DMA((10,))]
        + [pltpu.VMEM(value.shape, value.dtype) for value in small],
    )(x, f, dy, *small)


def load_kernel(*refs, count):
    sources, targets, sems = refs[:count], refs[-count - 1 : -1], refs[-1]
    copies = [
        pltpu.make_async_copy(source, target, sems.at[place])
        for place, (source, target) in enumerate(zip(sources, targets))
    ]
    for copy in copies:
        copy.start()
    for copy in copies:
        copy.wait()


def load(weights, after):
    return call(
        functools.partial(load_kernel, count=len(weights)),
        [array(*weight.shape) for weight in weights],
        [HBM] * len(weights) + [AFTER] * len(after),
        [VMEM] * len(weights),
        [pltpu.SemaphoreType.DMA((len(weights),))],
    )(*weights, *after)


class Plan:
    def __init__(self, blocks, rows, group, capacity, tokens, relative):
        self.blocks, self.rows, self.group = blocks, rows, group
        self.capacity, self.tokens, self.relative = capacity, tokens, relative


def slot_rows(own_meta, other_meta, plan, first_row):
    lanes = 2 * plan.tokens
    padded = max(8, plan.blocks)
    me = lax.axis_index("expert") if plan.relative else 0
    core = lax.axis_index("dp")
    meta = own_meta[plan.tokens : plan.tokens + META, 0:lanes].astype(F32)
    meta = meta + other_meta[plan.tokens : plan.tokens + META, 0:lanes].astype(F32)
    meta = meta[first_row : first_row + META // 2]
    first, second = meta[0:1], meta[1:2]
    route = meta[2:4] + meta[4:6] + meta[6:8]
    row = lax.broadcasted_iota(jnp.int32, (padded, lanes), 0)
    expert = ((row ^ me) // plan.group).astype(F32)
    is_first, is_second = expert == first, expert == second
    named = jnp.where(is_first | is_second, 1.0, 0.0)
    before = lax.broadcasted_iota(jnp.int32, (lanes, lanes), 0)
    after = lax.broadcasted_iota(jnp.int32, (lanes, lanes), 1)
    earlier = (before < after) & ((before < plan.tokens) == (after < plan.tokens))
    position = dot(named.astype(BF16), jnp.where(earlier, 1.0, 0.0).astype(BF16), 1, 0)
    lane = lax.broadcasted_iota(jnp.int32, (padded, lanes), 1)
    half = jnp.where(lane < plan.tokens, core, 1 - core).astype(F32)
    slot = jnp.where(named > 0.5, position + half * plan.capacity, -1.0)
    return slot, jnp.where(is_first, route[0:1], route[1:2])


def slot_table(slot, block, rows):
    index = lax.broadcasted_iota(jnp.int32, (rows, slot.shape[1]), 0).astype(F32)
    return jnp.where(index == slot[block : block + 1, :], 1.0, 0.0)


def dispatch_kernel(
    own_meta, other_meta, own_ref, other_ref, *refs, plan, first_row, other_row, weighted
):
    outs = refs[-plan.blocks :]
    width, tokens = outs[0].shape[1], plan.tokens
    slot, route = slot_rows(own_meta, other_meta, plan, first_row)
    values = jnp.concatenate([own_ref[0:tokens, :], other_ref[other_row : other_row + tokens, :]], axis=0)
    for block in range(plan.blocks):
        table = slot_table(slot, block, plan.rows)
        if weighted:
            scale = jnp.sum(table * route[block : block + 1, :], axis=1, keepdims=True)
        table = table.astype(BF16)
        for start in range(0, width, TILE):
            picked = dot(table, values[:, start : start + TILE], 1, 0)
            if weighted:
                picked = picked * scale
            outs[block][:, start : start + TILE] = picked.astype(BF16)


def dispatch(metas, own, other, plan, first_row, other_row, weighted, after=()):
    width = own.shape[1]
    return call(
        functools.partial(
            dispatch_kernel,
            plan=plan,
            first_row=first_row,
            other_row=other_row,
            weighted=weighted,
        ),
        [array(plan.rows, width)] * plan.blocks,
        [VMEM] * 4 + [AFTER] * len(after),
        [VMEM] * plan.blocks,
        [],
    )(*metas, own, other, *after)


def combine_kernel(own_meta, other_meta, *refs, plan, first_row, weighted):
    returned = refs[: plan.blocks]
    own_ref, other_ref = refs[-2:]
    width, tokens = returned[0].shape[1], plan.tokens
    slot, route = slot_rows(own_meta, other_meta, plan, first_row)
    high, low = [], []
    for block in range(plan.blocks):
        table = slot_table(slot, block, plan.rows)
        if weighted:
            table = table * route[block : block + 1, :]
        top = table.astype(BF16)
        high.append(top)
        low.append((table - top.astype(F32)).astype(BF16))
    high = jnp.concatenate(high, axis=0)
    low = jnp.concatenate(low, axis=0)
    for start in range(0, width, TILE):
        values = jnp.concatenate([ref[:, start : start + TILE] for ref in returned], axis=0)
        total = dot(high, values, 0, 0)
        if weighted:
            total += dot(low, values, 0, 0)
        total = total.astype(BF16)
        own_ref[:, start : start + TILE] = total[:tokens]
        other_ref[:, start : start + TILE] = total[tokens:]


def combine(metas, returned, plan, first_row, weighted, after=()):
    width = returned[0].shape[1]
    return call(
        functools.partial(combine_kernel, plan=plan, first_row=first_row, weighted=weighted),
        [array(plan.tokens, width)] * 2,
        [VMEM] * (2 + plan.blocks) + [AFTER] * len(after),
        [VMEM] * 2,
        [],
    )(*metas, *returned, *after)


def joined(refs):
    return jnp.concatenate([ref[...] for ref in refs], axis=0)


def gate_up_kernel(*refs, blocks):
    gate_w, up_w = refs[blocks : blocks + 2]
    out, rows = refs[-2:]
    rows[...] = joined(refs[:blocks])
    for start in range(0, out.shape[2], TILE):
        part = slice(start, start + TILE)
        out[0, :, part] = dot(rows[...], gate_w[:, part], 1, 0).astype(BF16)
        out[1, :, part] = dot(rows[...], up_w[:, part], 1, 0).astype(BF16)


def gate_up(inputs, gate_w, up_w, after=()):
    blocks, (rows, width) = len(inputs), inputs[0].shape
    units, total = gate_w.shape[1], blocks * rows
    return call(
        functools.partial(gate_up_kernel, blocks=blocks),
        array(2, total, units),
        [VMEM] * (blocks + 2) + [AFTER] * len(after),
        VMEM,
        [pltpu.VMEM((total, width), BF16)],
    )(*inputs, gate_w, up_w, *after)


def d_hidden_kernel(*refs, blocks):
    down_w = refs[blocks]
    out, rows = refs[-2:]
    rows[...] = joined(refs[:blocks])
    for start in range(0, out.shape[1], TILE):
        part = slice(start, start + TILE)
        out[:, part] = dot(rows[...], down_w[part, :], 1, 1).astype(BF16)


def d_hidden(inputs, down_w, after=()):
    blocks, (rows, width) = len(inputs), inputs[0].shape
    units, total = down_w.shape[0], blocks * rows
    return call(
        functools.partial(d_hidden_kernel, blocks=blocks),
        array(total, units),
        [VMEM] * (blocks + 1) + [AFTER] * len(after),
        VMEM,
        [pltpu.VMEM((total, width), BF16)],
        weight=1000,
    )(*inputs, down_w, *after)


def scatter_tile(value, outs, part):
    rows = outs[0].shape[0]
    for block, out in enumerate(outs):
        out[:, part] = value[block * rows : (block + 1) * rows]


def gate_and_up(own_ref, other_ref, part):
    gate = own_ref[0, :, part].astype(F32) + other_ref[0, :, part].astype(F32)
    up = own_ref[1, :, part].astype(F32) + other_ref[1, :, part].astype(F32)
    return gate, up


def down_kernel(own_ref, other_ref, down_w, *refs, blocks):
    outs, hidden = refs[-1 - blocks : -1], refs[-1]
    for start in range(0, hidden.shape[1], TILE):
        part = slice(start, start + TILE)
        gate, up = gate_and_up(own_ref, other_ref, part)
        hidden[:, part] = (gate * jax.nn.sigmoid(gate) * up).astype(BF16)
    for start in range(0, outs[0].shape[1], TILE):
        part = slice(start, start + TILE)
        scatter_tile(dot(hidden[...], down_w[:, part], 1, 0).astype(BF16), outs, part)


def down(own, other, down_w, blocks, after=()):
    _, total, units = own.shape
    width, rows = down_w.shape[1], total // blocks
    return call(
        functools.partial(down_kernel, blocks=blocks),
        [array(rows, width)] * blocks,
        [VMEM] * 3 + [AFTER] * len(after),
        [VMEM] * blocks,
        [pltpu.VMEM((total, units), BF16)],
    )(own, other, down_w, *after)


def back_kernel(
    own_ref, other_ref, own_d, other_d, gate_w, up_w, hidden, d_gate, d_up, *outs
):
    for start in range(0, hidden.shape[1], TILE):
        part = slice(start, start + TILE)
        gate, up = gate_and_up(own_ref, other_ref, part)
        d_hid = own_d[:, part].astype(F32) + other_d[:, part].astype(F32)
        sigmoid = jax.nn.sigmoid(gate)
        activated = gate * sigmoid
        hidden[:, part] = (activated * up).astype(BF16)
        d_up[:, part] = (d_hid * activated).astype(BF16)
        d_gate[:, part] = (d_hid * up * sigmoid * (1.0 + gate * (1.0 - sigmoid))).astype(BF16)
    for start in range(0, outs[0].shape[1], TILE):
        part = slice(start, start + TILE)
        total = dot(d_gate[...], gate_w[part, :], 1, 1)
        total += dot(d_up[...], up_w[part, :], 1, 1)
        scatter_tile(total.astype(BF16), outs, part)


def back(own, other, own_d, other_d, gate_w, up_w, blocks):
    _, total, units = own.shape
    width, rows = gate_w.shape[0], total // blocks
    return call(
        back_kernel,
        [array(total, units)] * 3 + [array(rows, width)] * blocks,
        [VMEM] * 6,
        [VMEM] * (3 + blocks),
        [],
    )(own, other, own_d, other_d, gate_w, up_w)


def grad_kernel(hidden, d_gate, d_up, *refs, blocks):
    inputs, cots = refs[:blocks], refs[blocks : 2 * blocks]
    grad_gate, grad_up, grad_down, turned, cot_all = refs[-5:]

    @pl.when(pl.program_id(0) == 0)
    def _():
        for start in range(0, turned.shape[0], TILE):
            part = slice(start, start + TILE)
            piece = jnp.concatenate([ref[:, part] for ref in inputs], axis=0)
            turned[part, :] = piece.T
        cot_all[...] = joined(cots)

    part = pl.ds(pl.multiple_of(pl.program_id(0) * TILE, TILE), TILE)
    grad_gate[...] = dot(turned[...], d_gate[:, part], 1, 0).astype(BF16)
    grad_up[...] = dot(turned[...], d_up[:, part], 1, 0).astype(BF16)
    grad_down[...] = dot(hidden[:, part], cot_all[...], 0, 0).astype(BF16)


def grads(hidden, d_gate, d_up, inputs, cots, after=()):
    blocks, (rows, width) = len(inputs), inputs[0].shape
    total, units = hidden.shape
    by_column = pl.BlockSpec((width, TILE), lambda i: (0, i))
    return call(
        functools.partial(grad_kernel, blocks=blocks),
        [
            pltpu.HBM((width, units), BF16),
            pltpu.HBM((width, units), BF16),
            pltpu.HBM((units, width), BF16),
        ],
        [VMEM] * (3 + 2 * blocks) + [AFTER] * len(after),
        [by_column, by_column, pl.BlockSpec((TILE, width), lambda i: (i, 0))],
        [pltpu.VMEM((width, total), BF16), pltpu.VMEM((total, width), BF16)],
        grid=(units // TILE,),
    )(hidden, d_gate, d_up, *inputs, *cots, *after)


def to_experts(blocks, relative):
    if not relative:
        stacked = lax.all_to_all(jnp.stack(blocks), "expert", split_axis=0, concat_axis=0)
        return [stacked[block] for block in range(len(blocks))]
    return [blocks[0]] + [
        exchange(block, "expert", mask) for mask, block in enumerate(blocks) if mask > 0
    ]


def finish_kernel(mine_ref, rest_ref, out_ref, sems):
    width = mine_ref.shape[1]
    core = lax.axis_index("dp")
    copies = []
    for place, (half, source) in enumerate(((core, mine_ref), (1 - core, rest_ref))):
        columns = pl.ds(pl.multiple_of(half * width, 128), width)
        copies.append(
            pltpu.make_async_copy(source, out_ref.at[:, columns], sems.at[place])
        )
    for copy in copies:
        copy.start()
    for copy in copies:
        copy.wait()


def next_section(own, other):
    mine, rest = section_shift(own, 0), section_shift(other, 1)
    tokens, width = mine.shape
    return call(
        finish_kernel,
        pltpu.HBM((tokens, 2 * width), BF16),
        [VMEM, VMEM],
        HBM,
        [pltpu.SemaphoreType.DMA((2,))],
    )(mine, rest)


def local(x_fwd, ids_fwd, route_fwd, x_bwd, ids_bwd, route_bwd, dy_bwd, w_gate, w_up, w_down):
    n_expert = lax.axis_size("expert")
    slab_width = w_gate.shape[-1]
    group = FF // slab_width
    experts = n_expert // group
    tokens = x_fwd.shape[1]
    spread = 4 * experts * group
    capacity = group * ((5 * tokens * TOP + spread - 1) // spread)
    rows = (2 * capacity + 15) // 16 * 16
    relative = n_expert <= 8
    plan = Plan(n_expert, rows, group, capacity, tokens, relative)
    row_b, row_f = 0, META // 2

    own_x, send_x, own_f, own_dy, send_rest = pack(
        *[in_hbm(value[0]) for value in (x_bwd, x_fwd, dy_bwd)],
        *[in_hbm(value[0].T) for value in (ids_bwd, route_bwd, ids_fwd, route_fwd)],
    )
    other_x = exchange(send_x, "dp", 1)
    other_rest = exchange(send_rest, "dp", 1)
    metas = (own_x, other_x)
    sent_x = dispatch(metas, own_x, other_x, plan, row_b, 0, False)
    rows_b = to_experts(sent_x, relative)
    sent_f = dispatch(metas, own_f, other_rest, plan, row_f, 0, False, after=sent_x[:1])
    rows_f = to_experts(sent_f, relative)
    gate_w, up_w, down_w = load(
        [in_hbm(weight[0, 0]) for weight in (w_gate, w_up, w_down)], after=sent_f[:1]
    )
    sent_dy = dispatch(
        metas, own_dy, other_rest, plan, row_b, tokens, True, after=(in_vmem(down_w),)
    )
    cots_b = to_experts(sent_dy, relative)

    part_b = gate_up(rows_b, gate_w, up_w, after=sent_dy[:1])
    part_b_other = exchange(part_b, "dp", 1)
    part_f = gate_up(rows_f, gate_w, up_w, after=(part_b,))
    part_f_other = exchange(part_f, "dp", 1)
    part_d = d_hidden(cots_b, down_w, after=(part_f,))
    part_d_other = exchange(part_d, "dp", 1)
    down_blocks = down(part_f, part_f_other, down_w, n_expert, after=(part_d,))
    returned_f = to_experts(down_blocks, relative)
    hidden, d_gate, d_up, *back_blocks = back(
        part_b, part_b_other, part_d, part_d_other, gate_w, up_w, n_expert
    )
    returned_b = to_experts(back_blocks, relative)

    sums_f = combine(metas, returned_f, plan, row_f, True, after=back_blocks[:1])
    y_next = next_section(*sums_f)
    grad_gate, grad_up, grad_down = grads(hidden, d_gate, d_up, rows_b, cots_b, after=sums_f[:1])
    sums_b = combine(metas, returned_b, plan, row_b, False, after=(in_hbm(grad_gate),))
    dx_next = next_section(*sums_b)
    return (
        y_next[None],
        dx_next[None],
        grad_gate[None, None],
        grad_up[None, None],
        grad_down[None, None],
    )


def solution(mesh):
    rows = P("section", ("expert", "dp"), None)
    by_feature = P("section", "expert", "dp", None)
    down_spec = P("section", "expert", None, "dp")
    return jax.shard_map(
        local,
        mesh=mesh,
        in_specs=(rows,) * 7 + (by_feature, by_feature, down_spec),
        out_specs=(rows, rows, by_feature, by_feature, down_spec),
        check_vma=False,
    )
```

```python
import functools

import jax
import jax.numpy as jnp
from jax import lax
from jax.experimental import pallas as pl
from jax.experimental.pallas import tpu as pltpu
from jax.sharding import PartitionSpec as P

FF = 1024
TOP = 2
TILE = 256
VMEM_LIMIT = 20 * 1024 * 1024
META = 16
COST = 10**7
F32 = jnp.float32
BF16 = jnp.bfloat16


def exchange(value, axis, mask):
    count = lax.axis_size(axis)
    return lax.ppermute(value, axis, [(source, source ^ mask) for source in range(count)])


def section_shift(value, flip):
    sections, cores = lax.axis_size("section"), lax.axis_size("dp")
    pairs = []
    for section in range(sections):
        for core in range(cores):
            target = ((section + 1) % sections) * cores + (core ^ flip)
            pairs.append((section * cores + core, target))
    return lax.ppermute(value, ("section", "dp"), pairs)


def dot(left, right, left_dim, right_dim):
    return lax.dot_general(
        left, right, (((left_dim,), (right_dim,)), ((), ())), preferred_element_type=F32
    )


VMEM = pl.BlockSpec(memory_space=pltpu.VMEM)
HBM = pl.BlockSpec(memory_space=pltpu.HBM)
AFTER = pl.BlockSpec(memory_space=pl.ANY)


def call(kernel, out_shape, in_specs, out_specs, scratch, grid=(), weight=1, aliases={}):
    return pl.pallas_call(
        kernel,
        out_shape=out_shape,
        grid=grid,
        in_specs=in_specs,
        out_specs=out_specs,
        scratch_shapes=scratch,
        input_output_aliases=aliases,
        compiler_params=pltpu.CompilerParams(vmem_limit_bytes=VMEM_LIMIT),
        cost_estimate=pl.CostEstimate(
            flops=weight * COST, bytes_accessed=1, transcendentals=0
        ),
    )


def array(*shape):
    return jax.ShapeDtypeStruct(shape, BF16)


def in_vmem(value):
    return pltpu.with_memory_space_constraint(value, pltpu.VMEM)


def in_hbm(value):
    return pltpu.with_memory_space_constraint(value, pltpu.HBM)


def halves(value_ref, own_ref, other_ref, sems, first):
    tokens, width = value_ref.shape[0], value_ref.shape[1] // 2
    core = lax.axis_index("dp")
    copies = []
    for place, (half, target) in enumerate(((core, own_ref), (1 - core, other_ref))):
        columns = pl.ds(pl.multiple_of(half * width, 128), width)
        copies.append(
            pltpu.make_async_copy(
                value_ref.at[:, columns], target.at[0:tokens], sems.at[first + place]
            )
        )
    for copy in copies:
        copy.start()
    return copies


def pack_kernel(f_ref, x_ref, dy_ref, *refs):
    sources, outs, (packed, sems), held = refs[:4], refs[4:9], refs[9:11], refs[11:]
    own_f, other_f, own_x, own_dy, other_rest = outs
    tokens = f_ref.shape[0]
    copies = halves(f_ref, own_f, other_f, sems, 0)
    small = [
        pltpu.make_async_copy(source, target, sems.at[6 + place])
        for place, (source, target) in enumerate(zip(sources, held))
    ]
    for copy in small:
        copy.start()
    copies += halves(x_ref, own_x, other_rest.at[0:tokens], sems, 2)
    copies += halves(dy_ref, own_dy, other_rest.at[tokens : 2 * tokens], sems, 4)
    packed[...] = jnp.zeros_like(packed)
    for copy in small:
        copy.wait()
    for start, ids, route in ((0, *held[:2]), (META // 2, *held[2:])):
        packed[start : start + 2, 0:tokens] = ids[...].astype(F32)
        rest = route[...]
        for piece in range(3):
            top = rest.astype(BF16).astype(F32)
            row = start + 2 + 2 * piece
            packed[row : row + 2, 0:tokens] = top
            rest = rest - top
    mine = packed[...]
    lanes = packed.shape[1]
    own_f[tokens : tokens + META, 0:lanes] = mine.astype(BF16)
    other_f[tokens : tokens + META, 0:lanes] = pltpu.roll(mine, tokens, 1).astype(BF16)
    for copy in copies:
        copy.wait()


def pack(f, x, dy, *small):
    tokens, width = f.shape[0], f.shape[1] // 2
    return call(
        pack_kernel,
        [array(tokens + META, width)] * 2 + [array(tokens, width)] * 2 + [array(2 * tokens, width)],
        [HBM] * 7,
        [VMEM] * 5,
        [pltpu.VMEM((META, 2 * tokens), F32), pltpu.SemaphoreType.DMA((10,))]
        + [pltpu.VMEM(value.shape, value.dtype) for value in small],
    )(f, x, dy, *small)


def load_kernel(*refs, count):
    sources, targets, sems = refs[:count], refs[-count - 1 : -1], refs[-1]
    copies = [
        pltpu.make_async_copy(source, target, sems.at[place])
        for place, (source, target) in enumerate(zip(sources, targets))
    ]
    for copy in copies:
        copy.start()
    for copy in copies:
        copy.wait()


def load(weights, after):
    return call(
        functools.partial(load_kernel, count=len(weights)),
        [array(*weight.shape) for weight in weights],
        [HBM] * len(weights) + [AFTER] * len(after),
        [VMEM] * len(weights),
        [pltpu.SemaphoreType.DMA((len(weights),))],
    )(*weights, *after)


class Plan:
    def __init__(self, blocks, part, group, tokens, relative):
        self.blocks, self.part, self.group = blocks, part, group
        self.tokens, self.relative = tokens, relative


def slot_rows(own_meta, other_meta, plan, first_row):
    lanes = 2 * plan.tokens
    padded = max(8, plan.blocks)
    me = lax.axis_index("expert") if plan.relative else 0
    meta = own_meta[plan.tokens : plan.tokens + META, 0:lanes].astype(F32)
    meta = meta + other_meta[plan.tokens : plan.tokens + META, 0:lanes].astype(F32)
    meta = meta[first_row : first_row + META // 2]
    first, second = meta[0:1], meta[1:2]
    route = meta[2:4] + meta[4:6] + meta[6:8]
    row = lax.broadcasted_iota(jnp.int32, (padded, lanes), 0)
    expert = ((row ^ me) // plan.group).astype(F32)
    is_first, is_second = expert == first, expert == second
    named = jnp.where(is_first | is_second, 1.0, 0.0)
    before = lax.broadcasted_iota(jnp.int32, (lanes, lanes), 0)
    after = lax.broadcasted_iota(jnp.int32, (lanes, lanes), 1)
    earlier = (before < after) & ((before < plan.tokens) == (after < plan.tokens))
    position = dot(named.astype(BF16), jnp.where(earlier, 1.0, 0.0).astype(BF16), 1, 0)
    lane = lax.broadcasted_iota(jnp.int32, (padded, lanes), 1)
    slot = position + jnp.where(lane < plan.tokens, 0, plan.part).astype(F32)
    slot = jnp.where(named > 0.5, slot, -1.0)
    return slot, jnp.where(is_first, route[0:1], route[1:2])


def slot_table(slot, block, first, rows):
    index = lax.broadcasted_iota(jnp.int32, (rows, slot.shape[1]), 0) + first
    index = index.astype(F32)
    return jnp.where(index == slot[block : block + 1, :], 1.0, 0.0)


def dispatch_kernel(
    own_meta, other_meta, own_ref, other_ref, *refs, plan, first_row, other_row, weighted, passed
):
    outs = refs[len(refs) - plan.blocks - passed : len(refs) - passed]
    width, tokens = outs[0].shape[1], plan.tokens
    slot, route = slot_rows(own_meta, other_meta, plan, first_row)
    values = jnp.concatenate([own_ref[0:tokens, :], other_ref[other_row : other_row + tokens, :]], axis=0)
    for block in range(plan.blocks):
        table = slot_table(slot, block, 0, 2 * plan.part)
        if weighted:
            scale = jnp.sum(table * route[block : block + 1, :], axis=1, keepdims=True)
        table = table.astype(BF16)
        for start in range(0, width, TILE):
            picked = dot(table, values[:, start : start + TILE], 1, 0)
            if weighted:
                picked = picked * scale
            outs[block][:, start : start + TILE] = picked.astype(BF16)


def dispatch(metas, own, other, plan, first_row, other_row, weighted, after=(), passing=()):
    width = own.shape[1]
    return call(
        functools.partial(
            dispatch_kernel,
            plan=plan,
            first_row=first_row,
            other_row=other_row,
            weighted=weighted,
            passed=len(passing),
        ),
        [array(2 * plan.part, width)] * plan.blocks + [array(*value.shape) for value in passing],
        [VMEM] * (4 + len(passing)) + [AFTER] * len(after),
        [VMEM] * (plan.blocks + len(passing)),
        [],
        aliases={4 + place: plan.blocks + place for place in range(len(passing))},
    )(*metas, own, other, *passing, *after)


def combine_kernel(own_meta, other_meta, *refs, plan, first_row, weighted, other):
    returned, out = refs[: plan.blocks], refs[-1]
    width, tokens = out.shape[1], plan.tokens
    slot, route = slot_rows(own_meta, other_meta, plan, first_row)
    table = []
    for block in range(plan.blocks):
        table.append(slot_table(slot, block, plan.part if other else 0, plan.part))
        if weighted:
            table[block] = table[block] * route[block : block + 1, :]
    table = jnp.concatenate(table, axis=0)
    high = table.astype(BF16)
    low = (table - high.astype(F32)).astype(BF16)
    for start in range(0, width, TILE):
        part = slice(start, start + TILE)
        values = jnp.concatenate([ref[:, part].astype(F32) for ref in returned], axis=0)
        values = values.astype(BF16)
        total = dot(high, values, 0, 0)
        if weighted:
            total += dot(low, values, 0, 0)
        out[:, part] = total[tokens if other else 0 :][:tokens].astype(BF16)


def combine(metas, returned, plan, first_row, weighted, other, after=(), weight=1):
    return call(
        functools.partial(
            combine_kernel, plan=plan, first_row=first_row, weighted=weighted, other=other
        ),
        array(plan.tokens, returned[0].shape[1]),
        [VMEM] * (2 + plan.blocks) + [AFTER] * len(after),
        VMEM,
        [],
        weight=weight,
    )(*metas, *returned, *after)


def joined(refs):
    return jnp.concatenate([ref[...] for ref in refs], axis=0)


def gate_up_kernel(*refs, blocks):
    gate_w, up_w = refs[blocks : blocks + 2]
    out, rows = refs[-2:]
    rows[...] = joined(refs[:blocks])
    for start in range(0, out.shape[2], TILE):
        part = slice(start, start + TILE)
        out[0, :, part] = dot(rows[...], gate_w[:, part], 1, 0).astype(BF16)
        out[1, :, part] = dot(rows[...], up_w[:, part], 1, 0).astype(BF16)


def gate_up(inputs, gate_w, up_w, after=(), weight=1):
    blocks, (rows, width) = len(inputs), inputs[0].shape
    units, total = gate_w.shape[1], blocks * rows
    return call(
        functools.partial(gate_up_kernel, blocks=blocks),
        array(2, total, units),
        [VMEM] * (blocks + 2) + [AFTER] * len(after),
        VMEM,
        [pltpu.VMEM((total, width), BF16)],
        weight=weight,
    )(*inputs, gate_w, up_w, *after)


def d_hidden_kernel(*refs, blocks):
    down_w = refs[blocks]
    out, rows = refs[-2:]
    rows[...] = joined(refs[:blocks])
    for start in range(0, out.shape[1], TILE):
        part = slice(start, start + TILE)
        out[:, part] = dot(rows[...], down_w[part, :], 1, 1).astype(BF16)


def d_hidden(inputs, down_w, after=(), weight=1):
    blocks, (rows, width) = len(inputs), inputs[0].shape
    units, total = down_w.shape[0], blocks * rows
    return call(
        functools.partial(d_hidden_kernel, blocks=blocks),
        array(total, units),
        [VMEM] * (blocks + 1) + [AFTER] * len(after),
        VMEM,
        [pltpu.VMEM((total, width), BF16)],
        weight=weight,
    )(*inputs, down_w, *after)


def scatter_tile(value, outs, columns):
    blocks, part = len(outs) // 2, outs[0].shape[0]
    for place, out in enumerate(outs):
        first = (2 * (place % blocks) + place // blocks) * part
        out[:, columns] = value[first : first + part].astype(BF16)


def total_of(own, other, part):
    own, other = own.astype(F32), other.astype(F32)
    rows = own.shape[0]
    turned = []
    for first in range(0, rows, 2 * part):
        turned += [other[first + part : first + 2 * part], other[first : first + part]]
    return own + jnp.concatenate(turned, axis=0)


def down_kernel(own_ref, other_ref, down_w, *refs, blocks):
    outs, hidden = refs[-1 - 2 * blocks : -1], refs[-1]
    part = outs[0].shape[0]
    for start in range(0, hidden.shape[1], TILE):
        columns = slice(start, start + TILE)
        gate = total_of(own_ref[0, :, columns], other_ref[0, :, columns], part)
        up = total_of(own_ref[1, :, columns], other_ref[1, :, columns], part)
        hidden[:, columns] = (gate * jax.nn.sigmoid(gate) * up).astype(BF16)
    for start in range(0, outs[0].shape[1], TILE):
        columns = slice(start, start + TILE)
        scatter_tile(dot(hidden[...], down_w[:, columns], 1, 0), outs, columns)


def down(own, other, down_w, plan, after=()):
    _, total, units = own.shape
    return call(
        functools.partial(down_kernel, blocks=plan.blocks),
        [array(plan.part, down_w.shape[1])] * (2 * plan.blocks),
        [VMEM] * 3 + [AFTER] * len(after),
        [VMEM] * (2 * plan.blocks),
        [pltpu.VMEM((total, units), BF16)],
    )(own, other, down_w, *after)


def back_kernel(
    own_ref, other_ref, own_d, other_d, gate_w, up_w, hidden, d_gate, d_up, *outs
):
    part = outs[0].shape[0]
    for start in range(0, hidden.shape[1], TILE):
        columns = slice(start, start + TILE)
        gate = total_of(own_ref[0, :, columns], other_ref[0, :, columns], part)
        up = total_of(own_ref[1, :, columns], other_ref[1, :, columns], part)
        d_hid = total_of(own_d[:, columns], other_d[:, columns], part)
        sigmoid = jax.nn.sigmoid(gate)
        activated = gate * sigmoid
        hidden[:, columns] = (activated * up).astype(BF16)
        d_up[:, columns] = (d_hid * activated).astype(BF16)
        d_gate[:, columns] = (
            d_hid * up * sigmoid * (1.0 + gate * (1.0 - sigmoid))
        ).astype(BF16)
    for start in range(0, outs[0].shape[1], TILE):
        columns = slice(start, start + TILE)
        total = dot(d_gate[...], gate_w[columns, :], 1, 1)
        total += dot(d_up[...], up_w[columns, :], 1, 1)
        scatter_tile(total, outs, columns)


def back(own, other, own_d, other_d, gate_w, up_w, plan):
    _, total, units = own.shape
    return call(
        back_kernel,
        [array(total, units)] * 3 + [array(plan.part, gate_w.shape[0])] * (2 * plan.blocks),
        [VMEM] * 6,
        [VMEM] * (3 + 2 * plan.blocks),
        [],
    )(own, other, own_d, other_d, gate_w, up_w)


def grad_in_kernel(d_gate, d_up, *refs, blocks):
    inputs, (grad_gate, grad_up, turned) = refs[:blocks], refs[-3:]

    @pl.when(pl.program_id(0) == 0)
    def _():
        for start in range(0, turned.shape[0], TILE):
            part = slice(start, start + TILE)
            piece = jnp.concatenate([ref[:, part] for ref in inputs], axis=0)
            turned[part, :] = piece.T

    part = pl.ds(pl.multiple_of(pl.program_id(0) * TILE, TILE), TILE)
    grad_gate[...] = dot(turned[...], d_gate[:, part], 1, 0).astype(BF16)
    grad_up[...] = dot(turned[...], d_up[:, part], 1, 0).astype(BF16)


def grad_in(d_gate, d_up, inputs, after=(), weight=1):
    blocks, (rows, width) = len(inputs), inputs[0].shape
    total, units = d_gate.shape
    return call(
        functools.partial(grad_in_kernel, blocks=blocks),
        [pltpu.HBM((width, units), BF16)] * 2,
        [VMEM] * (2 + blocks) + [AFTER] * len(after),
        [pl.BlockSpec((width, TILE), lambda i: (0, i))] * 2,
        [pltpu.VMEM((width, total), BF16)],
        grid=(units // TILE,),
        weight=weight,
    )(d_gate, d_up, *inputs, *after)


def grad_down_kernel(hidden, *refs, blocks):
    cots, (grad, cot_all) = refs[:blocks], refs[-2:]

    @pl.when(pl.program_id(0) == 0)
    def _():
        cot_all[...] = joined(cots)

    part = pl.ds(pl.multiple_of(pl.program_id(0) * TILE, TILE), TILE)
    grad[...] = dot(hidden[:, part], cot_all[...], 0, 0).astype(BF16)


def grad_down(hidden, cots, after=()):
    blocks, (rows, width) = len(cots), cots[0].shape
    total, units = hidden.shape
    return call(
        functools.partial(grad_down_kernel, blocks=blocks),
        pltpu.HBM((units, width), BF16),
        [VMEM] * (1 + blocks) + [AFTER] * len(after),
        pl.BlockSpec((TILE, width), lambda i: (i, 0)),
        [pltpu.VMEM((total, width), BF16)],
        grid=(units // TILE,),
    )(hidden, *cots, *after)


def to_experts(blocks, relative):
    if not relative:
        stacked = lax.all_to_all(jnp.stack(blocks), "expert", split_axis=0, concat_axis=0)
        return [stacked[block] for block in range(len(blocks))]
    return [blocks[0]] + [
        exchange(block, "expert", mask) for mask, block in enumerate(blocks) if mask > 0
    ]


def finish_kernel(mine_ref, rest_ref, out_ref, sems):
    width = mine_ref.shape[1]
    core = lax.axis_index("dp")
    copies = []
    for place, (half, source) in enumerate(((core, mine_ref), (1 - core, rest_ref))):
        columns = pl.ds(pl.multiple_of(half * width, 128), width)
        copies.append(
            pltpu.make_async_copy(source, out_ref.at[:, columns], sems.at[place])
        )
    for copy in copies:
        copy.start()
    for copy in copies:
        copy.wait()


def finish(mine, rest):
    tokens, width = mine.shape
    return call(
        finish_kernel,
        pltpu.HBM((tokens, 2 * width), BF16),
        [VMEM, VMEM],
        HBM,
        [pltpu.SemaphoreType.DMA((2,))],
    )(mine, rest)


def local(x_fwd, ids_fwd, route_fwd, x_bwd, ids_bwd, route_bwd, dy_bwd, w_gate, w_up, w_down):
    n_expert = lax.axis_size("expert")
    slab_width = w_gate.shape[-1]
    group = FF // slab_width
    experts = n_expert // group
    tokens = x_fwd.shape[1]
    spread = 4 * experts * group
    capacity = group * ((5 * tokens * TOP + spread - 1) // spread)
    relative = n_expert <= 8
    plan = Plan(n_expert, (capacity + 7) // 8 * 8, group, tokens, relative)
    row_b, row_f = 0, META // 2

    own_f, send_f, own_x, own_dy, send_rest = pack(
        *[in_hbm(value[0]) for value in (x_fwd, x_bwd, dy_bwd)],
        *[in_hbm(value[0].T) for value in (ids_bwd, route_bwd, ids_fwd, route_fwd)],
    )
    other_f = exchange(send_f, "dp", 1)
    metas = (own_f, other_f)
    *sent_f, send_rest = dispatch(
        metas, own_f, other_f, plan, row_f, 0, False, passing=(send_rest,)
    )
    rows_f = to_experts(sent_f, relative)
    other_rest = exchange(send_rest, "dp", 1)
    sent_x = dispatch(metas, own_x, other_rest, plan, row_b, 0, False)
    rows_b = to_experts(sent_x, relative)
    gate_w, up_w, down_w = load(
        [in_hbm(weight[0, 0]) for weight in (w_gate, w_up, w_down)], after=sent_x[:1]
    )
    sent_dy = dispatch(
        metas, own_dy, other_rest, plan, row_b, tokens, True, after=(in_vmem(down_w),)
    )
    cots_b = to_experts(sent_dy, relative)

    part_f = gate_up(rows_f, gate_w, up_w, after=sent_dy[:1])
    part_f_other = exchange(part_f, "dp", 1)
    part_b = gate_up(rows_b, gate_w, up_w, after=(part_f,), weight=1000)
    part_b_other = exchange(part_b, "dp", 1)
    down_blocks = down(part_f, part_f_other, down_w, plan, after=(part_b,))
    part_d = d_hidden(cots_b, down_w, after=(down_blocks[0], in_vmem(part_b_other)), weight=1000)
    part_d_other = exchange(part_d, "dp", 1)
    own_back_f = to_experts(down_blocks[:n_expert], relative)
    other_back_f = to_experts(down_blocks[n_expert:], relative)
    hidden, d_gate, d_up, *back_blocks = back(
        part_b, part_b_other, part_d, part_d_other, gate_w, up_w, plan
    )
    own_back_b = to_experts(back_blocks[:n_expert], relative)
    other_back_b = to_experts(back_blocks[n_expert:], relative)

    own_sum = combine(
        metas, own_back_f, plan, row_f, True, False, after=back_blocks[:1]
    )
    y_mine = section_shift(own_sum, 0)
    grad_d = grad_down(hidden, cots_b, after=(own_sum,))
    other_sum = combine(
        metas, other_back_f, plan, row_f, True, True, after=(in_hbm(grad_d),), weight=150
    )
    y_rest = section_shift(other_sum, 1)
    own_sum = combine(
        metas, own_back_b, plan, row_b, False, False, after=(other_sum, in_vmem(y_mine)), weight=150
    )
    dx_mine = section_shift(own_sum, 0)
    y_next = finish(y_mine, y_rest)
    grad_g, grad_u = grad_in(d_gate, d_up, rows_b, after=(own_sum, in_hbm(y_next)))
    other_sum = combine(
        metas,
        other_back_b,
        plan,
        row_b,
        False,
        True,
        after=(in_hbm(grad_g),),
    )
    dx_rest = section_shift(other_sum, 1)
    dx_next = finish(dx_mine, dx_rest)
    return (
        y_next[None],
        dx_next[None],
        grad_g[None, None],
        grad_u[None, None],
        grad_d[None, None],
    )


def solution(mesh):
    rows = P("section", ("expert", "dp"), None)
    by_feature = P("section", "expert", "dp", None)
    down_spec = P("section", "expert", None, "dp")
    return jax.shard_map(
        local,
        mesh=mesh,
        in_specs=(rows,) * 7 + (by_feature, by_feature, down_spec),
        out_specs=(rows, rows, by_feature, by_feature, down_spec),
        check_vma=False,
    )
```

```python
import functools

import jax
import jax.numpy as jnp
from jax import lax
from jax.experimental import pallas as pl
from jax.experimental.pallas import tpu as pltpu
from jax.sharding import PartitionSpec as P

FF = 1024
TOP = 2
TILE = 256
VMEM_LIMIT = 20 * 1024 * 1024
META = 16
COST = 10**7
F32 = jnp.float32
BF16 = jnp.bfloat16


def exchange(value, axis, mask):
    count = lax.axis_size(axis)
    return lax.ppermute(value, axis, [(source, source ^ mask) for source in range(count)])


def section_shift(value, flip):
    sections, cores = lax.axis_size("section"), lax.axis_size("dp")
    pairs = []
    for section in range(sections):
        for core in range(cores):
            target = ((section + 1) % sections) * cores + (core ^ flip)
            pairs.append((section * cores + core, target))
    return lax.ppermute(value, ("section", "dp"), pairs)


def dot(left, right, left_dim, right_dim):
    return lax.dot_general(
        left, right, (((left_dim,), (right_dim,)), ((), ())), preferred_element_type=F32
    )


VMEM = pl.BlockSpec(memory_space=pltpu.VMEM)
HBM = pl.BlockSpec(memory_space=pltpu.HBM)
AFTER = pl.BlockSpec(memory_space=pl.ANY)


def call(kernel, out_shape, in_specs, out_specs, scratch, grid=(), weight=1, aliases={}):
    return pl.pallas_call(
        kernel,
        out_shape=out_shape,
        grid=grid,
        in_specs=in_specs,
        out_specs=out_specs,
        scratch_shapes=scratch,
        input_output_aliases=aliases,
        compiler_params=pltpu.CompilerParams(vmem_limit_bytes=VMEM_LIMIT),
        cost_estimate=pl.CostEstimate(
            flops=weight * COST, bytes_accessed=1, transcendentals=0
        ),
    )


def array(*shape):
    return jax.ShapeDtypeStruct(shape, BF16)


def in_vmem(value):
    return pltpu.with_memory_space_constraint(value, pltpu.VMEM)


def in_hbm(value):
    return pltpu.with_memory_space_constraint(value, pltpu.HBM)


def halves(value_ref, own_ref, other_ref, sems, first):
    tokens, width = value_ref.shape[0], value_ref.shape[1] // 2
    core = lax.axis_index("dp")
    copies = []
    for place, (half, target) in enumerate(((core, own_ref), (1 - core, other_ref))):
        columns = pl.ds(pl.multiple_of(half * width, 128), width)
        copies.append(
            pltpu.make_async_copy(
                value_ref.at[:, columns], target.at[0:tokens], sems.at[first + place]
            )
        )
    for copy in copies:
        copy.start()
    return copies


def pack_kernel(f_ref, x_ref, dy_ref, *refs):
    sources, outs, (packed, sems), held = refs[:4], refs[4:9], refs[9:11], refs[11:]
    own_f, other_f, own_x, own_dy, other_rest = outs
    tokens = f_ref.shape[0]
    copies = halves(f_ref, own_f, other_f, sems, 0)
    small = [
        pltpu.make_async_copy(source, target, sems.at[6 + place])
        for place, (source, target) in enumerate(zip(sources, held))
    ]
    for copy in small:
        copy.start()
    copies += halves(x_ref, own_x, other_rest.at[0:tokens], sems, 2)
    copies += halves(dy_ref, own_dy, other_rest.at[tokens : 2 * tokens], sems, 4)
    packed[...] = jnp.zeros_like(packed)
    for copy in small:
        copy.wait()
    for start, ids, route in ((0, *held[:2]), (META // 2, *held[2:])):
        packed[start : start + 2, 0:tokens] = ids[...].astype(F32)
        rest = route[...]
        for piece in range(3):
            top = rest.astype(BF16).astype(F32)
            row = start + 2 + 2 * piece
            packed[row : row + 2, 0:tokens] = top
            rest = rest - top
    mine = packed[...]
    lanes = packed.shape[1]
    own_f[tokens : tokens + META, 0:lanes] = mine.astype(BF16)
    other_f[tokens : tokens + META, 0:lanes] = pltpu.roll(mine, tokens, 1).astype(BF16)
    for copy in copies:
        copy.wait()


def pack(f, x, dy, *small):
    tokens, width = f.shape[0], f.shape[1] // 2
    return call(
        pack_kernel,
        [array(tokens + META, width)] * 2 + [array(tokens, width)] * 2 + [array(2 * tokens, width)],
        [HBM] * 7,
        [VMEM] * 5,
        [pltpu.VMEM((META, 2 * tokens), F32), pltpu.SemaphoreType.DMA((10,))]
        + [pltpu.VMEM(value.shape, value.dtype) for value in small],
    )(f, x, dy, *small)


def load_kernel(*refs, count):
    sources, targets, sems = refs[:count], refs[-count - 1 : -1], refs[-1]
    copies = [
        pltpu.make_async_copy(source, target, sems.at[place])
        for place, (source, target) in enumerate(zip(sources, targets))
    ]
    for copy in copies:
        copy.start()
    for copy in copies:
        copy.wait()


def load(weights, after):
    return call(
        functools.partial(load_kernel, count=len(weights)),
        [array(*weight.shape) for weight in weights],
        [HBM] * len(weights) + [AFTER] * len(after),
        [VMEM] * len(weights),
        [pltpu.SemaphoreType.DMA((len(weights),))],
    )(*weights, *after)


class Plan:
    def __init__(self, blocks, part, group, tokens, relative):
        self.blocks, self.part, self.group = blocks, part, group
        self.tokens, self.relative = tokens, relative


def slot_rows(own_meta, other_meta, plan, first_row):
    lanes = 2 * plan.tokens
    padded = max(8, plan.blocks)
    me = lax.axis_index("expert") if plan.relative else 0
    meta = own_meta[plan.tokens : plan.tokens + META, 0:lanes].astype(F32)
    meta = meta + other_meta[plan.tokens : plan.tokens + META, 0:lanes].astype(F32)
    meta = meta[first_row : first_row + META // 2]
    first, second = meta[0:1], meta[1:2]
    route = meta[2:4] + meta[4:6] + meta[6:8]
    row = lax.broadcasted_iota(jnp.int32, (padded, lanes), 0)
    expert = ((row ^ me) // plan.group).astype(F32)
    is_first, is_second = expert == first, expert == second
    named = jnp.where(is_first | is_second, 1.0, 0.0)
    before = lax.broadcasted_iota(jnp.int32, (lanes, lanes), 0)
    after = lax.broadcasted_iota(jnp.int32, (lanes, lanes), 1)
    earlier = (before < after) & ((before < plan.tokens) == (after < plan.tokens))
    position = dot(named.astype(BF16), jnp.where(earlier, 1.0, 0.0).astype(BF16), 1, 0)
    lane = lax.broadcasted_iota(jnp.int32, (padded, lanes), 1)
    slot = position + jnp.where(lane < plan.tokens, 0, plan.part).astype(F32)
    slot = jnp.where(named > 0.5, slot, -1.0)
    return slot, jnp.where(is_first, route[0:1], route[1:2])


def slot_table(slot, block, first, rows):
    index = lax.broadcasted_iota(jnp.int32, (rows, slot.shape[1]), 0) + first
    index = index.astype(F32)
    return jnp.where(index == slot[block : block + 1, :], 1.0, 0.0)


def dispatch_kernel(
    own_meta, other_meta, own_ref, other_ref, *refs, plan, first_row, other_row, weighted, passed
):
    outs = refs[len(refs) - plan.blocks - passed : len(refs) - passed]
    width, tokens = outs[0].shape[1], plan.tokens
    slot, route = slot_rows(own_meta, other_meta, plan, first_row)
    values = jnp.concatenate([own_ref[0:tokens, :], other_ref[other_row : other_row + tokens, :]], axis=0)
    for block in range(plan.blocks):
        table = slot_table(slot, block, 0, 2 * plan.part)
        if weighted:
            scale = jnp.sum(table * route[block : block + 1, :], axis=1, keepdims=True)
        table = table.astype(BF16)
        for start in range(0, width, TILE):
            picked = dot(table, values[:, start : start + TILE], 1, 0)
            if weighted:
                picked = picked * scale
            outs[block][:, start : start + TILE] = picked.astype(BF16)


def dispatch(metas, own, other, plan, first_row, other_row, weighted, after=(), passing=()):
    width = own.shape[1]
    return call(
        functools.partial(
            dispatch_kernel,
            plan=plan,
            first_row=first_row,
            other_row=other_row,
            weighted=weighted,
            passed=len(passing),
        ),
        [array(2 * plan.part, width)] * plan.blocks + [array(*value.shape) for value in passing],
        [VMEM] * (4 + len(passing)) + [AFTER] * len(after),
        [VMEM] * (plan.blocks + len(passing)),
        [],
        aliases={4 + place: plan.blocks + place for place in range(len(passing))},
    )(*metas, own, other, *passing, *after)


def combine_kernel(own_meta, other_meta, *refs, plan, first_row, weighted, other):
    returned, out = refs[: plan.blocks], refs[-1]
    width, tokens = out.shape[1], plan.tokens
    slot, route = slot_rows(own_meta, other_meta, plan, first_row)
    table = []
    for block in range(plan.blocks):
        table.append(slot_table(slot, block, plan.part if other else 0, plan.part))
        if weighted:
            table[block] = table[block] * route[block : block + 1, :]
    table = jnp.concatenate(table, axis=0)
    high = table.astype(BF16)
    low = (table - high.astype(F32)).astype(BF16)
    for start in range(0, width, TILE):
        part = slice(start, start + TILE)
        values = jnp.concatenate([ref[:, part].astype(F32) for ref in returned], axis=0)
        values = values.astype(BF16)
        total = dot(high, values, 0, 0)
        if weighted:
            total += dot(low, values, 0, 0)
        out[:, part] = total[tokens if other else 0 :][:tokens].astype(BF16)


def combine(metas, returned, plan, first_row, weighted, other, after=(), weight=1):
    return call(
        functools.partial(
            combine_kernel, plan=plan, first_row=first_row, weighted=weighted, other=other
        ),
        array(plan.tokens, returned[0].shape[1]),
        [VMEM] * (2 + plan.blocks) + [AFTER] * len(after),
        VMEM,
        [],
        weight=weight,
    )(*metas, *returned, *after)


def joined(refs):
    return jnp.concatenate([ref[...] for ref in refs], axis=0)


def gate_up_kernel(*refs, blocks):
    gate_w, up_w = refs[blocks : blocks + 2]
    out, rows = refs[-2:]
    rows[...] = joined(refs[:blocks])
    for start in range(0, out.shape[2], TILE):
        part = slice(start, start + TILE)
        out[0, :, part] = dot(rows[...], gate_w[:, part], 1, 0).astype(BF16)
        out[1, :, part] = dot(rows[...], up_w[:, part], 1, 0).astype(BF16)


def gate_up(inputs, gate_w, up_w, after=(), weight=1):
    blocks, (rows, width) = len(inputs), inputs[0].shape
    units, total = gate_w.shape[1], blocks * rows
    return call(
        functools.partial(gate_up_kernel, blocks=blocks),
        array(2, total, units),
        [VMEM] * (blocks + 2) + [AFTER] * len(after),
        VMEM,
        [pltpu.VMEM((total, width), BF16)],
        weight=weight,
    )(*inputs, gate_w, up_w, *after)


def d_hidden_kernel(*refs, blocks):
    down_w = refs[blocks]
    out, rows = refs[-2:]
    rows[...] = joined(refs[:blocks])
    for start in range(0, out.shape[1], TILE):
        part = slice(start, start + TILE)
        out[:, part] = dot(rows[...], down_w[part, :], 1, 1).astype(BF16)


def d_hidden(inputs, down_w, after=(), weight=1):
    blocks, (rows, width) = len(inputs), inputs[0].shape
    units, total = down_w.shape[0], blocks * rows
    return call(
        functools.partial(d_hidden_kernel, blocks=blocks),
        array(total, units),
        [VMEM] * (blocks + 1) + [AFTER] * len(after),
        VMEM,
        [pltpu.VMEM((total, width), BF16)],
        weight=weight,
    )(*inputs, down_w, *after)


def scatter_tile(value, outs, columns):
    blocks, part = len(outs) // 2, outs[0].shape[0]
    for place, out in enumerate(outs):
        first = (2 * (place % blocks) + place // blocks) * part
        out[:, columns] = value[first : first + part].astype(BF16)


def total_of(own, other, part):
    own, other = own.astype(F32), other.astype(F32)
    rows = own.shape[0]
    turned = []
    for first in range(0, rows, 2 * part):
        turned += [other[first + part : first + 2 * part], other[first : first + part]]
    return own + jnp.concatenate(turned, axis=0)


def down_kernel(own_ref, other_ref, down_w, *refs, blocks):
    outs, hidden = refs[-1 - 2 * blocks : -1], refs[-1]
    part = outs[0].shape[0]
    for start in range(0, hidden.shape[1], TILE):
        columns = slice(start, start + TILE)
        gate = total_of(own_ref[0, :, columns], other_ref[0, :, columns], part)
        up = total_of(own_ref[1, :, columns], other_ref[1, :, columns], part)
        hidden[:, columns] = (gate * jax.nn.sigmoid(gate) * up).astype(BF16)
    for start in range(0, outs[0].shape[1], TILE):
        columns = slice(start, start + TILE)
        scatter_tile(dot(hidden[...], down_w[:, columns], 1, 0), outs, columns)


def down(own, other, down_w, plan, after=()):
    _, total, units = own.shape
    return call(
        functools.partial(down_kernel, blocks=plan.blocks),
        [array(plan.part, down_w.shape[1])] * (2 * plan.blocks),
        [VMEM] * 3 + [AFTER] * len(after),
        [VMEM] * (2 * plan.blocks),
        [pltpu.VMEM((total, units), BF16)],
    )(own, other, down_w, *after)


def back_kernel(own_ref, other_ref, own_d, other_d, gate_w, up_w, *refs, blocks):
    hidden, d_gate, d_up, *outs = refs[-3 - 2 * blocks :]
    part = outs[0].shape[0]
    for start in range(0, hidden.shape[1], TILE):
        columns = slice(start, start + TILE)
        gate = total_of(own_ref[0, :, columns], other_ref[0, :, columns], part)
        up = total_of(own_ref[1, :, columns], other_ref[1, :, columns], part)
        d_hid = total_of(own_d[:, columns], other_d[:, columns], part)
        sigmoid = jax.nn.sigmoid(gate)
        activated = gate * sigmoid
        hidden[:, columns] = (activated * up).astype(BF16)
        d_up[:, columns] = (d_hid * activated).astype(BF16)
        d_gate[:, columns] = (
            d_hid * up * sigmoid * (1.0 + gate * (1.0 - sigmoid))
        ).astype(BF16)
    for start in range(0, outs[0].shape[1], TILE):
        columns = slice(start, start + TILE)
        total = dot(d_gate[...], gate_w[columns, :], 1, 1)
        total += dot(d_up[...], up_w[columns, :], 1, 1)
        scatter_tile(total, outs, columns)


def back(own, other, own_d, other_d, gate_w, up_w, plan, after=()):
    _, total, units = own.shape
    return call(
        functools.partial(back_kernel, blocks=plan.blocks),
        [array(total, units)] * 3 + [array(plan.part, gate_w.shape[0])] * (2 * plan.blocks),
        [VMEM] * 6 + [AFTER] * len(after),
        [VMEM] * (3 + 2 * plan.blocks),
        [],
    )(own, other, own_d, other_d, gate_w, up_w, *after)


def grad_in_kernel(d_gate, d_up, *refs, blocks):
    inputs, (grad_gate, grad_up, turned) = refs[:blocks], refs[-3:]

    @pl.when(pl.program_id(0) == 0)
    def _():
        for start in range(0, turned.shape[0], TILE):
            part = slice(start, start + TILE)
            piece = jnp.concatenate([ref[:, part] for ref in inputs], axis=0)
            turned[part, :] = piece.T

    part = pl.ds(pl.multiple_of(pl.program_id(0) * TILE, TILE), TILE)
    grad_gate[...] = dot(turned[...], d_gate[:, part], 1, 0).astype(BF16)
    grad_up[...] = dot(turned[...], d_up[:, part], 1, 0).astype(BF16)


def grad_in(d_gate, d_up, inputs, after=(), weight=1):
    blocks, (rows, width) = len(inputs), inputs[0].shape
    total, units = d_gate.shape
    return call(
        functools.partial(grad_in_kernel, blocks=blocks),
        [pltpu.HBM((width, units), BF16)] * 2,
        [VMEM] * (2 + blocks) + [AFTER] * len(after),
        [pl.BlockSpec((width, TILE), lambda i: (0, i))] * 2,
        [pltpu.VMEM((width, total), BF16)],
        grid=(units // TILE,),
        weight=weight,
    )(d_gate, d_up, *inputs, *after)


def grad_down_kernel(hidden, *refs, blocks):
    cots, (grad, cot_all) = refs[:blocks], refs[-2:]

    @pl.when(pl.program_id(0) == 0)
    def _():
        cot_all[...] = joined(cots)

    part = pl.ds(pl.multiple_of(pl.program_id(0) * TILE, TILE), TILE)
    grad[...] = dot(hidden[:, part], cot_all[...], 0, 0).astype(BF16)


def grad_down(hidden, cots, after=(), weight=1):
    blocks, (rows, width) = len(cots), cots[0].shape
    total, units = hidden.shape
    return call(
        functools.partial(grad_down_kernel, blocks=blocks),
        pltpu.HBM((units, width), BF16),
        [VMEM] * (1 + blocks) + [AFTER] * len(after),
        pl.BlockSpec((TILE, width), lambda i: (i, 0)),
        [pltpu.VMEM((total, width), BF16)],
        grid=(units // TILE,),
        weight=weight,
    )(hidden, *cots, *after)


def to_experts(blocks, relative):
    if not relative:
        stacked = lax.all_to_all(jnp.stack(blocks), "expert", split_axis=0, concat_axis=0)
        return [stacked[block] for block in range(len(blocks))]
    return [blocks[0]] + [
        exchange(block, "expert", mask) for mask, block in enumerate(blocks) if mask > 0
    ]


def finish_kernel(mine_ref, rest_ref, *refs):
    out_ref, sems = refs[-2:]
    width = mine_ref.shape[1]
    core = lax.axis_index("dp")
    copies = []
    for place, (half, source) in enumerate(((core, mine_ref), (1 - core, rest_ref))):
        columns = pl.ds(pl.multiple_of(half * width, 128), width)
        copies.append(
            pltpu.make_async_copy(source, out_ref.at[:, columns], sems.at[place])
        )
    for copy in copies:
        copy.start()
    for copy in copies:
        copy.wait()


def finish(mine, rest, after=()):
    tokens, width = mine.shape
    return call(
        finish_kernel,
        pltpu.HBM((tokens, 2 * width), BF16),
        [VMEM, VMEM] + [AFTER] * len(after),
        HBM,
        [pltpu.SemaphoreType.DMA((2,))],
    )(mine, rest, *after)


def local(x_fwd, ids_fwd, route_fwd, x_bwd, ids_bwd, route_bwd, dy_bwd, w_gate, w_up, w_down):
    n_expert = lax.axis_size("expert")
    slab_width = w_gate.shape[-1]
    group = FF // slab_width
    experts = n_expert // group
    tokens = x_fwd.shape[1]
    spread = 4 * experts * group
    capacity = group * ((5 * tokens * TOP + spread - 1) // spread)
    relative = n_expert <= 8
    plan = Plan(n_expert, (capacity + 7) // 8 * 8, group, tokens, relative)
    row_b, row_f = 0, META // 2

    own_f, send_f, own_x, own_dy, send_rest = pack(
        *[in_hbm(value[0]) for value in (x_fwd, x_bwd, dy_bwd)],
        *[in_hbm(value[0].T) for value in (ids_bwd, route_bwd, ids_fwd, route_fwd)],
    )
    other_f = exchange(send_f, "dp", 1)
    metas = (own_f, other_f)
    *sent_f, send_rest = dispatch(
        metas, own_f, other_f, plan, row_f, 0, False, passing=(send_rest,)
    )
    rows_f = to_experts(sent_f, relative)
    other_rest = exchange(send_rest, "dp", 1)
    sent_x = dispatch(metas, own_x, other_rest, plan, row_b, 0, False)
    rows_b = to_experts(sent_x, relative)
    gate_w, up_w, down_w = load(
        [in_hbm(weight[0, 0]) for weight in (w_gate, w_up, w_down)], after=sent_x[:1]
    )
    sent_dy = dispatch(
        metas, own_dy, other_rest, plan, row_b, tokens, True, after=(in_vmem(down_w),)
    )
    cots_b = to_experts(sent_dy, relative)

    part_f = gate_up(rows_f, gate_w, up_w, after=sent_dy[:1])
    part_f_other = exchange(part_f, "dp", 1)
    part_b = gate_up(rows_b, gate_w, up_w, after=(part_f,), weight=3000)
    part_b_other = exchange(part_b, "dp", 1)
    down_blocks = down(part_f, part_f_other, down_w, plan, after=(part_b,))
    part_d = d_hidden(cots_b, down_w, after=down_blocks[:1], weight=1000)
    part_d_other = exchange(part_d, "dp", 1)
    own_back_f = to_experts(down_blocks[:n_expert], relative)
    other_back_f = to_experts(down_blocks[n_expert:], relative)
    own_sum = combine(
        metas, own_back_f, plan, row_f, True, False, after=(part_d,), weight=1000
    )
    y_mine = section_shift(own_sum, 0)
    hidden, d_gate, d_up, *back_blocks = back(
        part_b, part_b_other, part_d, part_d_other, gate_w, up_w, plan, after=(own_sum,)
    )
    own_back_b = to_experts(back_blocks[:n_expert], relative)
    other_back_b = to_experts(back_blocks[n_expert:], relative)
    other_sum = combine(
        metas, other_back_f, plan, row_f, True, True, after=back_blocks[:1], weight=150
    )
    y_rest = section_shift(other_sum, 1)
    own_sum = combine(
        metas,
        own_back_b,
        plan,
        row_b,
        False,
        False,
        after=(other_sum, in_vmem(y_mine)),
        weight=150,
    )
    dx_mine = section_shift(own_sum, 0)
    grad_g, grad_u = grad_in(d_gate, d_up, rows_b, after=(own_sum,))
    y_next = finish(y_mine, y_rest)
    other_sum = combine(
        metas,
        other_back_b,
        plan,
        row_b,
        False,
        True,
        after=(in_hbm(grad_g), in_hbm(y_next)),
    )
    dx_rest = section_shift(other_sum, 1)
    grad_d = grad_down(hidden, cots_b, after=(other_sum, in_vmem(dx_mine)), weight=100)
    dx_next = finish(dx_mine, dx_rest, after=(in_hbm(grad_d),))
    return (
        y_next[None],
        dx_next[None],
        grad_g[None, None],
        grad_u[None, None],
        grad_d[None, None],
    )


def solution(mesh):
    rows = P("section", ("expert", "dp"), None)
    by_feature = P("section", "expert", "dp", None)
    down_spec = P("section", "expert", None, "dp")
    return jax.shard_map(
        local,
        mesh=mesh,
        in_specs=(rows,) * 7 + (by_feature, by_feature, down_spec),
        out_specs=(rows, rows, by_feature, by_feature, down_spec),
        check_vma=False,
    )
```

```python
import functools

import jax
import jax.numpy as jnp
from jax import lax
from jax.experimental import pallas as pl
from jax.experimental.pallas import tpu as pltpu
from jax.sharding import PartitionSpec as P

FF = 1024
TOP = 2
TILE = 256
VMEM_LIMIT = 20 * 1024 * 1024
META = 16
COST = 10**7
F32 = jnp.float32
BF16 = jnp.bfloat16


def exchange(value, axis, mask):
    count = lax.axis_size(axis)
    return lax.ppermute(value, axis, [(source, source ^ mask) for source in range(count)])


def section_shift(value, flip):
    sections, cores = lax.axis_size("section"), lax.axis_size("dp")
    pairs = []
    for section in range(sections):
        for core in range(cores):
            target = ((section + 1) % sections) * cores + (core ^ flip)
            pairs.append((section * cores + core, target))
    return lax.ppermute(value, ("section", "dp"), pairs)


def dot(left, right, left_dim, right_dim):
    return lax.dot_general(
        left, right, (((left_dim,), (right_dim,)), ((), ())), preferred_element_type=F32
    )


VMEM = pl.BlockSpec(memory_space=pltpu.VMEM)
HBM = pl.BlockSpec(memory_space=pltpu.HBM)
AFTER = pl.BlockSpec(memory_space=pl.ANY)


def call(kernel, out_shape, in_specs, out_specs, scratch, grid=(), weight=1, aliases={}):
    return pl.pallas_call(
        kernel,
        out_shape=out_shape,
        grid=grid,
        in_specs=in_specs,
        out_specs=out_specs,
        scratch_shapes=scratch,
        input_output_aliases=aliases,
        compiler_params=pltpu.CompilerParams(vmem_limit_bytes=VMEM_LIMIT),
        cost_estimate=pl.CostEstimate(
            flops=weight * COST, bytes_accessed=1, transcendentals=0
        ),
    )


def array(*shape):
    return jax.ShapeDtypeStruct(shape, BF16)


def in_vmem(value):
    return pltpu.with_memory_space_constraint(value, pltpu.VMEM)


def in_hbm(value):
    return pltpu.with_memory_space_constraint(value, pltpu.HBM)


def halves(value_ref, own_ref, other_ref, sems, first):
    tokens, width = value_ref.shape[0], value_ref.shape[1] // 2
    core = lax.axis_index("dp")
    copies = []
    for place, (half, target) in enumerate(((core, own_ref), (1 - core, other_ref))):
        columns = pl.ds(pl.multiple_of(half * width, 128), width)
        copies.append(
            pltpu.make_async_copy(
                value_ref.at[:, columns], target.at[0:tokens], sems.at[first + place]
            )
        )
    for copy in copies:
        copy.start()
    return copies


def pack_kernel(f_ref, x_ref, dy_ref, *refs):
    sources, outs, (packed, sems), held = refs[:4], refs[4:9], refs[9:11], refs[11:]
    own_f, other_f, own_x, own_dy, other_rest = outs
    tokens = f_ref.shape[0]
    copies = halves(f_ref, own_f, other_f, sems, 0)
    small = [
        pltpu.make_async_copy(source, target, sems.at[6 + place])
        for place, (source, target) in enumerate(zip(sources, held))
    ]
    for copy in small:
        copy.start()
    copies += halves(x_ref, own_x, other_rest.at[0:tokens], sems, 2)
    copies += halves(dy_ref, own_dy, other_rest.at[tokens : 2 * tokens], sems, 4)
    packed[...] = jnp.zeros_like(packed)
    for copy in small:
        copy.wait()
    for start, ids, route in ((0, *held[:2]), (META // 2, *held[2:])):
        packed[start : start + 2, 0:tokens] = ids[...].astype(F32)
        rest = route[...]
        for piece in range(3):
            top = rest.astype(BF16).astype(F32)
            row = start + 2 + 2 * piece
            packed[row : row + 2, 0:tokens] = top
            rest = rest - top
    mine = packed[...]
    lanes = packed.shape[1]
    own_f[tokens : tokens + META, 0:lanes] = mine.astype(BF16)
    other_f[tokens : tokens + META, 0:lanes] = pltpu.roll(mine, tokens, 1).astype(BF16)
    for copy in copies:
        copy.wait()


def pack(f, x, dy, *small):
    tokens, width = f.shape[0], f.shape[1] // 2
    return call(
        pack_kernel,
        [array(tokens + META, width)] * 2 + [array(tokens, width)] * 2 + [array(2 * tokens, width)],
        [HBM] * 7,
        [VMEM] * 5,
        [pltpu.VMEM((META, 2 * tokens), F32), pltpu.SemaphoreType.DMA((10,))]
        + [pltpu.VMEM(value.shape, value.dtype) for value in small],
    )(f, x, dy, *small)


def load_kernel(*refs, count):
    sources, targets, sems = refs[:count], refs[-count - 1 : -1], refs[-1]
    copies = [
        pltpu.make_async_copy(source, target, sems.at[place])
        for place, (source, target) in enumerate(zip(sources, targets))
    ]
    for copy in copies:
        copy.start()
    for copy in copies:
        copy.wait()


def load(weights, after):
    return call(
        functools.partial(load_kernel, count=len(weights)),
        [array(*weight.shape) for weight in weights],
        [HBM] * len(weights) + [AFTER] * len(after),
        [VMEM] * len(weights),
        [pltpu.SemaphoreType.DMA((len(weights),))],
    )(*weights, *after)


class Plan:
    def __init__(self, blocks, part, group, tokens, relative):
        self.blocks, self.part, self.group = blocks, part, group
        self.tokens, self.relative = tokens, relative


def slot_rows(own_meta, other_meta, plan, first_row):
    lanes = 2 * plan.tokens
    padded = max(8, plan.blocks)
    me = lax.axis_index("expert") if plan.relative else 0
    meta = own_meta[plan.tokens : plan.tokens + META, 0:lanes].astype(F32)
    meta = meta + other_meta[plan.tokens : plan.tokens + META, 0:lanes].astype(F32)
    meta = meta[first_row : first_row + META // 2]
    first, second = meta[0:1], meta[1:2]
    route = meta[2:4] + meta[4:6] + meta[6:8]
    row = lax.broadcasted_iota(jnp.int32, (padded, lanes), 0)
    expert = ((row ^ me) // plan.group).astype(F32)
    is_first, is_second = expert == first, expert == second
    named = jnp.where(is_first | is_second, 1.0, 0.0)
    before = lax.broadcasted_iota(jnp.int32, (lanes, lanes), 0)
    after = lax.broadcasted_iota(jnp.int32, (lanes, lanes), 1)
    earlier = (before < after) & ((before < plan.tokens) == (after < plan.tokens))
    position = dot(named.astype(BF16), jnp.where(earlier, 1.0, 0.0).astype(BF16), 1, 0)
    lane = lax.broadcasted_iota(jnp.int32, (padded, lanes), 1)
    slot = position + jnp.where(lane < plan.tokens, 0, plan.part).astype(F32)
    slot = jnp.where(named > 0.5, slot, -1.0)
    return slot, jnp.where(is_first, route[0:1], route[1:2])


def slot_table(slot, block, first, rows):
    index = lax.broadcasted_iota(jnp.int32, (rows, slot.shape[1]), 0) + first
    index = index.astype(F32)
    return jnp.where(index == slot[block : block + 1, :], 1.0, 0.0)


def dispatch_kernel(
    own_meta, other_meta, own_ref, other_ref, *refs, plan, first_row, other_row, weighted, passed
):
    outs = refs[len(refs) - plan.blocks - passed : len(refs) - passed]
    width, tokens = outs[0].shape[1], plan.tokens
    slot, route = slot_rows(own_meta, other_meta, plan, first_row)
    values = jnp.concatenate([own_ref[0:tokens, :], other_ref[other_row : other_row + tokens, :]], axis=0)
    for block in range(plan.blocks):
        table = slot_table(slot, block, 0, 2 * plan.part)
        if weighted:
            scale = jnp.sum(table * route[block : block + 1, :], axis=1, keepdims=True)
        table = table.astype(BF16)
        for start in range(0, width, TILE):
            picked = dot(table, values[:, start : start + TILE], 1, 0)
            if weighted:
                picked = picked * scale
            outs[block][:, start : start + TILE] = picked.astype(BF16)


def dispatch(metas, own, other, plan, first_row, other_row, weighted, after=(), passing=()):
    width = own.shape[1]
    return call(
        functools.partial(
            dispatch_kernel,
            plan=plan,
            first_row=first_row,
            other_row=other_row,
            weighted=weighted,
            passed=len(passing),
        ),
        [array(2 * plan.part, width)] * plan.blocks + [array(*value.shape) for value in passing],
        [VMEM] * (4 + len(passing)) + [AFTER] * len(after),
        [VMEM] * (plan.blocks + len(passing)),
        [],
        aliases={4 + place: plan.blocks + place for place in range(len(passing))},
    )(*metas, own, other, *passing, *after)


def combine_kernel(own_meta, other_meta, *refs, plan, first_row, weighted, other):
    returned, out = refs[: plan.blocks], refs[-1]
    width, tokens = out.shape[1], plan.tokens
    slot, route = slot_rows(own_meta, other_meta, plan, first_row)
    table = []
    for block in range(plan.blocks):
        table.append(slot_table(slot, block, plan.part if other else 0, plan.part))
        if weighted:
            table[block] = table[block] * route[block : block + 1, :]
    table = jnp.concatenate(table, axis=0)
    high = table.astype(BF16)
    low = (table - high.astype(F32)).astype(BF16)
    for start in range(0, width, TILE):
        part = slice(start, start + TILE)
        values = jnp.concatenate([ref[:, part].astype(F32) for ref in returned], axis=0)
        values = values.astype(BF16)
        total = dot(high, values, 0, 0)
        if weighted:
            total += dot(low, values, 0, 0)
        out[:, part] = total[tokens if other else 0 :][:tokens].astype(BF16)


def combine(metas, returned, plan, first_row, weighted, other, after=(), weight=1):
    return call(
        functools.partial(
            combine_kernel, plan=plan, first_row=first_row, weighted=weighted, other=other
        ),
        array(plan.tokens, returned[0].shape[1]),
        [VMEM] * (2 + plan.blocks) + [AFTER] * len(after),
        VMEM,
        [],
        weight=weight,
    )(*metas, *returned, *after)


def joined(refs):
    return jnp.concatenate([ref[...] for ref in refs], axis=0)


def gate_up_kernel(*refs, blocks):
    gate_w, up_w = refs[blocks : blocks + 2]
    out, rows = refs[-2:]
    rows[...] = joined(refs[:blocks])
    for start in range(0, out.shape[2], TILE):
        part = slice(start, start + TILE)
        out[0, :, part] = dot(rows[...], gate_w[:, part], 1, 0).astype(BF16)
        out[1, :, part] = dot(rows[...], up_w[:, part], 1, 0).astype(BF16)


def gate_up(inputs, gate_w, up_w, planes=2, after=(), weight=1):
    blocks, (rows, width) = len(inputs), inputs[0].shape
    units, total = gate_w.shape[1], blocks * rows
    return call(
        functools.partial(gate_up_kernel, blocks=blocks),
        array(planes, total, units),
        [VMEM] * (blocks + 2) + [AFTER] * len(after),
        VMEM,
        [pltpu.VMEM((total, width), BF16)],
        weight=weight,
    )(*inputs, gate_w, up_w, *after)


def d_hidden_kernel(*refs, blocks):
    down_w = refs[blocks]
    out, rows = refs[-2:]
    rows[...] = joined(refs[:blocks])
    for start in range(0, out.shape[2], TILE):
        part = slice(start, start + TILE)
        out[2, :, part] = dot(rows[...], down_w[part, :], 1, 1).astype(BF16)


def d_hidden(inputs, down_w, partial, after=(), weight=1):
    blocks, (rows, width) = len(inputs), inputs[0].shape
    return call(
        functools.partial(d_hidden_kernel, blocks=blocks),
        array(*partial.shape),
        [VMEM] * (blocks + 2) + [AFTER] * len(after),
        VMEM,
        [pltpu.VMEM((blocks * rows, width), BF16)],
        weight=weight,
        aliases={blocks + 1: 0},
    )(*inputs, down_w, partial, *after)


def scatter_tile(value, outs, columns):
    blocks, part = len(outs) // 2, outs[0].shape[0]
    for place, out in enumerate(outs):
        first = (2 * (place % blocks) + place // blocks) * part
        out[:, columns] = value[first : first + part].astype(BF16)


def total_of(own, other, part):
    own, other = own.astype(F32), other.astype(F32)
    rows = own.shape[0]
    turned = []
    for first in range(0, rows, 2 * part):
        turned += [other[first + part : first + 2 * part], other[first : first + part]]
    return own + jnp.concatenate(turned, axis=0)


def down_kernel(own_ref, other_ref, down_w, *refs, blocks):
    outs, hidden = refs[-1 - 2 * blocks : -1], refs[-1]
    part = outs[0].shape[0]
    for start in range(0, hidden.shape[1], TILE):
        columns = slice(start, start + TILE)
        gate = total_of(own_ref[0, :, columns], other_ref[0, :, columns], part)
        up = total_of(own_ref[1, :, columns], other_ref[1, :, columns], part)
        hidden[:, columns] = (gate * jax.nn.sigmoid(gate) * up).astype(BF16)
    for start in range(0, outs[0].shape[1], TILE):
        columns = slice(start, start + TILE)
        scatter_tile(dot(hidden[...], down_w[:, columns], 1, 0), outs, columns)


def down(own, other, down_w, plan, after=()):
    _, total, units = own.shape
    return call(
        functools.partial(down_kernel, blocks=plan.blocks),
        [array(plan.part, down_w.shape[1])] * (2 * plan.blocks),
        [VMEM] * 3 + [AFTER] * len(after),
        [VMEM] * (2 * plan.blocks),
        [pltpu.VMEM((total, units), BF16)],
    )(own, other, down_w, *after)


def back_kernel(own_ref, other_ref, gate_w, up_w, *refs, blocks):
    hidden, d_gate, d_up, *outs = refs[-3 - 2 * blocks :]
    part = outs[0].shape[0]
    for start in range(0, hidden.shape[1], TILE):
        columns = slice(start, start + TILE)
        gate = total_of(own_ref[0, :, columns], other_ref[0, :, columns], part)
        up = total_of(own_ref[1, :, columns], other_ref[1, :, columns], part)
        d_hid = total_of(own_ref[2, :, columns], other_ref[2, :, columns], part)
        sigmoid = jax.nn.sigmoid(gate)
        activated = gate * sigmoid
        hidden[:, columns] = (activated * up).astype(BF16)
        d_up[:, columns] = (d_hid * activated).astype(BF16)
        d_gate[:, columns] = (
            d_hid * up * sigmoid * (1.0 + gate * (1.0 - sigmoid))
        ).astype(BF16)
    for start in range(0, outs[0].shape[1], TILE):
        columns = slice(start, start + TILE)
        total = dot(d_gate[...], gate_w[columns, :], 1, 1)
        total += dot(d_up[...], up_w[columns, :], 1, 1)
        scatter_tile(total, outs, columns)


def back(own, other, gate_w, up_w, plan, after=()):
    _, total, units = own.shape
    return call(
        functools.partial(back_kernel, blocks=plan.blocks),
        [array(total, units)] * 3 + [array(plan.part, gate_w.shape[0])] * (2 * plan.blocks),
        [VMEM] * 4 + [AFTER] * len(after),
        [VMEM] * (3 + 2 * plan.blocks),
        [],
    )(own, other, gate_w, up_w, *after)


def turn_kernel(*refs, blocks):
    inputs, turned = refs[:blocks], refs[-1]
    for start in range(0, turned.shape[0], TILE):
        part = slice(start, start + TILE)
        turned[part, :] = jnp.concatenate([ref[:, part] for ref in inputs], axis=0).T


def turn(inputs, after=()):
    blocks, (rows, width) = len(inputs), inputs[0].shape
    return call(
        functools.partial(turn_kernel, blocks=blocks),
        array(width, blocks * rows),
        [VMEM] * blocks + [AFTER] * len(after),
        VMEM,
        [],
    )(*inputs, *after)


def grad_in_kernel(d_gate, d_up, turned, *refs):
    grad_gate, grad_up = refs[-2:]
    part = pl.ds(pl.multiple_of(pl.program_id(0) * TILE, TILE), TILE)
    grad_gate[...] = dot(turned[...], d_gate[:, part], 1, 0).astype(BF16)
    grad_up[...] = dot(turned[...], d_up[:, part], 1, 0).astype(BF16)


def grad_in(d_gate, d_up, turned, after=(), weight=1):
    width, units = turned.shape[0], d_gate.shape[1]
    return call(
        grad_in_kernel,
        [pltpu.HBM((width, units), BF16)] * 2,
        [VMEM] * 3 + [AFTER] * len(after),
        [pl.BlockSpec((width, TILE), lambda i: (0, i))] * 2,
        [],
        grid=(units // TILE,),
        weight=weight,
    )(d_gate, d_up, turned, *after)


def grad_down_kernel(hidden, *refs, blocks):
    cots, (grad, cot_all) = refs[:blocks], refs[-2:]

    @pl.when(pl.program_id(0) == 0)
    def _():
        cot_all[...] = joined(cots)

    part = pl.ds(pl.multiple_of(pl.program_id(0) * TILE, TILE), TILE)
    grad[...] = dot(hidden[:, part], cot_all[...], 0, 0).astype(BF16)


def grad_down(hidden, cots, after=(), weight=1):
    blocks, (rows, width) = len(cots), cots[0].shape
    total, units = hidden.shape
    return call(
        functools.partial(grad_down_kernel, blocks=blocks),
        pltpu.HBM((units, width), BF16),
        [VMEM] * (1 + blocks) + [AFTER] * len(after),
        pl.BlockSpec((TILE, width), lambda i: (i, 0)),
        [pltpu.VMEM((total, width), BF16)],
        grid=(units // TILE,),
        weight=weight,
    )(hidden, *cots, *after)


def to_experts(blocks, relative):
    if not relative:
        stacked = lax.all_to_all(jnp.stack(blocks), "expert", split_axis=0, concat_axis=0)
        return [stacked[block] for block in range(len(blocks))]
    return [blocks[0]] + [
        exchange(block, "expert", mask) for mask, block in enumerate(blocks) if mask > 0
    ]


def finish_kernel(mine_ref, rest_ref, *refs):
    out_ref, sems = refs[-2:]
    width = mine_ref.shape[1]
    core = lax.axis_index("dp")
    copies = []
    for place, (half, source) in enumerate(((core, mine_ref), (1 - core, rest_ref))):
        columns = pl.ds(pl.multiple_of(half * width, 128), width)
        copies.append(
            pltpu.make_async_copy(source, out_ref.at[:, columns], sems.at[place])
        )
    for copy in copies:
        copy.start()
    for copy in copies:
        copy.wait()


def finish(mine, rest, after=()):
    tokens, width = mine.shape
    return call(
        finish_kernel,
        pltpu.HBM((tokens, 2 * width), BF16),
        [VMEM, VMEM] + [AFTER] * len(after),
        HBM,
        [pltpu.SemaphoreType.DMA((2,))],
    )(mine, rest, *after)


def local(x_fwd, ids_fwd, route_fwd, x_bwd, ids_bwd, route_bwd, dy_bwd, w_gate, w_up, w_down):
    n_expert = lax.axis_size("expert")
    slab_width = w_gate.shape[-1]
    group = FF // slab_width
    experts = n_expert // group
    tokens = x_fwd.shape[1]
    spread = 4 * experts * group
    capacity = group * ((5 * tokens * TOP + spread - 1) // spread)
    relative = n_expert <= 8
    plan = Plan(n_expert, (capacity + 7) // 8 * 8, group, tokens, relative)
    row_b, row_f = 0, META // 2

    own_f, send_f, own_x, own_dy, send_rest = pack(
        *[in_hbm(value[0]) for value in (x_fwd, x_bwd, dy_bwd)],
        *[in_hbm(value[0].T) for value in (ids_bwd, route_bwd, ids_fwd, route_fwd)],
    )
    other_f = exchange(send_f, "dp", 1)
    metas = (own_f, other_f)
    *sent_f, send_rest = dispatch(
        metas, own_f, other_f, plan, row_f, 0, False, passing=(send_rest,)
    )
    rows_f = to_experts(sent_f, relative)
    other_rest = exchange(send_rest, "dp", 1)
    sent_x = dispatch(metas, own_x, other_rest, plan, row_b, 0, False)
    rows_b = to_experts(sent_x, relative)
    gate_w, up_w, down_w = load(
        [in_hbm(weight[0, 0]) for weight in (w_gate, w_up, w_down)], after=sent_x[:1]
    )
    sent_dy = dispatch(
        metas, own_dy, other_rest, plan, row_b, tokens, True, after=(in_vmem(down_w),)
    )
    cots_b = to_experts(sent_dy, relative)

    part_f = gate_up(rows_f, gate_w, up_w, after=sent_dy[:1])
    part_f_other = exchange(part_f, "dp", 1)
    part_b = gate_up(rows_b, gate_w, up_w, planes=3, after=(part_f,), weight=3000)
    down_blocks = down(part_f, part_f_other, down_w, plan, after=(in_vmem(part_b),))
    own_back_f = to_experts(down_blocks[:n_expert], relative)
    other_back_f = to_experts(down_blocks[n_expert:], relative)
    turned = turn(rows_b, after=down_blocks[:1])
    part_b = d_hidden(cots_b, down_w, part_b, after=(in_vmem(turned),), weight=1000)
    part_b_other = exchange(part_b, "dp", 1)
    own_sum = combine(
        metas, own_back_f, plan, row_f, True, False, after=(in_vmem(part_b),), weight=2000
    )
    y_mine = section_shift(own_sum, 0)
    hidden, d_gate, d_up, *back_blocks = back(
        part_b, part_b_other, gate_w, up_w, plan, after=(own_sum,)
    )
    own_back_b = to_experts(back_blocks[:n_expert], relative)
    other_back_b = to_experts(back_blocks[n_expert:], relative)
    other_sum = combine(
        metas, other_back_f, plan, row_f, True, True, after=back_blocks[:1], weight=150
    )
    y_rest = section_shift(other_sum, 1)
    own_sum = combine(
        metas,
        own_back_b,
        plan,
        row_b,
        False,
        False,
        after=(other_sum, in_vmem(y_mine)),
        weight=150,
    )
    dx_mine = section_shift(own_sum, 0)
    grad_d = grad_down(hidden, cots_b, after=(own_sum, in_vmem(y_rest)), weight=100)
    other_sum = combine(
        metas,
        other_back_b,
        plan,
        row_b,
        False,
        True,
        after=(in_hbm(grad_d),),
    )
    dx_rest = section_shift(other_sum, 1)
    y_next = finish(y_mine, y_rest, after=(other_sum,))
    grad_g, grad_u = grad_in(
        d_gate, d_up, turned, after=(in_hbm(y_next), in_vmem(dx_mine)), weight=100
    )
    dx_next = finish(dx_mine, dx_rest, after=(in_hbm(grad_g),))
    return (
        y_next[None],
        dx_next[None],
        grad_g[None, None],
        grad_u[None, None],
        grad_d[None, None],
    )


def solution(mesh):
    rows = P("section", ("expert", "dp"), None)
    by_feature = P("section", "expert", "dp", None)
    down_spec = P("section", "expert", None, "dp")
    return jax.shard_map(
        local,
        mesh=mesh,
        in_specs=(rows,) * 7 + (by_feature, by_feature, down_spec),
        out_specs=(rows, rows, by_feature, by_feature, down_spec),
        check_vma=False,
    )
```

```python
import functools

import jax
import jax.numpy as jnp
from jax import lax
from jax.experimental import pallas as pl
from jax.experimental.pallas import tpu as pltpu
from jax.sharding import PartitionSpec as P

FF = 1024
TOP = 2
TILE = 256
VMEM_LIMIT = 20 * 1024 * 1024
META = 16
COST = 10**7
F32 = jnp.float32
BF16 = jnp.bfloat16


def exchange(value, axis, mask):
    count = lax.axis_size(axis)
    return lax.ppermute(value, axis, [(source, source ^ mask) for source in range(count)])


def section_shift(value, flip):
    sections, cores = lax.axis_size("section"), lax.axis_size("dp")
    pairs = []
    for section in range(sections):
        for core in range(cores):
            target = ((section + 1) % sections) * cores + (core ^ flip)
            pairs.append((section * cores + core, target))
    return lax.ppermute(value, ("section", "dp"), pairs)


def dot(left, right, left_dim, right_dim):
    return lax.dot_general(
        left, right, (((left_dim,), (right_dim,)), ((), ())), preferred_element_type=F32
    )


VMEM = pl.BlockSpec(memory_space=pltpu.VMEM)
HBM = pl.BlockSpec(memory_space=pltpu.HBM)
AFTER = pl.BlockSpec(memory_space=pl.ANY)


def call(kernel, out_shape, in_specs, out_specs, scratch, grid=(), weight=1, aliases={}):
    return pl.pallas_call(
        kernel,
        out_shape=out_shape,
        grid=grid,
        in_specs=in_specs,
        out_specs=out_specs,
        scratch_shapes=scratch,
        input_output_aliases=aliases,
        compiler_params=pltpu.CompilerParams(vmem_limit_bytes=VMEM_LIMIT),
        cost_estimate=pl.CostEstimate(
            flops=weight * COST, bytes_accessed=1, transcendentals=0
        ),
    )


def array(*shape):
    return jax.ShapeDtypeStruct(shape, BF16)


def in_vmem(value):
    return pltpu.with_memory_space_constraint(value, pltpu.VMEM)


def in_hbm(value):
    return pltpu.with_memory_space_constraint(value, pltpu.HBM)


def halves(value_ref, own_ref, other_ref, sems, first):
    tokens, width = value_ref.shape[0], value_ref.shape[1] // 2
    core = lax.axis_index("dp")
    copies = []
    for place, (half, target) in enumerate(((core, own_ref), (1 - core, other_ref))):
        columns = pl.ds(pl.multiple_of(half * width, 128), width)
        copies.append(
            pltpu.make_async_copy(
                value_ref.at[:, columns], target.at[0:tokens], sems.at[first + place]
            )
        )
    for copy in copies:
        copy.start()
    return copies


def pack_kernel(f_ref, *refs):
    sources, (own, other, packed, sems), held = refs[:4], refs[4:8], refs[8:]
    tokens = f_ref.shape[0]
    small = [
        pltpu.make_async_copy(source, target, sems.at[2 + place])
        for place, (source, target) in enumerate(zip(sources, held))
    ]
    for copy in small:
        copy.start()
    copies = halves(f_ref, own, other, sems, 0)
    packed[...] = jnp.zeros_like(packed)
    for copy in small:
        copy.wait()
    for start, ids, route in ((0, *held[:2]), (META // 2, *held[2:])):
        packed[start : start + 2, 0:tokens] = ids[...].astype(F32)
        rest = route[...]
        for piece in range(3):
            top = rest.astype(BF16).astype(F32)
            row = start + 2 + 2 * piece
            packed[row : row + 2, 0:tokens] = top
            rest = rest - top
    mine = packed[...]
    lanes = packed.shape[1]
    own[tokens : tokens + META, 0:lanes] = mine.astype(BF16)
    other[tokens : tokens + META, 0:lanes] = pltpu.roll(mine, tokens, 1).astype(BF16)
    for copy in copies:
        copy.wait()


def pack(f, *small):
    tokens, width = f.shape[0], f.shape[1] // 2
    return call(
        pack_kernel,
        [array(tokens + META, width)] * 2,
        [HBM] * 5,
        [VMEM] * 2,
        [pltpu.VMEM((META, 2 * tokens), F32), pltpu.SemaphoreType.DMA((6,))]
        + [pltpu.VMEM(value.shape, value.dtype) for value in small],
    )(f, *small)


def cut_kernel(x_ref, dy_ref, *refs):
    own_x, own_dy, other, sems = refs[-4:]
    tokens = x_ref.shape[0]
    copies = halves(x_ref, own_x, other.at[0:tokens], sems, 0)
    copies += halves(dy_ref, own_dy, other.at[tokens : 2 * tokens], sems, 2)
    for copy in copies:
        copy.wait()


def cut(x, dy, after):
    tokens, width = x.shape[0], x.shape[1] // 2
    return call(
        cut_kernel,
        [array(tokens, width)] * 2 + [array(2 * tokens, width)],
        [HBM] * 2 + [AFTER] * len(after),
        [VMEM] * 3,
        [pltpu.SemaphoreType.DMA((4,))],
    )(x, dy, *after)


def load_kernel(*refs, count):
    sources, targets, sems = refs[:count], refs[-count - 1 : -1], refs[-1]
    copies = [
        pltpu.make_async_copy(source, target, sems.at[place])
        for place, (source, target) in enumerate(zip(sources, targets))
    ]
    for copy in copies:
        copy.start()
    for copy in copies:
        copy.wait()


def load(weights, after):
    return call(
        functools.partial(load_kernel, count=len(weights)),
        [array(*weight.shape) for weight in weights],
        [HBM] * len(weights) + [AFTER] * len(after),
        [VMEM] * len(weights),
        [pltpu.SemaphoreType.DMA((len(weights),))],
    )(*weights, *after)


class Plan:
    def __init__(self, blocks, part, group, tokens, relative):
        self.blocks, self.part, self.group = blocks, part, group
        self.tokens, self.relative = tokens, relative


def slot_rows(own_meta, other_meta, plan, first_row):
    lanes = 2 * plan.tokens
    padded = max(8, plan.blocks)
    me = lax.axis_index("expert") if plan.relative else 0
    meta = own_meta[plan.tokens : plan.tokens + META, 0:lanes].astype(F32)
    meta = meta + other_meta[plan.tokens : plan.tokens + META, 0:lanes].astype(F32)
    meta = meta[first_row : first_row + META // 2]
    first, second = meta[0:1], meta[1:2]
    route = meta[2:4] + meta[4:6] + meta[6:8]
    row = lax.broadcasted_iota(jnp.int32, (padded, lanes), 0)
    expert = ((row ^ me) // plan.group).astype(F32)
    is_first, is_second = expert == first, expert == second
    named = jnp.where(is_first | is_second, 1.0, 0.0)
    before = lax.broadcasted_iota(jnp.int32, (lanes, lanes), 0)
    after = lax.broadcasted_iota(jnp.int32, (lanes, lanes), 1)
    earlier = (before < after) & ((before < plan.tokens) == (after < plan.tokens))
    position = dot(named.astype(BF16), jnp.where(earlier, 1.0, 0.0).astype(BF16), 1, 0)
    lane = lax.broadcasted_iota(jnp.int32, (padded, lanes), 1)
    slot = position + jnp.where(lane < plan.tokens, 0, plan.part).astype(F32)
    slot = jnp.where(named > 0.5, slot, -1.0)
    return slot, jnp.where(is_first, route[0:1], route[1:2])


def slot_table(slot, block, first, rows):
    index = lax.broadcasted_iota(jnp.int32, (rows, slot.shape[1]), 0) + first
    index = index.astype(F32)
    return jnp.where(index == slot[block : block + 1, :], 1.0, 0.0)


def dispatch_kernel(
    own_meta, other_meta, own_ref, other_ref, *refs, plan, first_row, other_row, weighted, passed
):
    outs = refs[len(refs) - plan.blocks - passed : len(refs) - passed]
    width, tokens = outs[0].shape[1], plan.tokens
    slot, route = slot_rows(own_meta, other_meta, plan, first_row)
    values = jnp.concatenate([own_ref[0:tokens, :], other_ref[other_row : other_row + tokens, :]], axis=0)
    for block in range(plan.blocks):
        table = slot_table(slot, block, 0, 2 * plan.part)
        if weighted:
            scale = jnp.sum(table * route[block : block + 1, :], axis=1, keepdims=True)
        table = table.astype(BF16)
        for start in range(0, width, TILE):
            picked = dot(table, values[:, start : start + TILE], 1, 0)
            if weighted:
                picked = picked * scale
            outs[block][:, start : start + TILE] = picked.astype(BF16)


def dispatch(metas, own, other, plan, first_row, other_row, weighted, after=(), passing=()):
    width = own.shape[1]
    return call(
        functools.partial(
            dispatch_kernel,
            plan=plan,
            first_row=first_row,
            other_row=other_row,
            weighted=weighted,
            passed=len(passing),
        ),
        [array(2 * plan.part, width)] * plan.blocks + [array(*value.shape) for value in passing],
        [VMEM] * (4 + len(passing)) + [AFTER] * len(after),
        [VMEM] * (plan.blocks + len(passing)),
        [],
        aliases={4 + place: plan.blocks + place for place in range(len(passing))},
    )(*metas, own, other, *passing, *after)


def combine_kernel(own_meta, other_meta, *refs, plan, first_row, weighted, other):
    returned, out = refs[: plan.blocks], refs[-1]
    width, tokens = out.shape[1], plan.tokens
    slot, route = slot_rows(own_meta, other_meta, plan, first_row)
    table = []
    for block in range(plan.blocks):
        table.append(slot_table(slot, block, plan.part if other else 0, plan.part))
        if weighted:
            table[block] = table[block] * route[block : block + 1, :]
    table = jnp.concatenate(table, axis=0)
    high = table.astype(BF16)
    low = (table - high.astype(F32)).astype(BF16)
    for start in range(0, width, TILE):
        part = slice(start, start + TILE)
        values = jnp.concatenate([ref[:, part].astype(F32) for ref in returned], axis=0)
        values = values.astype(BF16)
        total = dot(high, values, 0, 0)
        if weighted:
            total += dot(low, values, 0, 0)
        out[:, part] = total[tokens if other else 0 :][:tokens].astype(BF16)


def combine(metas, returned, plan, first_row, weighted, other, after=(), weight=1):
    return call(
        functools.partial(
            combine_kernel, plan=plan, first_row=first_row, weighted=weighted, other=other
        ),
        array(plan.tokens, returned[0].shape[1]),
        [VMEM] * (2 + plan.blocks) + [AFTER] * len(after),
        VMEM,
        [],
        weight=weight,
    )(*metas, *returned, *after)


def joined(refs):
    return jnp.concatenate([ref[...] for ref in refs], axis=0)


def gate_up_kernel(*refs, blocks):
    gate_w, up_w = refs[blocks : blocks + 2]
    out, rows = refs[-2:]
    rows[...] = joined(refs[:blocks])
    for start in range(0, out.shape[2], TILE):
        part = slice(start, start + TILE)
        out[0, :, part] = dot(rows[...], gate_w[:, part], 1, 0).astype(BF16)
        out[1, :, part] = dot(rows[...], up_w[:, part], 1, 0).astype(BF16)


def gate_up(inputs, gate_w, up_w, planes=2, after=(), weight=1):
    blocks, (rows, width) = len(inputs), inputs[0].shape
    units, total = gate_w.shape[1], blocks * rows
    return call(
        functools.partial(gate_up_kernel, blocks=blocks),
        array(planes, total, units),
        [VMEM] * (blocks + 2) + [AFTER] * len(after),
        VMEM,
        [pltpu.VMEM((total, width), BF16)],
        weight=weight,
    )(*inputs, gate_w, up_w, *after)


def d_hidden_kernel(*refs, blocks):
    down_w = refs[blocks]
    rows, out = refs[-2:]
    rows[...] = joined(refs[:blocks])
    for start in range(0, out.shape[2], TILE):
        part = slice(start, start + TILE)
        out[2, :, part] = dot(rows[...], down_w[part, :], 1, 1).astype(BF16)


def d_hidden(inputs, down_w, partial, after=(), weight=1):
    blocks, (rows, width) = len(inputs), inputs[0].shape
    return call(
        functools.partial(d_hidden_kernel, blocks=blocks),
        [array(blocks * rows, width), array(*partial.shape)],
        [VMEM] * (blocks + 2) + [AFTER] * len(after),
        [VMEM] * 2,
        [],
        weight=weight,
        aliases={blocks + 1: 1},
    )(*inputs, down_w, partial, *after)


def scatter_tile(value, outs, columns):
    blocks, part = len(outs) // 2, outs[0].shape[0]
    for place, out in enumerate(outs):
        first = (2 * (place % blocks) + place // blocks) * part
        out[:, columns] = value[first : first + part].astype(BF16)


def total_of(own, other, part):
    own, other = own.astype(F32), other.astype(F32)
    rows = own.shape[0]
    turned = []
    for first in range(0, rows, 2 * part):
        turned += [other[first + part : first + 2 * part], other[first : first + part]]
    return own + jnp.concatenate(turned, axis=0)


def down_kernel(own_ref, other_ref, down_w, *refs, blocks):
    outs, hidden = refs[-1 - 2 * blocks : -1], refs[-1]
    part = outs[0].shape[0]
    for start in range(0, hidden.shape[1], TILE):
        columns = slice(start, start + TILE)
        gate = total_of(own_ref[0, :, columns], other_ref[0, :, columns], part)
        up = total_of(own_ref[1, :, columns], other_ref[1, :, columns], part)
        hidden[:, columns] = (gate * jax.nn.sigmoid(gate) * up).astype(BF16)
    for start in range(0, outs[0].shape[1], TILE):
        columns = slice(start, start + TILE)
        scatter_tile(dot(hidden[...], down_w[:, columns], 1, 0), outs, columns)


def down(own, other, down_w, plan, after=()):
    _, total, units = own.shape
    return call(
        functools.partial(down_kernel, blocks=plan.blocks),
        [array(plan.part, down_w.shape[1])] * (2 * plan.blocks),
        [VMEM] * 3 + [AFTER] * len(after),
        [VMEM] * (2 * plan.blocks),
        [pltpu.VMEM((total, units), BF16)],
    )(own, other, down_w, *after)


def back_kernel(own_ref, other_ref, gate_w, up_w, *refs, blocks):
    hidden, d_gate, d_up, *outs = refs[-3 - 2 * blocks :]
    part = outs[0].shape[0]
    for start in range(0, hidden.shape[1], TILE):
        columns = slice(start, start + TILE)
        gate = total_of(own_ref[0, :, columns], other_ref[0, :, columns], part)
        up = total_of(own_ref[1, :, columns], other_ref[1, :, columns], part)
        d_hid = total_of(own_ref[2, :, columns], other_ref[2, :, columns], part)
        sigmoid = jax.nn.sigmoid(gate)
        activated = gate * sigmoid
        hidden[:, columns] = (activated * up).astype(BF16)
        d_up[:, columns] = (d_hid * activated).astype(BF16)
        d_gate[:, columns] = (
            d_hid * up * sigmoid * (1.0 + gate * (1.0 - sigmoid))
        ).astype(BF16)
    for start in range(0, outs[0].shape[1], TILE):
        columns = slice(start, start + TILE)
        total = dot(d_gate[...], gate_w[columns, :], 1, 1)
        total += dot(d_up[...], up_w[columns, :], 1, 1)
        scatter_tile(total, outs, columns)


def back(own, other, gate_w, up_w, plan, after=()):
    _, total, units = own.shape
    return call(
        functools.partial(back_kernel, blocks=plan.blocks),
        [array(total, units)] * 3 + [array(plan.part, gate_w.shape[0])] * (2 * plan.blocks),
        [VMEM] * 4 + [AFTER] * len(after),
        [VMEM] * (3 + 2 * plan.blocks),
        [],
    )(own, other, gate_w, up_w, *after)


def turn_kernel(*refs, blocks):
    inputs, turned = refs[:blocks], refs[-1]
    for start in range(0, turned.shape[0], TILE):
        part = slice(start, start + TILE)
        turned[part, :] = jnp.concatenate([ref[:, part] for ref in inputs], axis=0).T


def turn(inputs, after=()):
    blocks, (rows, width) = len(inputs), inputs[0].shape
    return call(
        functools.partial(turn_kernel, blocks=blocks),
        array(width, blocks * rows),
        [VMEM] * blocks + [AFTER] * len(after),
        VMEM,
        [],
    )(*inputs, *after)


def grad_kernel(hidden, d_gate, d_up, turned, cots, *refs):
    grad_gate, grad_up, grad_down = refs[-3:]
    part = pl.ds(pl.multiple_of(pl.program_id(0) * TILE, TILE), TILE)
    grad_gate[...] = dot(turned[...], d_gate[:, part], 1, 0).astype(BF16)
    grad_up[...] = dot(turned[...], d_up[:, part], 1, 0).astype(BF16)
    grad_down[...] = dot(hidden[:, part], cots[...], 0, 0).astype(BF16)


def grads(hidden, d_gate, d_up, turned, cots, after=(), weight=1):
    width, units = turned.shape[0], d_gate.shape[1]
    by_column = pl.BlockSpec((width, TILE), lambda i: (0, i))
    return call(
        grad_kernel,
        [pltpu.HBM((width, units), BF16)] * 2 + [pltpu.HBM((units, width), BF16)],
        [VMEM] * 5 + [AFTER] * len(after),
        [by_column, by_column, pl.BlockSpec((TILE, width), lambda i: (i, 0))],
        [],
        grid=(units // TILE,),
        weight=weight,
    )(hidden, d_gate, d_up, turned, cots, *after)


def to_experts(blocks, relative):
    if not relative:
        stacked = lax.all_to_all(jnp.stack(blocks), "expert", split_axis=0, concat_axis=0)
        return [stacked[block] for block in range(len(blocks))]
    return [blocks[0]] + [
        exchange(block, "expert", mask) for mask, block in enumerate(blocks) if mask > 0
    ]


def finish_kernel(*refs):
    sources, outs, sems = refs[:4], refs[-3:-1], refs[-1]
    width = sources[0].shape[1]
    core = lax.axis_index("dp")
    copies = []
    for place, source in enumerate(sources):
        half = core if place % 2 == 0 else 1 - core
        columns = pl.ds(pl.multiple_of(half * width, 128), width)
        copies.append(
            pltpu.make_async_copy(source, outs[place // 2].at[:, columns], sems.at[place])
        )
    for copy in copies:
        copy.start()
    for copy in copies:
        copy.wait()


def finish(y_mine, y_rest, dx_mine, dx_rest, after):
    tokens, width = y_mine.shape
    return call(
        finish_kernel,
        [pltpu.HBM((tokens, 2 * width), BF16)] * 2,
        [VMEM] * 4 + [AFTER] * len(after),
        [HBM] * 2,
        [pltpu.SemaphoreType.DMA((4,))],
    )(y_mine, y_rest, dx_mine, dx_rest, *after)


def local(x_fwd, ids_fwd, route_fwd, x_bwd, ids_bwd, route_bwd, dy_bwd, w_gate, w_up, w_down):
    n_expert = lax.axis_size("expert")
    slab_width = w_gate.shape[-1]
    group = FF // slab_width
    experts = n_expert // group
    tokens = x_fwd.shape[1]
    spread = 4 * experts * group
    capacity = group * ((5 * tokens * TOP + spread - 1) // spread)
    relative = n_expert <= 8
    plan = Plan(n_expert, (capacity + 7) // 8 * 8, group, tokens, relative)
    row_b, row_f = 0, META // 2

    own_f, send_f = pack(
        in_hbm(x_fwd[0]),
        *[in_hbm(value[0].T) for value in (ids_bwd, route_bwd, ids_fwd, route_fwd)],
    )
    other_f = exchange(send_f, "dp", 1)
    own_x, own_dy, send_rest = cut(in_hbm(x_bwd[0]), in_hbm(dy_bwd[0]), after=(own_f,))
    metas = (own_f, other_f)
    *sent_f, send_rest = dispatch(
        metas, own_f, other_f, plan, row_f, 0, False, passing=(send_rest,)
    )
    rows_f = to_experts(sent_f, relative)
    other_rest = exchange(send_rest, "dp", 1)
    sent_x = dispatch(metas, own_x, other_rest, plan, row_b, 0, False)
    rows_b = to_experts(sent_x, relative)
    gate_w, up_w, down_w = load(
        [in_hbm(weight[0, 0]) for weight in (w_gate, w_up, w_down)], after=sent_x[:1]
    )
    sent_dy = dispatch(
        metas, own_dy, other_rest, plan, row_b, tokens, True, after=(in_vmem(down_w),)
    )
    cots_b = to_experts(sent_dy, relative)

    part_f = gate_up(rows_f, gate_w, up_w, after=sent_dy[:1])
    part_f_other = exchange(part_f, "dp", 1)
    part_b = gate_up(rows_b, gate_w, up_w, planes=3, after=(part_f,), weight=3000)
    down_blocks = down(part_f, part_f_other, down_w, plan, after=(in_vmem(part_b),))
    own_back_f = to_experts(down_blocks[:n_expert], relative)
    other_back_f = to_experts(down_blocks[n_expert:], relative)
    turned = turn(rows_b, after=down_blocks[:1])
    cots, part_b = d_hidden(cots_b, down_w, part_b, after=(in_vmem(turned),), weight=1000)
    part_b_other = exchange(part_b, "dp", 1)
    own_sum = combine(
        metas, own_back_f, plan, row_f, True, False, after=(in_vmem(part_b),), weight=2000
    )
    y_mine = section_shift(own_sum, 0)
    hidden, d_gate, d_up, *back_blocks = back(
        part_b, part_b_other, gate_w, up_w, plan, after=(own_sum,)
    )
    own_back_b = to_experts(back_blocks[:n_expert], relative)
    other_back_b = to_experts(back_blocks[n_expert:], relative)
    other_sum = combine(
        metas, other_back_f, plan, row_f, True, True, after=back_blocks[:1], weight=150
    )
    y_rest = section_shift(other_sum, 1)
    own_sum = combine(
        metas,
        own_back_b,
        plan,
        row_b,
        False,
        False,
        after=(other_sum, in_vmem(y_mine)),
        weight=150,
    )
    dx_mine = section_shift(own_sum, 0)
    other_sum = combine(
        metas,
        other_back_b,
        plan,
        row_b,
        False,
        True,
        after=(own_sum, in_vmem(y_rest)),
        weight=100,
    )
    dx_rest = section_shift(other_sum, 1)
    grad_g, grad_u, grad_d = grads(
        hidden, d_gate, d_up, turned, cots, after=(other_sum, in_vmem(dx_mine)), weight=100
    )
    y_next, dx_next = finish(y_mine, y_rest, dx_mine, dx_rest, after=(in_hbm(grad_g),))
    return (
        y_next[None],
        dx_next[None],
        grad_g[None, None],
        grad_u[None, None],
        grad_d[None, None],
    )


def solution(mesh):
    rows = P("section", ("expert", "dp"), None)
    by_feature = P("section", "expert", "dp", None)
    down_spec = P("section", "expert", None, "dp")
    return jax.shard_map(
        local,
        mesh=mesh,
        in_specs=(rows,) * 7 + (by_feature, by_feature, down_spec),
        out_specs=(rows, rows, by_feature, by_feature, down_spec),
        check_vma=False,
    )
```

```python
import functools

import jax
import jax.numpy as jnp
from jax import lax
from jax.experimental import pallas as pl
from jax.experimental.pallas import tpu as pltpu
from jax.sharding import PartitionSpec as P

FF = 1024
TOP = 2
TILE = 256
VMEM_LIMIT = 20 * 1024 * 1024
META = 16
COST = 10**7
F32 = jnp.float32
BF16 = jnp.bfloat16


def exchange(value, axis, mask):
    count = lax.axis_size(axis)
    return lax.ppermute(value, axis, [(source, source ^ mask) for source in range(count)])


def section_shift(value, flip):
    sections, cores = lax.axis_size("section"), lax.axis_size("dp")
    pairs = []
    for section in range(sections):
        for core in range(cores):
            target = ((section + 1) % sections) * cores + (core ^ flip)
            pairs.append((section * cores + core, target))
    return lax.ppermute(value, ("section", "dp"), pairs)


def dot(left, right, left_dim, right_dim):
    return lax.dot_general(
        left, right, (((left_dim,), (right_dim,)), ((), ())), preferred_element_type=F32
    )


VMEM = pl.BlockSpec(memory_space=pltpu.VMEM)
HBM = pl.BlockSpec(memory_space=pltpu.HBM)
AFTER = pl.BlockSpec(memory_space=pl.ANY)


def call(kernel, out_shape, in_specs, out_specs, scratch, grid=(), weight=1, aliases={}):
    return pl.pallas_call(
        kernel,
        out_shape=out_shape,
        grid=grid,
        in_specs=in_specs,
        out_specs=out_specs,
        scratch_shapes=scratch,
        input_output_aliases=aliases,
        compiler_params=pltpu.CompilerParams(vmem_limit_bytes=VMEM_LIMIT),
        cost_estimate=pl.CostEstimate(
            flops=weight * COST, bytes_accessed=1, transcendentals=0
        ),
    )


def array(*shape):
    return jax.ShapeDtypeStruct(shape, BF16)


def in_vmem(value):
    return pltpu.with_memory_space_constraint(value, pltpu.VMEM)


def in_hbm(value):
    return pltpu.with_memory_space_constraint(value, pltpu.HBM)


def halves(value_ref, own_ref, other_ref, sems, first):
    tokens, width = value_ref.shape[0], value_ref.shape[1] // 2
    core = lax.axis_index("dp")
    copies = []
    for place, (half, target) in enumerate(((core, own_ref), (1 - core, other_ref))):
        columns = pl.ds(pl.multiple_of(half * width, 128), width)
        copies.append(
            pltpu.make_async_copy(
                value_ref.at[:, columns], target.at[0:tokens], sems.at[first + place]
            )
        )
    for copy in copies:
        copy.start()
    return copies


def pack_kernel(f_ref, *refs):
    sources, (own, other, packed, sems), held = refs[:4], refs[4:8], refs[8:]
    tokens = f_ref.shape[0]
    small = [
        pltpu.make_async_copy(source, target, sems.at[2 + place])
        for place, (source, target) in enumerate(zip(sources, held))
    ]
    for copy in small:
        copy.start()
    copies = halves(f_ref, own, other, sems, 0)
    packed[...] = jnp.zeros_like(packed)
    for copy in small:
        copy.wait()
    for start, ids, route in ((0, *held[:2]), (META // 2, *held[2:])):
        packed[start : start + 2, 0:tokens] = ids[...].astype(F32)
        rest = route[...]
        for piece in range(3):
            top = rest.astype(BF16).astype(F32)
            row = start + 2 + 2 * piece
            packed[row : row + 2, 0:tokens] = top
            rest = rest - top
    mine = packed[...]
    lanes = packed.shape[1]
    own[tokens : tokens + META, 0:lanes] = mine.astype(BF16)
    other[tokens : tokens + META, 0:lanes] = pltpu.roll(mine, tokens, 1).astype(BF16)
    for copy in copies:
        copy.wait()


def pack(f, *small):
    tokens, width = f.shape[0], f.shape[1] // 2
    return call(
        pack_kernel,
        [array(tokens + META, width)] * 2,
        [HBM] * 5,
        [VMEM] * 2,
        [pltpu.VMEM((META, 2 * tokens), F32), pltpu.SemaphoreType.DMA((6,))]
        + [pltpu.VMEM(value.shape, value.dtype) for value in small],
    )(f, *small)


def cut_kernel(x_ref, dy_ref, *refs):
    own_x, own_dy, other, sems = refs[-4:]
    tokens = x_ref.shape[0]
    copies = halves(x_ref, own_x, other.at[0:tokens], sems, 0)
    copies += halves(dy_ref, own_dy, other.at[tokens : 2 * tokens], sems, 2)
    for copy in copies:
        copy.wait()


def cut(x, dy, after):
    tokens, width = x.shape[0], x.shape[1] // 2
    return call(
        cut_kernel,
        [array(tokens, width)] * 2 + [array(2 * tokens, width)],
        [HBM] * 2 + [AFTER] * len(after),
        [VMEM] * 3,
        [pltpu.SemaphoreType.DMA((4,))],
    )(x, dy, *after)


def load_kernel(*refs, count):
    sources, targets, sems = refs[:count], refs[-count - 1 : -1], refs[-1]
    copies = [
        pltpu.make_async_copy(source, target, sems.at[place])
        for place, (source, target) in enumerate(zip(sources, targets))
    ]
    for copy in copies:
        copy.start()
    for copy in copies:
        copy.wait()


def load(weights, after):
    return call(
        functools.partial(load_kernel, count=len(weights)),
        [array(*weight.shape) for weight in weights],
        [HBM] * len(weights) + [AFTER] * len(after),
        [VMEM] * len(weights),
        [pltpu.SemaphoreType.DMA((len(weights),))],
    )(*weights, *after)


class Plan:
    def __init__(self, blocks, part, group, tokens, relative):
        self.blocks, self.part, self.group = blocks, part, group
        self.tokens, self.relative = tokens, relative


def slot_rows(own_meta, other_meta, plan, first_row):
    lanes = 2 * plan.tokens
    padded = max(8, plan.blocks)
    me = lax.axis_index("expert") if plan.relative else 0
    meta = own_meta[plan.tokens : plan.tokens + META, 0:lanes].astype(F32)
    meta = meta + other_meta[plan.tokens : plan.tokens + META, 0:lanes].astype(F32)
    meta = meta[first_row : first_row + META // 2]
    first, second = meta[0:1], meta[1:2]
    route = meta[2:4] + meta[4:6] + meta[6:8]
    row = lax.broadcasted_iota(jnp.int32, (padded, lanes), 0)
    expert = ((row ^ me) // plan.group).astype(F32)
    is_first, is_second = expert == first, expert == second
    named = jnp.where(is_first | is_second, 1.0, 0.0)
    before = lax.broadcasted_iota(jnp.int32, (lanes, lanes), 0)
    after = lax.broadcasted_iota(jnp.int32, (lanes, lanes), 1)
    earlier = (before < after) & ((before < plan.tokens) == (after < plan.tokens))
    position = dot(named.astype(BF16), jnp.where(earlier, 1.0, 0.0).astype(BF16), 1, 0)
    lane = lax.broadcasted_iota(jnp.int32, (padded, lanes), 1)
    slot = position + jnp.where(lane < plan.tokens, 0, plan.part).astype(F32)
    slot = jnp.where(named > 0.5, slot, -1.0)
    return slot, jnp.where(is_first, route[0:1], route[1:2])


def slot_table(slot, block, first, rows):
    index = lax.broadcasted_iota(jnp.int32, (rows, slot.shape[1]), 0) + first
    index = index.astype(F32)
    return jnp.where(index == slot[block : block + 1, :], 1.0, 0.0)


def dispatch_kernel(
    own_meta, other_meta, own_ref, other_ref, *refs, plan, first_row, other_row, weighted, passed
):
    outs = refs[len(refs) - plan.blocks - passed : len(refs) - passed]
    width, tokens = outs[0].shape[1], plan.tokens
    slot, route = slot_rows(own_meta, other_meta, plan, first_row)
    values = jnp.concatenate([own_ref[0:tokens, :], other_ref[other_row : other_row + tokens, :]], axis=0)
    for block in range(plan.blocks):
        table = slot_table(slot, block, 0, 2 * plan.part)
        if weighted:
            scale = jnp.sum(table * route[block : block + 1, :], axis=1, keepdims=True)
        table = table.astype(BF16)
        for start in range(0, width, TILE):
            picked = dot(table, values[:, start : start + TILE], 1, 0)
            if weighted:
                picked = picked * scale
            outs[block][:, start : start + TILE] = picked.astype(BF16)


def dispatch(metas, own, other, plan, first_row, other_row, weighted, after=(), passing=()):
    width = own.shape[1]
    return call(
        functools.partial(
            dispatch_kernel,
            plan=plan,
            first_row=first_row,
            other_row=other_row,
            weighted=weighted,
            passed=len(passing),
        ),
        [array(2 * plan.part, width)] * plan.blocks + [array(*value.shape) for value in passing],
        [VMEM] * (4 + len(passing)) + [AFTER] * len(after),
        [VMEM] * (plan.blocks + len(passing)),
        [],
        aliases={4 + place: plan.blocks + place for place in range(len(passing))},
    )(*metas, own, other, *passing, *after)


def combine_kernel(own_meta, other_meta, *refs, plan, first_row, weighted, other):
    returned, out = refs[: plan.blocks], refs[-1]
    width, tokens = out.shape[1], plan.tokens
    slot, route = slot_rows(own_meta, other_meta, plan, first_row)
    table = []
    for block in range(plan.blocks):
        table.append(slot_table(slot, block, plan.part if other else 0, plan.part))
        if weighted:
            table[block] = table[block] * route[block : block + 1, :]
    table = jnp.concatenate(table, axis=0)
    high = table.astype(BF16)
    low = (table - high.astype(F32)).astype(BF16)
    for start in range(0, width, TILE):
        part = slice(start, start + TILE)
        values = jnp.concatenate([ref[:, part].astype(F32) for ref in returned], axis=0)
        values = values.astype(BF16)
        total = dot(high, values, 0, 0)
        if weighted:
            total += dot(low, values, 0, 0)
        out[:, part] = total[tokens if other else 0 :][:tokens].astype(BF16)


def combine(metas, returned, plan, first_row, weighted, other, after=(), weight=1):
    return call(
        functools.partial(
            combine_kernel, plan=plan, first_row=first_row, weighted=weighted, other=other
        ),
        array(plan.tokens, returned[0].shape[1]),
        [VMEM] * (2 + plan.blocks) + [AFTER] * len(after),
        VMEM,
        [],
        weight=weight,
    )(*metas, *returned, *after)


def joined(refs):
    return jnp.concatenate([ref[...] for ref in refs], axis=0)


def gate_up_kernel(*refs, blocks):
    gate_w, up_w = refs[blocks : blocks + 2]
    out, rows = refs[-2:]
    rows[...] = joined(refs[:blocks])
    for start in range(0, out.shape[2], TILE):
        part = slice(start, start + TILE)
        out[0, :, part] = dot(rows[...], gate_w[:, part], 1, 0).astype(BF16)
        out[1, :, part] = dot(rows[...], up_w[:, part], 1, 0).astype(BF16)


def gate_up(inputs, gate_w, up_w, after=(), weight=1):
    blocks, (rows, width) = len(inputs), inputs[0].shape
    units, total = gate_w.shape[1], blocks * rows
    return call(
        functools.partial(gate_up_kernel, blocks=blocks),
        array(2, total, units),
        [VMEM] * (blocks + 2) + [AFTER] * len(after),
        VMEM,
        [pltpu.VMEM((total, width), BF16)],
        weight=weight,
    )(*inputs, gate_w, up_w, *after)


def d_hidden_kernel(*refs, blocks):
    down_w = refs[blocks]
    rows, out = refs[-2:]
    rows[...] = joined(refs[:blocks])
    for start in range(0, out.shape[1], TILE):
        part = slice(start, start + TILE)
        out[:, part] = dot(rows[...], down_w[part, :], 1, 1).astype(BF16)


def d_hidden(inputs, down_w, after=(), weight=1):
    blocks, (rows, width) = len(inputs), inputs[0].shape
    return call(
        functools.partial(d_hidden_kernel, blocks=blocks),
        [array(blocks * rows, width), array(blocks * rows, down_w.shape[0])],
        [VMEM] * (blocks + 1) + [AFTER] * len(after),
        [VMEM] * 2,
        [],
        weight=weight,
    )(*inputs, down_w, *after)


def scatter_tile(value, outs, columns):
    blocks, part = len(outs) // 2, outs[0].shape[0]
    for place, out in enumerate(outs):
        first = (2 * (place % blocks) + place // blocks) * part
        out[:, columns] = value[first : first + part].astype(BF16)


def total_of(own, other, part):
    own, other = own.astype(F32), other.astype(F32)
    rows = own.shape[0]
    turned = []
    for first in range(0, rows, 2 * part):
        turned += [other[first + part : first + 2 * part], other[first : first + part]]
    return own + jnp.concatenate(turned, axis=0)


def down_kernel(own_ref, other_ref, down_w, *refs, blocks):
    outs, hidden = refs[-1 - 2 * blocks : -1], refs[-1]
    part = outs[0].shape[0]
    for start in range(0, hidden.shape[1], TILE):
        columns = slice(start, start + TILE)
        gate = total_of(own_ref[0, :, columns], other_ref[0, :, columns], part)
        up = total_of(own_ref[1, :, columns], other_ref[1, :, columns], part)
        hidden[:, columns] = (gate * jax.nn.sigmoid(gate) * up).astype(BF16)
    for start in range(0, outs[0].shape[1], TILE):
        columns = slice(start, start + TILE)
        scatter_tile(dot(hidden[...], down_w[:, columns], 1, 0), outs, columns)


def down(own, other, down_w, plan, after=()):
    _, total, units = own.shape
    return call(
        functools.partial(down_kernel, blocks=plan.blocks),
        [array(plan.part, down_w.shape[1])] * (2 * plan.blocks),
        [VMEM] * 3 + [AFTER] * len(after),
        [VMEM] * (2 * plan.blocks),
        [pltpu.VMEM((total, units), BF16)],
    )(own, other, down_w, *after)


def back_kernel(own_ref, other_ref, own_d, other_d, gate_w, up_w, *refs, blocks):
    hidden, d_gate, d_up, *outs = refs[-3 - 2 * blocks :]
    part = outs[0].shape[0]
    for start in range(0, hidden.shape[1], TILE):
        columns = slice(start, start + TILE)
        gate = total_of(own_ref[0, :, columns], other_ref[0, :, columns], part)
        up = total_of(own_ref[1, :, columns], other_ref[1, :, columns], part)
        d_hid = total_of(own_d[:, columns], other_d[:, columns], part)
        sigmoid = jax.nn.sigmoid(gate)
        activated = gate * sigmoid
        hidden[:, columns] = (activated * up).astype(BF16)
        d_up[:, columns] = (d_hid * activated).astype(BF16)
        d_gate[:, columns] = (
            d_hid * up * sigmoid * (1.0 + gate * (1.0 - sigmoid))
        ).astype(BF16)
    for start in range(0, outs[0].shape[1], TILE):
        columns = slice(start, start + TILE)
        total = dot(d_gate[...], gate_w[columns, :], 1, 1)
        total += dot(d_up[...], up_w[columns, :], 1, 1)
        scatter_tile(total, outs, columns)


def back(own, other, own_d, other_d, gate_w, up_w, plan, after=()):
    _, total, units = own.shape
    return call(
        functools.partial(back_kernel, blocks=plan.blocks),
        [array(total, units)] * 3 + [array(plan.part, gate_w.shape[0])] * (2 * plan.blocks),
        [VMEM] * 6 + [AFTER] * len(after),
        [VMEM] * (3 + 2 * plan.blocks),
        [],
    )(own, other, own_d, other_d, gate_w, up_w, *after)


def turn_kernel(*refs, blocks):
    inputs, turned = refs[:blocks], refs[-1]
    for start in range(0, turned.shape[0], TILE):
        part = slice(start, start + TILE)
        turned[part, :] = jnp.concatenate([ref[:, part] for ref in inputs], axis=0).T


def turn(inputs, after=()):
    blocks, (rows, width) = len(inputs), inputs[0].shape
    return call(
        functools.partial(turn_kernel, blocks=blocks),
        array(width, blocks * rows),
        [VMEM] * blocks + [AFTER] * len(after),
        VMEM,
        [],
    )(*inputs, *after)


def grad_kernel(hidden, d_gate, d_up, turned, cots, *refs):
    grad_gate, grad_up, grad_down = refs[-3:]
    part = pl.ds(pl.multiple_of(pl.program_id(0) * TILE, TILE), TILE)
    grad_gate[...] = dot(turned[...], d_gate[:, part], 1, 0).astype(BF16)
    grad_up[...] = dot(turned[...], d_up[:, part], 1, 0).astype(BF16)
    grad_down[...] = dot(hidden[:, part], cots[...], 0, 0).astype(BF16)


def grads(hidden, d_gate, d_up, turned, cots, after=(), weight=1):
    width, units = turned.shape[0], d_gate.shape[1]
    by_column = pl.BlockSpec((width, TILE), lambda i: (0, i))
    return call(
        grad_kernel,
        [pltpu.HBM((width, units), BF16)] * 2 + [pltpu.HBM((units, width), BF16)],
        [VMEM] * 5 + [AFTER] * len(after),
        [by_column, by_column, pl.BlockSpec((TILE, width), lambda i: (i, 0))],
        [],
        grid=(units // TILE,),
        weight=weight,
    )(hidden, d_gate, d_up, turned, cots, *after)


def to_experts(blocks, relative):
    if not relative:
        stacked = lax.all_to_all(jnp.stack(blocks), "expert", split_axis=0, concat_axis=0)
        return [stacked[block] for block in range(len(blocks))]
    return [blocks[0]] + [
        exchange(block, "expert", mask) for mask, block in enumerate(blocks) if mask > 0
    ]


def finish_kernel(*refs):
    sources, outs, sems = refs[:4], refs[-3:-1], refs[-1]
    width = sources[0].shape[1]
    core = lax.axis_index("dp")
    copies = []
    for place, source in enumerate(sources):
        half = core if place % 2 == 0 else 1 - core
        columns = pl.ds(pl.multiple_of(half * width, 128), width)
        copies.append(
            pltpu.make_async_copy(source, outs[place // 2].at[:, columns], sems.at[place])
        )
    for copy in copies:
        copy.start()
    for copy in copies:
        copy.wait()


def finish(y_mine, y_rest, dx_mine, dx_rest, after):
    tokens, width = y_mine.shape
    return call(
        finish_kernel,
        [pltpu.HBM((tokens, 2 * width), BF16)] * 2,
        [VMEM] * 4 + [AFTER] * len(after),
        [HBM] * 2,
        [pltpu.SemaphoreType.DMA((4,))],
    )(y_mine, y_rest, dx_mine, dx_rest, *after)


def local(x_fwd, ids_fwd, route_fwd, x_bwd, ids_bwd, route_bwd, dy_bwd, w_gate, w_up, w_down):
    n_expert = lax.axis_size("expert")
    slab_width = w_gate.shape[-1]
    group = FF // slab_width
    experts = n_expert // group
    tokens = x_fwd.shape[1]
    spread = 4 * experts * group
    capacity = group * ((5 * tokens * TOP + spread - 1) // spread)
    relative = n_expert <= 8
    plan = Plan(n_expert, (capacity + 7) // 8 * 8, group, tokens, relative)
    row_b, row_f = 0, META // 2

    own_f, send_f = pack(
        in_hbm(x_fwd[0]),
        *[in_hbm(value[0].T) for value in (ids_bwd, route_bwd, ids_fwd, route_fwd)],
    )
    other_f = exchange(send_f, "dp", 1)
    own_x, own_dy, send_rest = cut(in_hbm(x_bwd[0]), in_hbm(dy_bwd[0]), after=(own_f,))
    metas = (own_f, other_f)
    *sent_f, send_rest = dispatch(
        metas, own_f, other_f, plan, row_f, 0, False, passing=(send_rest,)
    )
    rows_f = to_experts(sent_f, relative)
    other_rest = exchange(send_rest, "dp", 1)
    sent_x = dispatch(metas, own_x, other_rest, plan, row_b, 0, False)
    rows_b = to_experts(sent_x, relative)
    gate_w, up_w, down_w = load(
        [in_hbm(weight[0, 0]) for weight in (w_gate, w_up, w_down)], after=sent_x[:1]
    )
    sent_dy = dispatch(
        metas, own_dy, other_rest, plan, row_b, tokens, True, after=(in_vmem(down_w),)
    )
    cots_b = to_experts(sent_dy, relative)

    part_f = gate_up(rows_f, gate_w, up_w, after=sent_dy[:1])
    part_f_other = exchange(part_f, "dp", 1)
    part_b = gate_up(rows_b, gate_w, up_w, after=(part_f,), weight=3000)
    part_b_other = exchange(part_b, "dp", 1)
    down_blocks = down(part_f, part_f_other, down_w, plan, after=(in_vmem(part_b),))
    own_back_f = to_experts(down_blocks[:n_expert], relative)
    other_back_f = to_experts(down_blocks[n_expert:], relative)
    turned = turn(rows_b, after=down_blocks[:1])
    cots, part_d = d_hidden(cots_b, down_w, after=(in_vmem(turned),), weight=1000)
    part_d_other = exchange(part_d, "dp", 1)
    hidden, d_gate, d_up, *back_blocks = back(
        part_b, part_b_other, part_d, part_d_other, gate_w, up_w, plan
    )
    own_sum = combine(
        metas, own_back_f, plan, row_f, True, False, after=(back_blocks[0],), weight=2000
    )
    y_mine = section_shift(own_sum, 0)
    own_back_b = to_experts(back_blocks[:n_expert], relative)
    other_back_b = to_experts(back_blocks[n_expert:], relative)
    other_sum = combine(
        metas, other_back_f, plan, row_f, True, True, after=back_blocks[:1], weight=150
    )
    y_rest = section_shift(other_sum, 1)
    own_sum = combine(
        metas,
        own_back_b,
        plan,
        row_b,
        False,
        False,
        after=(other_sum, in_vmem(y_mine)),
        weight=150,
    )
    dx_mine = section_shift(own_sum, 0)
    other_sum = combine(
        metas,
        other_back_b,
        plan,
        row_b,
        False,
        True,
        after=(own_sum, in_vmem(y_rest)),
        weight=100,
    )
    dx_rest = section_shift(other_sum, 1)
    grad_g, grad_u, grad_d = grads(
        hidden, d_gate, d_up, turned, cots, after=(other_sum, in_vmem(dx_mine)), weight=100
    )
    y_next, dx_next = finish(y_mine, y_rest, dx_mine, dx_rest, after=(in_hbm(grad_g),))
    return (
        y_next[None],
        dx_next[None],
        grad_g[None, None],
        grad_u[None, None],
        grad_d[None, None],
    )


def solution(mesh):
    rows = P("section", ("expert", "dp"), None)
    by_feature = P("section", "expert", "dp", None)
    down_spec = P("section", "expert", None, "dp")
    return jax.shard_map(
        local,
        mesh=mesh,
        in_specs=(rows,) * 7 + (by_feature, by_feature, down_spec),
        out_specs=(rows, rows, by_feature, by_feature, down_spec),
        check_vma=False,
    )
```

```python
import functools

import jax
import jax.numpy as jnp
from jax import lax
from jax.experimental import pallas as pl
from jax.experimental.pallas import tpu as pltpu
from jax.sharding import PartitionSpec as P

FF = 1024
TOP = 2
TILE = 256
VMEM_LIMIT = 20 * 1024 * 1024
META = 16
COST = 10**7
F32 = jnp.float32
BF16 = jnp.bfloat16


def exchange(value, axis, mask):
    count = lax.axis_size(axis)
    return lax.ppermute(value, axis, [(source, source ^ mask) for source in range(count)])


def section_shift(value, flip):
    sections, cores = lax.axis_size("section"), lax.axis_size("dp")
    pairs = []
    for section in range(sections):
        for core in range(cores):
            target = ((section + 1) % sections) * cores + (core ^ flip)
            pairs.append((section * cores + core, target))
    return lax.ppermute(value, ("section", "dp"), pairs)


def dot(left, right, left_dim, right_dim):
    return lax.dot_general(
        left, right, (((left_dim,), (right_dim,)), ((), ())), preferred_element_type=F32
    )


VMEM = pl.BlockSpec(memory_space=pltpu.VMEM)
HBM = pl.BlockSpec(memory_space=pltpu.HBM)
AFTER = pl.BlockSpec(memory_space=pl.ANY)


def call(kernel, out_shape, in_specs, out_specs, scratch, grid=(), weight=1, aliases={}):
    return pl.pallas_call(
        kernel,
        out_shape=out_shape,
        grid=grid,
        in_specs=in_specs,
        out_specs=out_specs,
        scratch_shapes=scratch,
        input_output_aliases=aliases,
        compiler_params=pltpu.CompilerParams(vmem_limit_bytes=VMEM_LIMIT),
        cost_estimate=pl.CostEstimate(
            flops=weight * COST, bytes_accessed=1, transcendentals=0
        ),
    )


def array(*shape):
    return jax.ShapeDtypeStruct(shape, BF16)


def in_vmem(value):
    return pltpu.with_memory_space_constraint(value, pltpu.VMEM)


def in_hbm(value):
    return pltpu.with_memory_space_constraint(value, pltpu.HBM)


def halves(value_ref, own_ref, other_ref, sems, first):
    tokens, width = value_ref.shape[0], value_ref.shape[1] // 2
    core = lax.axis_index("dp")
    copies = []
    for place, (half, target) in enumerate(((core, own_ref), (1 - core, other_ref))):
        columns = pl.ds(pl.multiple_of(half * width, 128), width)
        copies.append(
            pltpu.make_async_copy(
                value_ref.at[:, columns], target.at[0:tokens], sems.at[first + place]
            )
        )
    for copy in copies:
        copy.start()
    return copies


def pack_kernel(f_ref, *refs):
    sources, (own, other, packed, sems), held = refs[:4], refs[4:8], refs[8:]
    tokens = f_ref.shape[0]
    small = [
        pltpu.make_async_copy(source, target, sems.at[2 + place])
        for place, (source, target) in enumerate(zip(sources, held))
    ]
    for copy in small:
        copy.start()
    copies = halves(f_ref, own, other, sems, 0)
    packed[...] = jnp.zeros_like(packed)
    for copy in small:
        copy.wait()
    for start, ids, route in ((0, *held[:2]), (META // 2, *held[2:])):
        packed[start : start + 2, 0:tokens] = ids[...].astype(F32)
        rest = route[...]
        for piece in range(3):
            top = rest.astype(BF16).astype(F32)
            row = start + 2 + 2 * piece
            packed[row : row + 2, 0:tokens] = top
            rest = rest - top
    mine = packed[...]
    lanes = packed.shape[1]
    own[tokens : tokens + META, 0:lanes] = mine.astype(BF16)
    other[tokens : tokens + META, 0:lanes] = pltpu.roll(mine, tokens, 1).astype(BF16)
    for copy in copies:
        copy.wait()


def pack(f, *small):
    tokens, width = f.shape[0], f.shape[1] // 2
    return call(
        pack_kernel,
        [array(tokens + META, width)] * 2,
        [HBM] * 5,
        [VMEM] * 2,
        [pltpu.VMEM((META, 2 * tokens), F32), pltpu.SemaphoreType.DMA((6,))]
        + [pltpu.VMEM(value.shape, value.dtype) for value in small],
    )(f, *small)


def cut_kernel(x_ref, dy_ref, *refs):
    own_x, own_dy, other, sems = refs[-4:]
    tokens = x_ref.shape[0]
    copies = halves(x_ref, own_x, other.at[0:tokens], sems, 0)
    copies += halves(dy_ref, own_dy, other.at[tokens : 2 * tokens], sems, 2)
    for copy in copies:
        copy.wait()


def cut(x, dy, after):
    tokens, width = x.shape[0], x.shape[1] // 2
    return call(
        cut_kernel,
        [array(tokens, width)] * 2 + [array(2 * tokens, width)],
        [HBM] * 2 + [AFTER] * len(after),
        [VMEM] * 3,
        [pltpu.SemaphoreType.DMA((4,))],
    )(x, dy, *after)


def load_kernel(*refs, count):
    sources, targets, sems = refs[:count], refs[-count - 1 : -1], refs[-1]
    copies = [
        pltpu.make_async_copy(source, target, sems.at[place])
        for place, (source, target) in enumerate(zip(sources, targets))
    ]
    for copy in copies:
        copy.start()
    for copy in copies:
        copy.wait()


def load(weights, after):
    return call(
        functools.partial(load_kernel, count=len(weights)),
        [array(*weight.shape) for weight in weights],
        [HBM] * len(weights) + [AFTER] * len(after),
        [VMEM] * len(weights),
        [pltpu.SemaphoreType.DMA((len(weights),))],
    )(*weights, *after)


class Plan:
    def __init__(self, blocks, part, group, tokens, relative):
        self.blocks, self.part, self.group = blocks, part, group
        self.tokens, self.relative = tokens, relative


def slot_rows(own_meta, other_meta, plan, first_row):
    lanes = 2 * plan.tokens
    padded = max(8, plan.blocks)
    me = lax.axis_index("expert") if plan.relative else 0
    meta = own_meta[plan.tokens : plan.tokens + META, 0:lanes].astype(F32)
    meta = meta + other_meta[plan.tokens : plan.tokens + META, 0:lanes].astype(F32)
    meta = meta[first_row : first_row + META // 2]
    first, second = meta[0:1], meta[1:2]
    route = meta[2:4] + meta[4:6] + meta[6:8]
    row = lax.broadcasted_iota(jnp.int32, (padded, lanes), 0)
    expert = ((row ^ me) // plan.group).astype(F32)
    is_first, is_second = expert == first, expert == second
    named = jnp.where(is_first | is_second, 1.0, 0.0)
    before = lax.broadcasted_iota(jnp.int32, (lanes, lanes), 0)
    after = lax.broadcasted_iota(jnp.int32, (lanes, lanes), 1)
    earlier = (before < after) & ((before < plan.tokens) == (after < plan.tokens))
    position = dot(named.astype(BF16), jnp.where(earlier, 1.0, 0.0).astype(BF16), 1, 0)
    lane = lax.broadcasted_iota(jnp.int32, (padded, lanes), 1)
    slot = position + jnp.where(lane < plan.tokens, 0, plan.part).astype(F32)
    slot = jnp.where(named > 0.5, slot, -1.0)
    return slot, jnp.where(is_first, route[0:1], route[1:2])


def slot_table(slot, block, first, rows):
    index = lax.broadcasted_iota(jnp.int32, (rows, slot.shape[1]), 0) + first
    index = index.astype(F32)
    return jnp.where(index == slot[block : block + 1, :], 1.0, 0.0)


def dispatch_kernel(
    own_meta, other_meta, own_ref, other_ref, *refs, plan, first_row, other_row, weighted, passed
):
    outs = refs[len(refs) - plan.blocks - passed : len(refs) - passed]
    width, tokens = outs[0].shape[1], plan.tokens
    slot, route = slot_rows(own_meta, other_meta, plan, first_row)
    values = jnp.concatenate([own_ref[0:tokens, :], other_ref[other_row : other_row + tokens, :]], axis=0)
    for block in range(plan.blocks):
        table = slot_table(slot, block, 0, 2 * plan.part)
        if weighted:
            scale = jnp.sum(table * route[block : block + 1, :], axis=1, keepdims=True)
        table = table.astype(BF16)
        for start in range(0, width, TILE):
            picked = dot(table, values[:, start : start + TILE], 1, 0)
            if weighted:
                picked = picked * scale
            outs[block][:, start : start + TILE] = picked.astype(BF16)


def dispatch(metas, own, other, plan, first_row, other_row, weighted, after=(), passing=()):
    width = own.shape[1]
    return call(
        functools.partial(
            dispatch_kernel,
            plan=plan,
            first_row=first_row,
            other_row=other_row,
            weighted=weighted,
            passed=len(passing),
        ),
        [array(2 * plan.part, width)] * plan.blocks + [array(*value.shape) for value in passing],
        [VMEM] * (4 + len(passing)) + [AFTER] * len(after),
        [VMEM] * (plan.blocks + len(passing)),
        [],
        aliases={4 + place: plan.blocks + place for place in range(len(passing))},
    )(*metas, own, other, *passing, *after)


def combine_kernel(own_meta, other_meta, *refs, plan, first_row, weighted, other):
    returned, out = refs[: plan.blocks], refs[-1]
    width, tokens = out.shape[1], plan.tokens
    slot, route = slot_rows(own_meta, other_meta, plan, first_row)
    table = []
    for block in range(plan.blocks):
        table.append(slot_table(slot, block, plan.part if other else 0, plan.part))
        if weighted:
            table[block] = table[block] * route[block : block + 1, :]
    table = jnp.concatenate(table, axis=0)
    high = table.astype(BF16)
    low = (table - high.astype(F32)).astype(BF16)
    for start in range(0, width, TILE):
        part = slice(start, start + TILE)
        values = jnp.concatenate([ref[:, part].astype(F32) for ref in returned], axis=0)
        values = values.astype(BF16)
        total = dot(high, values, 0, 0)
        if weighted:
            total += dot(low, values, 0, 0)
        out[:, part] = total[tokens if other else 0 :][:tokens].astype(BF16)


def combine(metas, returned, plan, first_row, weighted, other, after=(), weight=1):
    return call(
        functools.partial(
            combine_kernel, plan=plan, first_row=first_row, weighted=weighted, other=other
        ),
        array(plan.tokens, returned[0].shape[1]),
        [VMEM] * (2 + plan.blocks) + [AFTER] * len(after),
        VMEM,
        [],
        weight=weight,
    )(*metas, *returned, *after)


def joined(refs):
    return jnp.concatenate([ref[...] for ref in refs], axis=0)


def gate_up_kernel(*refs, blocks):
    gate_w, up_w = refs[blocks : blocks + 2]
    out, rows = refs[-2:]
    rows[...] = joined(refs[:blocks])
    for start in range(0, out.shape[2], TILE):
        part = slice(start, start + TILE)
        out[0, :, part] = dot(rows[...], gate_w[:, part], 1, 0).astype(BF16)
        out[1, :, part] = dot(rows[...], up_w[:, part], 1, 0).astype(BF16)


def gate_up(inputs, gate_w, up_w, after=(), weight=1):
    blocks, (rows, width) = len(inputs), inputs[0].shape
    units, total = gate_w.shape[1], blocks * rows
    return call(
        functools.partial(gate_up_kernel, blocks=blocks),
        array(2, total, units),
        [VMEM] * (blocks + 2) + [AFTER] * len(after),
        VMEM,
        [pltpu.VMEM((total, width), BF16)],
        weight=weight,
    )(*inputs, gate_w, up_w, *after)


def d_hidden_kernel(*refs, blocks):
    down_w = refs[blocks]
    rows, out = refs[-2:]
    rows[...] = joined(refs[:blocks])
    for start in range(0, out.shape[1], TILE):
        part = slice(start, start + TILE)
        out[:, part] = dot(rows[...], down_w[part, :], 1, 1).astype(BF16)


def d_hidden(inputs, down_w, after=(), weight=1):
    blocks, (rows, width) = len(inputs), inputs[0].shape
    return call(
        functools.partial(d_hidden_kernel, blocks=blocks),
        [array(blocks * rows, width), array(blocks * rows, down_w.shape[0])],
        [VMEM] * (blocks + 1) + [AFTER] * len(after),
        [VMEM] * 2,
        [],
        weight=weight,
    )(*inputs, down_w, *after)


def scatter_tile(value, outs, columns):
    blocks, part = len(outs) // 2, outs[0].shape[0]
    for place, out in enumerate(outs):
        first = (2 * (place % blocks) + place // blocks) * part
        out[:, columns] = value[first : first + part].astype(BF16)


def total_of(own, other, part):
    own, other = own.astype(F32), other.astype(F32)
    rows = own.shape[0]
    turned = []
    for first in range(0, rows, 2 * part):
        turned += [other[first + part : first + 2 * part], other[first : first + part]]
    return own + jnp.concatenate(turned, axis=0)


def down_kernel(own_ref, other_ref, down_w, *refs, blocks):
    outs, hidden = refs[-1 - 2 * blocks : -1], refs[-1]
    part = outs[0].shape[0]
    for start in range(0, hidden.shape[1], TILE):
        columns = slice(start, start + TILE)
        gate = total_of(own_ref[0, :, columns], other_ref[0, :, columns], part)
        up = total_of(own_ref[1, :, columns], other_ref[1, :, columns], part)
        hidden[:, columns] = (gate * jax.nn.sigmoid(gate) * up).astype(BF16)
    for start in range(0, outs[0].shape[1], TILE):
        columns = slice(start, start + TILE)
        scatter_tile(dot(hidden[...], down_w[:, columns], 1, 0), outs, columns)


def down(own, other, down_w, plan, after=()):
    _, total, units = own.shape
    return call(
        functools.partial(down_kernel, blocks=plan.blocks),
        [array(plan.part, down_w.shape[1])] * (2 * plan.blocks),
        [VMEM] * 3 + [AFTER] * len(after),
        [VMEM] * (2 * plan.blocks),
        [pltpu.VMEM((total, units), BF16)],
    )(own, other, down_w, *after)


def back_kernel(own_ref, other_ref, own_d, other_d, gate_w, up_w, *refs, blocks):
    hidden, d_gate, d_up, *outs = refs[-3 - 2 * blocks :]
    part = outs[0].shape[0]
    for start in range(0, hidden.shape[1], TILE):
        columns = slice(start, start + TILE)
        gate = total_of(own_ref[0, :, columns], other_ref[0, :, columns], part)
        up = total_of(own_ref[1, :, columns], other_ref[1, :, columns], part)
        d_hid = total_of(own_d[:, columns], other_d[:, columns], part)
        sigmoid = jax.nn.sigmoid(gate)
        activated = gate * sigmoid
        hidden[:, columns] = (activated * up).astype(BF16)
        d_up[:, columns] = (d_hid * activated).astype(BF16)
        d_gate[:, columns] = (
            d_hid * up * sigmoid * (1.0 + gate * (1.0 - sigmoid))
        ).astype(BF16)
    for start in range(0, outs[0].shape[1], TILE):
        columns = slice(start, start + TILE)
        total = dot(d_gate[...], gate_w[columns, :], 1, 1)
        total += dot(d_up[...], up_w[columns, :], 1, 1)
        scatter_tile(total, outs, columns)


def back(own, other, own_d, other_d, gate_w, up_w, plan, after=()):
    _, total, units = own.shape
    return call(
        functools.partial(back_kernel, blocks=plan.blocks),
        [array(total, units)] * 3 + [array(plan.part, gate_w.shape[0])] * (2 * plan.blocks),
        [VMEM] * 6 + [AFTER] * len(after),
        [VMEM] * (3 + 2 * plan.blocks),
        [],
    )(own, other, own_d, other_d, gate_w, up_w, *after)


def turn_kernel(*refs, blocks):
    inputs, turned = refs[:blocks], refs[-1]
    for start in range(0, turned.shape[0], TILE):
        part = slice(start, start + TILE)
        turned[part, :] = jnp.concatenate([ref[:, part] for ref in inputs], axis=0).T


def turn(inputs, after=()):
    blocks, (rows, width) = len(inputs), inputs[0].shape
    return call(
        functools.partial(turn_kernel, blocks=blocks),
        array(width, blocks * rows),
        [VMEM] * blocks + [AFTER] * len(after),
        VMEM,
        [],
    )(*inputs, *after)


def grad_kernel(hidden, d_gate, d_up, turned, cots, *refs):
    grad_gate, grad_up, grad_down = refs[-3:]
    part = pl.ds(pl.multiple_of(pl.program_id(0) * TILE, TILE), TILE)
    grad_gate[...] = dot(turned[...], d_gate[:, part], 1, 0).astype(BF16)
    grad_up[...] = dot(turned[...], d_up[:, part], 1, 0).astype(BF16)
    grad_down[...] = dot(hidden[:, part], cots[...], 0, 0).astype(BF16)


def grads(hidden, d_gate, d_up, turned, cots, after=(), weight=1):
    width, units = turned.shape[0], d_gate.shape[1]
    by_column = pl.BlockSpec((width, TILE), lambda i: (0, i))
    return call(
        grad_kernel,
        [pltpu.HBM((width, units), BF16)] * 2 + [pltpu.HBM((units, width), BF16)],
        [VMEM] * 5 + [AFTER] * len(after),
        [by_column, by_column, pl.BlockSpec((TILE, width), lambda i: (i, 0))],
        [],
        grid=(units // TILE,),
        weight=weight,
    )(hidden, d_gate, d_up, turned, cots, *after)


def to_experts(blocks, relative):
    if not relative:
        stacked = lax.all_to_all(jnp.stack(blocks), "expert", split_axis=0, concat_axis=0)
        return [stacked[block] for block in range(len(blocks))]
    return [blocks[0]] + [
        exchange(block, "expert", mask) for mask, block in enumerate(blocks) if mask > 0
    ]


def finish_kernel(*refs):
    sources, outs, sems = refs[:4], refs[-3:-1], refs[-1]
    width = sources[0].shape[1]
    core = lax.axis_index("dp")
    copies = []
    for place, source in enumerate(sources):
        half = core if place % 2 == 0 else 1 - core
        columns = pl.ds(pl.multiple_of(half * width, 128), width)
        copies.append(
            pltpu.make_async_copy(source, outs[place // 2].at[:, columns], sems.at[place])
        )
    for copy in copies:
        copy.start()
    for copy in copies:
        copy.wait()


def finish(y_mine, y_rest, dx_mine, dx_rest, after):
    tokens, width = y_mine.shape
    return call(
        finish_kernel,
        [pltpu.HBM((tokens, 2 * width), BF16)] * 2,
        [VMEM] * 4 + [AFTER] * len(after),
        [HBM] * 2,
        [pltpu.SemaphoreType.DMA((4,))],
    )(y_mine, y_rest, dx_mine, dx_rest, *after)


def local(x_fwd, ids_fwd, route_fwd, x_bwd, ids_bwd, route_bwd, dy_bwd, w_gate, w_up, w_down):
    n_expert = lax.axis_size("expert")
    slab_width = w_gate.shape[-1]
    group = FF // slab_width
    experts = n_expert // group
    tokens = x_fwd.shape[1]
    spread = 4 * experts * group
    capacity = group * ((5 * tokens * TOP + spread - 1) // spread)
    relative = n_expert <= 8
    plan = Plan(n_expert, (capacity + 7) // 8 * 8, group, tokens, relative)
    row_b, row_f = 0, META // 2

    own_f, send_f = pack(
        in_hbm(x_fwd[0]),
        *[in_hbm(value[0].T) for value in (ids_bwd, route_bwd, ids_fwd, route_fwd)],
    )
    other_f = exchange(send_f, "dp", 1)
    own_x, own_dy, send_rest = cut(in_hbm(x_bwd[0]), in_hbm(dy_bwd[0]), after=(own_f,))
    metas = (own_f, other_f)
    *sent_f, send_rest = dispatch(
        metas, own_f, other_f, plan, row_f, 0, False, passing=(send_rest,)
    )
    rows_f = to_experts(sent_f, relative)
    other_rest = exchange(send_rest, "dp", 1)
    sent_x = dispatch(metas, own_x, other_rest, plan, row_b, 0, False)
    rows_b = to_experts(sent_x, relative)
    gate_w, up_w, down_w = load(
        [in_hbm(weight[0, 0]) for weight in (w_gate, w_up, w_down)], after=sent_x[:1]
    )
    sent_dy = dispatch(
        metas, own_dy, other_rest, plan, row_b, tokens, True, after=(in_vmem(down_w),)
    )
    cots_b = to_experts(sent_dy, relative)

    part_f = gate_up(rows_f, gate_w, up_w, after=sent_dy[:1])
    part_f_other = exchange(part_f, "dp", 1)
    part_b = gate_up(rows_b, gate_w, up_w, after=(part_f,), weight=3000)
    part_b_other = exchange(part_b, "dp", 1)
    down_blocks = down(part_f, part_f_other, down_w, plan, after=(in_vmem(part_b),))
    own_back_f = to_experts(down_blocks[:n_expert], relative)
    other_back_f = to_experts(down_blocks[n_expert:], relative)
    turned = turn(rows_b, after=down_blocks[:1])
    cots, part_d = d_hidden(cots_b, down_w, after=(in_vmem(turned),), weight=1000)
    part_d_other = exchange(part_d, "dp", 1)
    own_sum = combine(
        metas, own_back_f, plan, row_f, True, False, after=(part_d,), weight=2000
    )
    y_mine = section_shift(own_sum, 0)
    hidden, d_gate, d_up, *back_blocks = back(
        part_b, part_b_other, part_d, part_d_other, gate_w, up_w, plan, after=(own_sum,)
    )
    own_back_b = to_experts(back_blocks[:n_expert], relative)
    other_back_b = to_experts(back_blocks[n_expert:], relative)
    other_sum = combine(
        metas, other_back_f, plan, row_f, True, True, after=back_blocks[:1], weight=150
    )
    y_rest = section_shift(other_sum, 1)
    own_sum = combine(
        metas,
        own_back_b,
        plan,
        row_b,
        False,
        False,
        after=(other_sum,),
        weight=300,
    )
    dx_mine = section_shift(own_sum, 0)
    other_sum = combine(
        metas,
        other_back_b,
        plan,
        row_b,
        False,
        True,
        after=(own_sum, in_vmem(y_rest), in_vmem(y_mine)),
        weight=100,
    )
    dx_rest = section_shift(other_sum, 1)
    grad_g, grad_u, grad_d = grads(
        hidden, d_gate, d_up, turned, cots, after=(other_sum, in_vmem(dx_mine)), weight=100
    )
    y_next, dx_next = finish(y_mine, y_rest, dx_mine, dx_rest, after=(in_hbm(grad_g),))
    return (
        y_next[None],
        dx_next[None],
        grad_g[None, None],
        grad_u[None, None],
        grad_d[None, None],
    )


def solution(mesh):
    rows = P("section", ("expert", "dp"), None)
    by_feature = P("section", "expert", "dp", None)
    down_spec = P("section", "expert", None, "dp")
    return jax.shard_map(
        local,
        mesh=mesh,
        in_specs=(rows,) * 7 + (by_feature, by_feature, down_spec),
        out_specs=(rows, rows, by_feature, by_feature, down_spec),
        check_vma=False,
    )
```

```python
import functools

import jax
import jax.numpy as jnp
from jax import lax
from jax.experimental import pallas as pl
from jax.experimental.pallas import tpu as pltpu
from jax.sharding import PartitionSpec as P

FF = 1024
TOP = 2
TILE = 256
VMEM_LIMIT = 20 * 1024 * 1024
META = 16
COST = 10**7
F32 = jnp.float32
BF16 = jnp.bfloat16


def exchange(value, axis, mask):
    count = lax.axis_size(axis)
    return lax.ppermute(value, axis, [(source, source ^ mask) for source in range(count)])


def section_shift(value, flip):
    sections, cores = lax.axis_size("section"), lax.axis_size("dp")
    pairs = []
    for section in range(sections):
        for core in range(cores):
            target = ((section + 1) % sections) * cores + (core ^ flip)
            pairs.append((section * cores + core, target))
    return lax.ppermute(value, ("section", "dp"), pairs)


def dot(left, right, left_dim, right_dim):
    return lax.dot_general(
        left, right, (((left_dim,), (right_dim,)), ((), ())), preferred_element_type=F32
    )


VMEM = pl.BlockSpec(memory_space=pltpu.VMEM)
HBM = pl.BlockSpec(memory_space=pltpu.HBM)
AFTER = pl.BlockSpec(memory_space=pl.ANY)


def call(kernel, out_shape, in_specs, out_specs, scratch, grid=(), weight=1, aliases={}):
    return pl.pallas_call(
        kernel,
        out_shape=out_shape,
        grid=grid,
        in_specs=in_specs,
        out_specs=out_specs,
        scratch_shapes=scratch,
        input_output_aliases=aliases,
        compiler_params=pltpu.CompilerParams(vmem_limit_bytes=VMEM_LIMIT),
        cost_estimate=pl.CostEstimate(
            flops=weight * COST, bytes_accessed=1, transcendentals=0
        ),
    )


def array(*shape):
    return jax.ShapeDtypeStruct(shape, BF16)


def in_vmem(value):
    return pltpu.with_memory_space_constraint(value, pltpu.VMEM)


def in_hbm(value):
    return pltpu.with_memory_space_constraint(value, pltpu.HBM)


def halves(value_ref, own_ref, other_ref, sems, first):
    tokens, width = value_ref.shape[0], value_ref.shape[1] // 2
    core = lax.axis_index("dp")
    copies = []
    for place, (half, target) in enumerate(((core, own_ref), (1 - core, other_ref))):
        columns = pl.ds(pl.multiple_of(half * width, 128), width)
        copies.append(
            pltpu.make_async_copy(
                value_ref.at[:, columns], target.at[0:tokens], sems.at[first + place]
            )
        )
    for copy in copies:
        copy.start()
    return copies


def pack_kernel(f_ref, *refs):
    sources, (own, other, packed, sems), held = refs[:4], refs[4:8], refs[8:]
    tokens = f_ref.shape[0]
    small = [
        pltpu.make_async_copy(source, target, sems.at[2 + place])
        for place, (source, target) in enumerate(zip(sources, held))
    ]
    for copy in small:
        copy.start()
    copies = halves(f_ref, own, other, sems, 0)
    packed[...] = jnp.zeros_like(packed)
    for copy in small:
        copy.wait()
    for start, ids, route in ((0, *held[:2]), (META // 2, *held[2:])):
        packed[start : start + 2, 0:tokens] = ids[...].astype(F32)
        rest = route[...]
        for piece in range(3):
            top = rest.astype(BF16).astype(F32)
            row = start + 2 + 2 * piece
            packed[row : row + 2, 0:tokens] = top
            rest = rest - top
    mine = packed[...]
    lanes = packed.shape[1]
    own[tokens : tokens + META, 0:lanes] = mine.astype(BF16)
    other[tokens : tokens + META, 0:lanes] = pltpu.roll(mine, tokens, 1).astype(BF16)
    for copy in copies:
        copy.wait()


def pack(f, *small):
    tokens, width = f.shape[0], f.shape[1] // 2
    return call(
        pack_kernel,
        [array(tokens + META, width)] * 2,
        [HBM] * 5,
        [VMEM] * 2,
        [pltpu.VMEM((META, 2 * tokens), F32), pltpu.SemaphoreType.DMA((6,))]
        + [pltpu.VMEM(value.shape, value.dtype) for value in small],
    )(f, *small)


def cut_kernel(x_ref, dy_ref, *refs):
    own_x, own_dy, other, sems = refs[-4:]
    tokens = x_ref.shape[0]
    copies = halves(x_ref, own_x, other.at[0:tokens], sems, 0)
    copies += halves(dy_ref, own_dy, other.at[tokens : 2 * tokens], sems, 2)
    for copy in copies:
        copy.wait()


def cut(x, dy, after):
    tokens, width = x.shape[0], x.shape[1] // 2
    return call(
        cut_kernel,
        [array(tokens, width)] * 2 + [array(2 * tokens, width)],
        [HBM] * 2 + [AFTER] * len(after),
        [VMEM] * 3,
        [pltpu.SemaphoreType.DMA((4,))],
    )(x, dy, *after)


def load_kernel(*refs, count):
    sources, targets, sems = refs[:count], refs[-count - 1 : -1], refs[-1]
    copies = [
        pltpu.make_async_copy(source, target, sems.at[place])
        for place, (source, target) in enumerate(zip(sources, targets))
    ]
    for copy in copies:
        copy.start()
    for copy in copies:
        copy.wait()


def load(weights, after):
    return call(
        functools.partial(load_kernel, count=len(weights)),
        [array(*weight.shape) for weight in weights],
        [HBM] * len(weights) + [AFTER] * len(after),
        [VMEM] * len(weights),
        [pltpu.SemaphoreType.DMA((len(weights),))],
    )(*weights, *after)


class Plan:
    def __init__(self, blocks, part, group, tokens, relative):
        self.blocks, self.part, self.group = blocks, part, group
        self.tokens, self.relative = tokens, relative


def slot_rows(own_meta, other_meta, plan, first_row):
    lanes = 2 * plan.tokens
    padded = max(8, plan.blocks)
    me = lax.axis_index("expert") if plan.relative else 0
    meta = own_meta[plan.tokens : plan.tokens + META, 0:lanes].astype(F32)
    meta = meta + other_meta[plan.tokens : plan.tokens + META, 0:lanes].astype(F32)
    meta = meta[first_row : first_row + META // 2]
    first, second = meta[0:1], meta[1:2]
    route = meta[2:4] + meta[4:6] + meta[6:8]
    row = lax.broadcasted_iota(jnp.int32, (padded, lanes), 0)
    expert = ((row ^ me) // plan.group).astype(F32)
    is_first, is_second = expert == first, expert == second
    named = jnp.where(is_first | is_second, 1.0, 0.0)
    before = lax.broadcasted_iota(jnp.int32, (lanes, lanes), 0)
    after = lax.broadcasted_iota(jnp.int32, (lanes, lanes), 1)
    earlier = (before < after) & ((before < plan.tokens) == (after < plan.tokens))
    position = dot(named.astype(BF16), jnp.where(earlier, 1.0, 0.0).astype(BF16), 1, 0)
    lane = lax.broadcasted_iota(jnp.int32, (padded, lanes), 1)
    slot = position + jnp.where(lane < plan.tokens, 0, plan.part).astype(F32)
    slot = jnp.where(named > 0.5, slot, -1.0)
    return slot, jnp.where(is_first, route[0:1], route[1:2])


def slot_table(slot, block, first, rows):
    index = lax.broadcasted_iota(jnp.int32, (rows, slot.shape[1]), 0) + first
    index = index.astype(F32)
    return jnp.where(index == slot[block : block + 1, :], 1.0, 0.0)


def dispatch_kernel(
    own_meta, other_meta, own_ref, other_ref, *refs, plan, first_row, other_row, weighted, passed
):
    outs = refs[len(refs) - plan.blocks - passed : len(refs) - passed]
    width, tokens = outs[0].shape[1], plan.tokens
    slot, route = slot_rows(own_meta, other_meta, plan, first_row)
    values = jnp.concatenate([own_ref[0:tokens, :], other_ref[other_row : other_row + tokens, :]], axis=0)
    for block in range(plan.blocks):
        table = slot_table(slot, block, 0, 2 * plan.part)
        if weighted:
            scale = jnp.sum(table * route[block : block + 1, :], axis=1, keepdims=True)
        table = table.astype(BF16)
        for start in range(0, width, TILE):
            picked = dot(table, values[:, start : start + TILE], 1, 0)
            if weighted:
                picked = picked * scale
            outs[block][:, start : start + TILE] = picked.astype(BF16)


def dispatch(metas, own, other, plan, first_row, other_row, weighted, after=(), passing=()):
    width = own.shape[1]
    return call(
        functools.partial(
            dispatch_kernel,
            plan=plan,
            first_row=first_row,
            other_row=other_row,
            weighted=weighted,
            passed=len(passing),
        ),
        [array(2 * plan.part, width)] * plan.blocks + [array(*value.shape) for value in passing],
        [VMEM] * (4 + len(passing)) + [AFTER] * len(after),
        [VMEM] * (plan.blocks + len(passing)),
        [],
        aliases={4 + place: plan.blocks + place for place in range(len(passing))},
    )(*metas, own, other, *passing, *after)


def combine_kernel(own_meta, other_meta, *refs, plan, first_row, weighted, cores):
    returned, outs = refs[: plan.blocks], refs[-len(cores) :]
    width, tokens = outs[0].shape[1], plan.tokens
    slot, route = slot_rows(own_meta, other_meta, plan, first_row)
    table = []
    for block in range(plan.blocks):
        table.append(slot_table(slot, block, plan.part * cores[0], plan.part * len(cores)))
        if weighted:
            table[block] = table[block] * route[block : block + 1, :]
    table = jnp.concatenate(table, axis=0)
    high = table.astype(BF16)
    low = (table - high.astype(F32)).astype(BF16)
    for start in range(0, width, TILE):
        part = slice(start, start + TILE)
        values = jnp.concatenate([ref[:, part].astype(F32) for ref in returned], axis=0)
        values = values.astype(BF16)
        total = dot(high, values, 0, 0)
        if weighted:
            total += dot(low, values, 0, 0)
        for core, out in zip(cores, outs):
            out[:, part] = total[core * tokens : (core + 1) * tokens].astype(BF16)


def combine(metas, returned, plan, first_row, weighted, cores, after=(), weight=1):
    return call(
        functools.partial(
            combine_kernel, plan=plan, first_row=first_row, weighted=weighted, cores=cores
        ),
        [array(plan.tokens, returned[0].shape[1])] * len(cores),
        [VMEM] * (2 + plan.blocks) + [AFTER] * len(after),
        [VMEM] * len(cores),
        [],
        weight=weight,
    )(*metas, *returned, *after)


def joined(refs):
    return jnp.concatenate([ref[...] for ref in refs], axis=0)


def gate_up_kernel(*refs, blocks):
    gate_w, up_w = refs[blocks : blocks + 2]
    out, rows = refs[-2:]
    rows[...] = joined(refs[:blocks])
    for start in range(0, out.shape[2], TILE):
        part = slice(start, start + TILE)
        out[0, :, part] = dot(rows[...], gate_w[:, part], 1, 0).astype(BF16)
        out[1, :, part] = dot(rows[...], up_w[:, part], 1, 0).astype(BF16)


def gate_up(inputs, gate_w, up_w, planes=2, after=(), weight=1):
    blocks, (rows, width) = len(inputs), inputs[0].shape
    units, total = gate_w.shape[1], blocks * rows
    return call(
        functools.partial(gate_up_kernel, blocks=blocks),
        array(planes, total, units),
        [VMEM] * (blocks + 2) + [AFTER] * len(after),
        VMEM,
        [pltpu.VMEM((total, width), BF16)],
        weight=weight,
    )(*inputs, gate_w, up_w, *after)


def d_hidden_kernel(*refs, blocks):
    down_w = refs[blocks]
    rows, out = refs[-2:]
    rows[...] = joined(refs[:blocks])
    for start in range(0, out.shape[2], TILE):
        part = slice(start, start + TILE)
        out[2, :, part] = dot(rows[...], down_w[part, :], 1, 1).astype(BF16)


def d_hidden(inputs, down_w, partial, after=(), weight=1):
    blocks, (rows, width) = len(inputs), inputs[0].shape
    return call(
        functools.partial(d_hidden_kernel, blocks=blocks),
        [array(blocks * rows, width), array(*partial.shape)],
        [VMEM] * (blocks + 2) + [AFTER] * len(after),
        [VMEM] * 2,
        [],
        weight=weight,
        aliases={blocks + 1: 1},
    )(*inputs, down_w, partial, *after)


def scatter_tile(value, outs, columns, blocks):
    pieces, rows = len(outs) // blocks, outs[0].shape[0]
    for place, out in enumerate(outs):
        first = (pieces * (place % blocks) + place // blocks) * rows
        out[:, columns] = value[first : first + rows].astype(BF16)


def total_of(own, other, part):
    own, other = own.astype(F32), other.astype(F32)
    rows = own.shape[0]
    turned = []
    for first in range(0, rows, 2 * part):
        turned += [other[first + part : first + 2 * part], other[first : first + part]]
    return own + jnp.concatenate(turned, axis=0)


def down_kernel(own_ref, other_ref, down_w, *refs, blocks):
    outs, hidden = refs[-1 - blocks : -1], refs[-1]
    part = outs[0].shape[0] // 2
    for start in range(0, hidden.shape[1], TILE):
        columns = slice(start, start + TILE)
        gate = total_of(own_ref[0, :, columns], other_ref[0, :, columns], part)
        up = total_of(own_ref[1, :, columns], other_ref[1, :, columns], part)
        hidden[:, columns] = (gate * jax.nn.sigmoid(gate) * up).astype(BF16)
    for start in range(0, outs[0].shape[1], TILE):
        columns = slice(start, start + TILE)
        scatter_tile(dot(hidden[...], down_w[:, columns], 1, 0), outs, columns, blocks)


def down(own, other, down_w, plan, after=()):
    _, total, units = own.shape
    return call(
        functools.partial(down_kernel, blocks=plan.blocks),
        [array(2 * plan.part, down_w.shape[1])] * plan.blocks,
        [VMEM] * 3 + [AFTER] * len(after),
        [VMEM] * plan.blocks,
        [pltpu.VMEM((total, units), BF16)],
    )(own, other, down_w, *after)


def back_kernel(own_ref, other_ref, gate_w, up_w, *refs, blocks):
    hidden, d_gate, d_up, *outs = refs[-3 - 2 * blocks :]
    part = outs[0].shape[0]
    for start in range(0, hidden.shape[1], TILE):
        columns = slice(start, start + TILE)
        gate = total_of(own_ref[0, :, columns], other_ref[0, :, columns], part)
        up = total_of(own_ref[1, :, columns], other_ref[1, :, columns], part)
        d_hid = total_of(own_ref[2, :, columns], other_ref[2, :, columns], part)
        sigmoid = jax.nn.sigmoid(gate)
        activated = gate * sigmoid
        hidden[:, columns] = (activated * up).astype(BF16)
        d_up[:, columns] = (d_hid * activated).astype(BF16)
        d_gate[:, columns] = (
            d_hid * up * sigmoid * (1.0 + gate * (1.0 - sigmoid))
        ).astype(BF16)
    for start in range(0, outs[0].shape[1], TILE):
        columns = slice(start, start + TILE)
        total = dot(d_gate[...], gate_w[columns, :], 1, 1)
        total += dot(d_up[...], up_w[columns, :], 1, 1)
        scatter_tile(total, outs, columns, blocks)


def back(own, other, gate_w, up_w, plan, after=()):
    _, total, units = own.shape
    return call(
        functools.partial(back_kernel, blocks=plan.blocks),
        [array(total, units)] * 3 + [array(plan.part, gate_w.shape[0])] * (2 * plan.blocks),
        [VMEM] * 4 + [AFTER] * len(after),
        [VMEM] * (3 + 2 * plan.blocks),
        [],
    )(own, other, gate_w, up_w, *after)


def turn_kernel(*refs, blocks):
    inputs, turned = refs[:blocks], refs[-1]
    for start in range(0, turned.shape[0], TILE):
        part = slice(start, start + TILE)
        turned[part, :] = jnp.concatenate([ref[:, part] for ref in inputs], axis=0).T


def turn(inputs, after=()):
    blocks, (rows, width) = len(inputs), inputs[0].shape
    return call(
        functools.partial(turn_kernel, blocks=blocks),
        array(width, blocks * rows),
        [VMEM] * blocks + [AFTER] * len(after),
        VMEM,
        [],
    )(*inputs, *after)


def grad_kernel(hidden, d_gate, d_up, turned, cots, *refs):
    grad_gate, grad_up, grad_down = refs[-3:]
    part = pl.ds(pl.multiple_of(pl.program_id(0) * TILE, TILE), TILE)
    grad_gate[...] = dot(turned[...], d_gate[:, part], 1, 0).astype(BF16)
    grad_up[...] = dot(turned[...], d_up[:, part], 1, 0).astype(BF16)
    grad_down[...] = dot(hidden[:, part], cots[...], 0, 0).astype(BF16)


def grads(hidden, d_gate, d_up, turned, cots, after=(), weight=1):
    width, units = turned.shape[0], d_gate.shape[1]
    by_column = pl.BlockSpec((width, TILE), lambda i: (0, i))
    return call(
        grad_kernel,
        [pltpu.HBM((width, units), BF16)] * 2 + [pltpu.HBM((units, width), BF16)],
        [VMEM] * 5 + [AFTER] * len(after),
        [by_column, by_column, pl.BlockSpec((TILE, width), lambda i: (i, 0))],
        [],
        grid=(units // TILE,),
        weight=weight,
    )(hidden, d_gate, d_up, turned, cots, *after)


def arrived_kernel(*refs):
    refs[-1][...] = jnp.zeros_like(refs[-1])


def arrived(values, after=(), weight=1):
    return call(
        arrived_kernel,
        array(16, 128),
        [AFTER] * (len(values) + len(after)),
        VMEM,
        [],
        weight=weight,
    )(*[in_vmem(value) for value in values], *after)


def to_experts(blocks, relative):
    if not relative:
        stacked = lax.all_to_all(jnp.stack(blocks), "expert", split_axis=0, concat_axis=0)
        return [stacked[block] for block in range(len(blocks))]
    return [blocks[0]] + [
        exchange(block, "expert", mask) for mask, block in enumerate(blocks) if mask > 0
    ]


def finish_kernel(*refs):
    sources, outs, sems = refs[:4], refs[-3:-1], refs[-1]
    width = sources[0].shape[1]
    core = lax.axis_index("dp")
    copies = []
    for place, source in enumerate(sources):
        half = core if place % 2 == 0 else 1 - core
        columns = pl.ds(pl.multiple_of(half * width, 128), width)
        copies.append(
            pltpu.make_async_copy(source, outs[place // 2].at[:, columns], sems.at[place])
        )
    for copy in copies:
        copy.start()
    for copy in copies:
        copy.wait()


def finish(y_mine, y_rest, dx_mine, dx_rest, after):
    tokens, width = y_mine.shape
    return call(
        finish_kernel,
        [pltpu.HBM((tokens, 2 * width), BF16)] * 2,
        [VMEM] * 4 + [AFTER] * len(after),
        [HBM] * 2,
        [pltpu.SemaphoreType.DMA((4,))],
    )(y_mine, y_rest, dx_mine, dx_rest, *after)


def local(x_fwd, ids_fwd, route_fwd, x_bwd, ids_bwd, route_bwd, dy_bwd, w_gate, w_up, w_down):
    n_expert = lax.axis_size("expert")
    slab_width = w_gate.shape[-1]
    group = FF // slab_width
    experts = n_expert // group
    tokens = x_fwd.shape[1]
    spread = 4 * experts * group
    capacity = group * ((5 * tokens * TOP + spread - 1) // spread)
    relative = n_expert <= 8
    plan = Plan(n_expert, (capacity + 7) // 8 * 8, group, tokens, relative)
    row_b, row_f = 0, META // 2

    own_f, send_f = pack(
        in_hbm(x_fwd[0]),
        *[in_hbm(value[0].T) for value in (ids_bwd, route_bwd, ids_fwd, route_fwd)],
    )
    other_f = exchange(send_f, "dp", 1)
    own_x, own_dy, send_rest = cut(in_hbm(x_bwd[0]), in_hbm(dy_bwd[0]), after=(own_f,))
    metas = (own_f, other_f)
    *sent_f, send_rest = dispatch(
        metas, own_f, other_f, plan, row_f, 0, False, passing=(send_rest,)
    )
    rows_f = to_experts(sent_f, relative)
    other_rest = exchange(send_rest, "dp", 1)
    sent_x = dispatch(metas, own_x, other_rest, plan, row_b, 0, False)
    rows_b = to_experts(sent_x, relative)
    gate_w, up_w, down_w = load(
        [in_hbm(weight[0, 0]) for weight in (w_gate, w_up, w_down)], after=sent_x[:1]
    )
    sent_dy = dispatch(
        metas, own_dy, other_rest, plan, row_b, tokens, True, after=(in_vmem(down_w),)
    )
    cots_b = to_experts(sent_dy, relative)

    part_f = gate_up(rows_f, gate_w, up_w, after=sent_dy[:1])
    part_f_other = exchange(part_f, "dp", 1)
    part_b = gate_up(rows_b, gate_w, up_w, planes=3, after=(part_f,), weight=3000)
    down_blocks = down(part_f, part_f_other, down_w, plan, after=(in_vmem(part_b),))
    back_f = to_experts(down_blocks, relative)
    turned = turn(rows_b, after=down_blocks[:1])
    cots, part_b = d_hidden(cots_b, down_w, part_b, after=(in_vmem(turned),), weight=1000)
    part_b_other = exchange(part_b, "dp", 1)
    near = arrived(back_f[1:3], after=(in_vmem(part_b),), weight=2000)
    hidden, d_gate, d_up, *back_blocks = back(
        part_b, part_b_other, gate_w, up_w, plan, after=(near,)
    )
    own_back_b = to_experts(back_blocks[:n_expert], relative)
    other_back_b = to_experts(back_blocks[n_expert:], relative)
    own_sum, other_sum = combine(
        metas, back_f, plan, row_f, True, (0, 1), after=back_blocks[:1], weight=150
    )
    y_mine, y_rest = section_shift(own_sum, 0), section_shift(other_sum, 1)
    (own_sum,) = combine(
        metas, own_back_b, plan, row_b, False, (0,), after=(other_sum,), weight=150
    )
    dx_mine = section_shift(own_sum, 0)
    (other_sum,) = combine(
        metas,
        other_back_b,
        plan,
        row_b,
        False,
        (1,),
        after=(own_sum, in_vmem(y_mine), in_vmem(y_rest)),
        weight=100,
    )
    dx_rest = section_shift(other_sum, 1)
    grad_g, grad_u, grad_d = grads(
        hidden,
        d_gate,
        d_up,
        turned,
        cots,
        after=(other_sum, in_vmem(y_rest), in_vmem(dx_mine)),
        weight=100,
    )
    y_next, dx_next = finish(y_mine, y_rest, dx_mine, dx_rest, after=(in_hbm(grad_g),))
    return (
        y_next[None],
        dx_next[None],
        grad_g[None, None],
        grad_u[None, None],
        grad_d[None, None],
    )


def solution(mesh):
    rows = P("section", ("expert", "dp"), None)
    by_feature = P("section", "expert", "dp", None)
    down_spec = P("section", "expert", None, "dp")
    return jax.shard_map(
        local,
        mesh=mesh,
        in_specs=(rows,) * 7 + (by_feature, by_feature, down_spec),
        out_specs=(rows, rows, by_feature, by_feature, down_spec),
        check_vma=False,
    )
```

```python
import functools

import jax
import jax.numpy as jnp
from jax import lax
from jax.experimental import pallas as pl
from jax.experimental.pallas import tpu as pltpu
from jax.sharding import PartitionSpec as P

FF = 1024
TOP = 2
TILE = 256
VMEM_LIMIT = 20 * 1024 * 1024
META = 16
COST = 10**7
F32 = jnp.float32
BF16 = jnp.bfloat16


def exchange(value, axis, mask):
    count = lax.axis_size(axis)
    return lax.ppermute(value, axis, [(source, source ^ mask) for source in range(count)])


def section_shift(value, flip):
    sections, cores = lax.axis_size("section"), lax.axis_size("dp")
    pairs = []
    for section in range(sections):
        for core in range(cores):
            target = ((section + 1) % sections) * cores + (core ^ flip)
            pairs.append((section * cores + core, target))
    return lax.ppermute(value, ("section", "dp"), pairs)


def dot(left, right, left_dim, right_dim):
    return lax.dot_general(
        left, right, (((left_dim,), (right_dim,)), ((), ())), preferred_element_type=F32
    )


VMEM = pl.BlockSpec(memory_space=pltpu.VMEM)
HBM = pl.BlockSpec(memory_space=pltpu.HBM)
AFTER = pl.BlockSpec(memory_space=pl.ANY)


def call(kernel, out_shape, in_specs, out_specs, scratch, grid=(), weight=1, aliases={}):
    return pl.pallas_call(
        kernel,
        out_shape=out_shape,
        grid=grid,
        in_specs=in_specs,
        out_specs=out_specs,
        scratch_shapes=scratch,
        input_output_aliases=aliases,
        compiler_params=pltpu.CompilerParams(vmem_limit_bytes=VMEM_LIMIT),
        cost_estimate=pl.CostEstimate(
            flops=weight * COST, bytes_accessed=1, transcendentals=0
        ),
    )


def array(*shape):
    return jax.ShapeDtypeStruct(shape, BF16)


def in_vmem(value):
    return pltpu.with_memory_space_constraint(value, pltpu.VMEM)


def in_hbm(value):
    return pltpu.with_memory_space_constraint(value, pltpu.HBM)


def halves(value_ref, own_ref, other_ref, sems, first):
    tokens, width = value_ref.shape[0], value_ref.shape[1] // 2
    core = lax.axis_index("dp")
    copies = []
    for place, (half, target) in enumerate(((core, own_ref), (1 - core, other_ref))):
        columns = pl.ds(pl.multiple_of(half * width, 128), width)
        copies.append(
            pltpu.make_async_copy(
                value_ref.at[:, columns], target.at[0:tokens], sems.at[first + place]
            )
        )
    for copy in copies:
        copy.start()
    return copies


def pack_kernel(f_ref, *refs):
    sources, (own, other, packed, sems), held = refs[:4], refs[4:8], refs[8:]
    tokens = f_ref.shape[0]
    small = [
        pltpu.make_async_copy(source, target, sems.at[2 + place])
        for place, (source, target) in enumerate(zip(sources, held))
    ]
    for copy in small:
        copy.start()
    copies = halves(f_ref, own, other, sems, 0)
    packed[...] = jnp.zeros_like(packed)
    for copy in small:
        copy.wait()
    for start, ids, route in ((0, *held[:2]), (META // 2, *held[2:])):
        packed[start : start + 2, 0:tokens] = ids[...].astype(F32)
        rest = route[...]
        for piece in range(3):
            top = rest.astype(BF16).astype(F32)
            row = start + 2 + 2 * piece
            packed[row : row + 2, 0:tokens] = top
            rest = rest - top
    mine = packed[...]
    lanes = packed.shape[1]
    own[tokens : tokens + META, 0:lanes] = mine.astype(BF16)
    other[tokens : tokens + META, 0:lanes] = pltpu.roll(mine, tokens, 1).astype(BF16)
    for copy in copies:
        copy.wait()


def pack(f, *small):
    tokens, width = f.shape[0], f.shape[1] // 2
    return call(
        pack_kernel,
        [array(tokens + META, width)] * 2,
        [HBM] * 5,
        [VMEM] * 2,
        [pltpu.VMEM((META, 2 * tokens), F32), pltpu.SemaphoreType.DMA((6,))]
        + [pltpu.VMEM(value.shape, value.dtype) for value in small],
    )(f, *small)


def cut_kernel(x_ref, dy_ref, *refs):
    own_x, own_dy, other, sems = refs[-4:]
    tokens = x_ref.shape[0]
    copies = halves(x_ref, own_x, other.at[0:tokens], sems, 0)
    copies += halves(dy_ref, own_dy, other.at[tokens : 2 * tokens], sems, 2)
    for copy in copies:
        copy.wait()


def cut(x, dy, after):
    tokens, width = x.shape[0], x.shape[1] // 2
    return call(
        cut_kernel,
        [array(tokens, width)] * 2 + [array(2 * tokens, width)],
        [HBM] * 2 + [AFTER] * len(after),
        [VMEM] * 3,
        [pltpu.SemaphoreType.DMA((4,))],
    )(x, dy, *after)


def load_kernel(*refs, count):
    sources, targets, sems = refs[:count], refs[-count - 1 : -1], refs[-1]
    copies = [
        pltpu.make_async_copy(source, target, sems.at[place])
        for place, (source, target) in enumerate(zip(sources, targets))
    ]
    for copy in copies:
        copy.start()
    for copy in copies:
        copy.wait()


def load(weights, after):
    return call(
        functools.partial(load_kernel, count=len(weights)),
        [array(*weight.shape) for weight in weights],
        [HBM] * len(weights) + [AFTER] * len(after),
        [VMEM] * len(weights),
        [pltpu.SemaphoreType.DMA((len(weights),))],
    )(*weights, *after)


class Plan:
    def __init__(self, blocks, part, group, tokens, relative):
        self.blocks, self.part, self.group = blocks, part, group
        self.tokens, self.relative = tokens, relative


def slot_rows(own_meta, other_meta, plan, first_row):
    lanes = 2 * plan.tokens
    padded = max(8, plan.blocks)
    me = lax.axis_index("expert") if plan.relative else 0
    meta = own_meta[plan.tokens : plan.tokens + META, 0:lanes].astype(F32)
    meta = meta + other_meta[plan.tokens : plan.tokens + META, 0:lanes].astype(F32)
    meta = meta[first_row : first_row + META // 2]
    first, second = meta[0:1], meta[1:2]
    route = meta[2:4] + meta[4:6] + meta[6:8]
    row = lax.broadcasted_iota(jnp.int32, (padded, lanes), 0)
    expert = ((row ^ me) // plan.group).astype(F32)
    is_first, is_second = expert == first, expert == second
    named = jnp.where(is_first | is_second, 1.0, 0.0)
    before = lax.broadcasted_iota(jnp.int32, (lanes, lanes), 0)
    after = lax.broadcasted_iota(jnp.int32, (lanes, lanes), 1)
    earlier = (before < after) & ((before < plan.tokens) == (after < plan.tokens))
    position = dot(named.astype(BF16), jnp.where(earlier, 1.0, 0.0).astype(BF16), 1, 0)
    lane = lax.broadcasted_iota(jnp.int32, (padded, lanes), 1)
    slot = position + jnp.where(lane < plan.tokens, 0, plan.part).astype(F32)
    slot = jnp.where(named > 0.5, slot, -1.0)
    return slot, jnp.where(is_first, route[0:1], route[1:2])


def slot_table(slot, block, first, rows):
    index = lax.broadcasted_iota(jnp.int32, (rows, slot.shape[1]), 0) + first
    index = index.astype(F32)
    return jnp.where(index == slot[block : block + 1, :], 1.0, 0.0)


def dispatch_kernel(
    own_meta, other_meta, own_ref, other_ref, *refs, plan, first_row, other_row, weighted, passed
):
    outs = refs[len(refs) - plan.blocks - passed : len(refs) - passed]
    width, tokens = outs[0].shape[1], plan.tokens
    slot, route = slot_rows(own_meta, other_meta, plan, first_row)
    values = jnp.concatenate([own_ref[0:tokens, :], other_ref[other_row : other_row + tokens, :]], axis=0)
    for block in range(plan.blocks):
        table = slot_table(slot, block, 0, 2 * plan.part)
        if weighted:
            scale = jnp.sum(table * route[block : block + 1, :], axis=1, keepdims=True)
        table = table.astype(BF16)
        for start in range(0, width, TILE):
            picked = dot(table, values[:, start : start + TILE], 1, 0)
            if weighted:
                picked = picked * scale
            outs[block][:, start : start + TILE] = picked.astype(BF16)


def dispatch(metas, own, other, plan, first_row, other_row, weighted, after=(), passing=()):
    width = own.shape[1]
    return call(
        functools.partial(
            dispatch_kernel,
            plan=plan,
            first_row=first_row,
            other_row=other_row,
            weighted=weighted,
            passed=len(passing),
        ),
        [array(2 * plan.part, width)] * plan.blocks + [array(*value.shape) for value in passing],
        [VMEM] * (4 + len(passing)) + [AFTER] * len(after),
        [VMEM] * (plan.blocks + len(passing)),
        [],
        aliases={4 + place: plan.blocks + place for place in range(len(passing))},
    )(*metas, own, other, *passing, *after)


def combine_kernel(own_meta, other_meta, *refs, plan, first_row, weighted, other):
    returned, out = refs[: plan.blocks], refs[-1]
    width, tokens = out.shape[1], plan.tokens
    slot, route = slot_rows(own_meta, other_meta, plan, first_row)
    table = []
    for block in range(plan.blocks):
        table.append(slot_table(slot, block, plan.part if other else 0, plan.part))
        if weighted:
            table[block] = table[block] * route[block : block + 1, :]
    table = jnp.concatenate(table, axis=0)
    high = table.astype(BF16)
    low = (table - high.astype(F32)).astype(BF16)
    for start in range(0, width, TILE):
        part = slice(start, start + TILE)
        values = jnp.concatenate([ref[:, part].astype(F32) for ref in returned], axis=0)
        values = values.astype(BF16)
        total = dot(high, values, 0, 0)
        if weighted:
            total += dot(low, values, 0, 0)
        out[:, part] = total[tokens if other else 0 :][:tokens].astype(BF16)


def combine(metas, returned, plan, first_row, weighted, other, after=(), weight=1):
    return call(
        functools.partial(
            combine_kernel, plan=plan, first_row=first_row, weighted=weighted, other=other
        ),
        array(plan.tokens, returned[0].shape[1]),
        [VMEM] * (2 + plan.blocks) + [AFTER] * len(after),
        VMEM,
        [],
        weight=weight,
    )(*metas, *returned, *after)


def joined(refs):
    return jnp.concatenate([ref[...] for ref in refs], axis=0)


def gate_up_kernel(*refs, blocks):
    gate_w, up_w = refs[blocks : blocks + 2]
    out, rows = refs[-2:]
    rows[...] = joined(refs[:blocks])
    for start in range(0, out.shape[2], TILE):
        part = slice(start, start + TILE)
        out[0, :, part] = dot(rows[...], gate_w[:, part], 1, 0).astype(BF16)
        out[1, :, part] = dot(rows[...], up_w[:, part], 1, 0).astype(BF16)


def gate_up(inputs, gate_w, up_w, planes=2, after=(), weight=1):
    blocks, (rows, width) = len(inputs), inputs[0].shape
    units, total = gate_w.shape[1], blocks * rows
    return call(
        functools.partial(gate_up_kernel, blocks=blocks),
        array(planes, total, units),
        [VMEM] * (blocks + 2) + [AFTER] * len(after),
        VMEM,
        [pltpu.VMEM((total, width), BF16)],
        weight=weight,
    )(*inputs, gate_w, up_w, *after)


def d_hidden_kernel(*refs, blocks):
    down_w = refs[blocks]
    rows, out = refs[-2:]
    rows[...] = joined(refs[:blocks])
    for start in range(0, out.shape[2], TILE):
        part = slice(start, start + TILE)
        out[2, :, part] = dot(rows[...], down_w[part, :], 1, 1).astype(BF16)


def d_hidden(inputs, down_w, partial, after=(), weight=1):
    blocks, (rows, width) = len(inputs), inputs[0].shape
    return call(
        functools.partial(d_hidden_kernel, blocks=blocks),
        [array(blocks * rows, width), array(*partial.shape)],
        [VMEM] * (blocks + 2) + [AFTER] * len(after),
        [VMEM] * 2,
        [],
        weight=weight,
        aliases={blocks + 1: 1},
    )(*inputs, down_w, partial, *after)


def scatter_tile(value, outs, columns):
    blocks, part = len(outs) // 2, outs[0].shape[0]
    for place, out in enumerate(outs):
        first = (2 * (place % blocks) + place // blocks) * part
        out[:, columns] = value[first : first + part].astype(BF16)


def total_of(own, other, part):
    own, other = own.astype(F32), other.astype(F32)
    rows = own.shape[0]
    turned = []
    for first in range(0, rows, 2 * part):
        turned += [other[first + part : first + 2 * part], other[first : first + part]]
    return own + jnp.concatenate(turned, axis=0)


def down_kernel(own_ref, other_ref, down_w, *refs, blocks):
    outs, hidden = refs[-1 - 2 * blocks : -1], refs[-1]
    part = outs[0].shape[0]
    for start in range(0, hidden.shape[1], TILE):
        columns = slice(start, start + TILE)
        gate = total_of(own_ref[0, :, columns], other_ref[0, :, columns], part)
        up = total_of(own_ref[1, :, columns], other_ref[1, :, columns], part)
        hidden[:, columns] = (gate * jax.nn.sigmoid(gate) * up).astype(BF16)
    for start in range(0, outs[0].shape[1], TILE):
        columns = slice(start, start + TILE)
        scatter_tile(dot(hidden[...], down_w[:, columns], 1, 0), outs, columns)


def down(own, other, down_w, plan, after=()):
    _, total, units = own.shape
    return call(
        functools.partial(down_kernel, blocks=plan.blocks),
        [array(plan.part, down_w.shape[1])] * (2 * plan.blocks),
        [VMEM] * 3 + [AFTER] * len(after),
        [VMEM] * (2 * plan.blocks),
        [pltpu.VMEM((total, units), BF16)],
    )(own, other, down_w, *after)


def back_kernel(own_ref, other_ref, gate_w, up_w, *refs, blocks):
    hidden, d_gate, d_up, *outs = refs[-3 - 2 * blocks :]
    part = outs[0].shape[0]
    for start in range(0, hidden.shape[1], TILE):
        columns = slice(start, start + TILE)
        gate = total_of(own_ref[0, :, columns], other_ref[0, :, columns], part)
        up = total_of(own_ref[1, :, columns], other_ref[1, :, columns], part)
        d_hid = total_of(own_ref[2, :, columns], other_ref[2, :, columns], part)
        sigmoid = jax.nn.sigmoid(gate)
        activated = gate * sigmoid
        hidden[:, columns] = (activated * up).astype(BF16)
        d_up[:, columns] = (d_hid * activated).astype(BF16)
        d_gate[:, columns] = (
            d_hid * up * sigmoid * (1.0 + gate * (1.0 - sigmoid))
        ).astype(BF16)
    for start in range(0, outs[0].shape[1], TILE):
        columns = slice(start, start + TILE)
        total = dot(d_gate[...], gate_w[columns, :], 1, 1)
        total += dot(d_up[...], up_w[columns, :], 1, 1)
        scatter_tile(total, outs, columns)


def back(own, other, gate_w, up_w, plan, after=()):
    _, total, units = own.shape
    return call(
        functools.partial(back_kernel, blocks=plan.blocks),
        [array(total, units)] * 3 + [array(plan.part, gate_w.shape[0])] * (2 * plan.blocks),
        [VMEM] * 4 + [AFTER] * len(after),
        [VMEM] * (3 + 2 * plan.blocks),
        [],
    )(own, other, gate_w, up_w, *after)


def turn_kernel(*refs, blocks):
    inputs, turned = refs[:blocks], refs[-1]
    for start in range(0, turned.shape[0], TILE):
        part = slice(start, start + TILE)
        turned[part, :] = jnp.concatenate([ref[:, part] for ref in inputs], axis=0).T


def turn(inputs, after=()):
    blocks, (rows, width) = len(inputs), inputs[0].shape
    return call(
        functools.partial(turn_kernel, blocks=blocks),
        array(width, blocks * rows),
        [VMEM] * blocks + [AFTER] * len(after),
        VMEM,
        [],
    )(*inputs, *after)


def grad_in_kernel(d_gate, d_up, turned, *refs):
    grad_gate, grad_up = refs[-2:]
    part = pl.ds(pl.multiple_of(pl.program_id(0) * TILE, TILE), TILE)
    grad_gate[...] = dot(turned[...], d_gate[:, part], 1, 0).astype(BF16)
    grad_up[...] = dot(turned[...], d_up[:, part], 1, 0).astype(BF16)


def grad_in(d_gate, d_up, turned, after=(), weight=1):
    width, units = turned.shape[0], d_gate.shape[1]
    return call(
        grad_in_kernel,
        [pltpu.HBM((width, units), BF16)] * 2,
        [VMEM] * 3 + [AFTER] * len(after),
        [pl.BlockSpec((width, TILE), lambda i: (0, i))] * 2,
        [],
        grid=(units // TILE,),
        weight=weight,
    )(d_gate, d_up, turned, *after)


def grad_down_kernel(hidden, cots, *refs):
    part = pl.ds(pl.multiple_of(pl.program_id(0) * TILE, TILE), TILE)
    refs[-1][...] = dot(hidden[:, part], cots[...], 0, 0).astype(BF16)


def grad_down(hidden, cots, after=(), weight=1):
    units, width = hidden.shape[1], cots.shape[1]
    return call(
        grad_down_kernel,
        pltpu.HBM((units, width), BF16),
        [VMEM] * 2 + [AFTER] * len(after),
        pl.BlockSpec((TILE, width), lambda i: (i, 0)),
        [],
        grid=(units // TILE,),
        weight=weight,
    )(hidden, cots, *after)


def to_experts(blocks, relative):
    if not relative:
        stacked = lax.all_to_all(jnp.stack(blocks), "expert", split_axis=0, concat_axis=0)
        return [stacked[block] for block in range(len(blocks))]
    return [blocks[0]] + [
        exchange(block, "expert", mask) for mask, block in enumerate(blocks) if mask > 0
    ]


def finish_kernel(*refs):
    sources, outs, sems = refs[:4], refs[-3:-1], refs[-1]
    width = sources[0].shape[1]
    core = lax.axis_index("dp")
    copies = []
    for place, source in enumerate(sources):
        half = core if place % 2 == 0 else 1 - core
        columns = pl.ds(pl.multiple_of(half * width, 128), width)
        copies.append(
            pltpu.make_async_copy(source, outs[place // 2].at[:, columns], sems.at[place])
        )
    for copy in copies:
        copy.start()
    for copy in copies:
        copy.wait()


def finish(y_mine, y_rest, dx_mine, dx_rest, after):
    tokens, width = y_mine.shape
    return call(
        finish_kernel,
        [pltpu.HBM((tokens, 2 * width), BF16)] * 2,
        [VMEM] * 4 + [AFTER] * len(after),
        [HBM] * 2,
        [pltpu.SemaphoreType.DMA((4,))],
    )(y_mine, y_rest, dx_mine, dx_rest, *after)


def local(x_fwd, ids_fwd, route_fwd, x_bwd, ids_bwd, route_bwd, dy_bwd, w_gate, w_up, w_down):
    n_expert = lax.axis_size("expert")
    slab_width = w_gate.shape[-1]
    group = FF // slab_width
    experts = n_expert // group
    tokens = x_fwd.shape[1]
    spread = 4 * experts * group
    capacity = group * ((5 * tokens * TOP + spread - 1) // spread)
    relative = n_expert <= 8
    plan = Plan(n_expert, (capacity + 7) // 8 * 8, group, tokens, relative)
    row_b, row_f = 0, META // 2

    own_f, send_f = pack(
        in_hbm(x_fwd[0]),
        *[in_hbm(value[0].T) for value in (ids_bwd, route_bwd, ids_fwd, route_fwd)],
    )
    other_f = exchange(send_f, "dp", 1)
    own_x, own_dy, send_rest = cut(in_hbm(x_bwd[0]), in_hbm(dy_bwd[0]), after=(own_f,))
    metas = (own_f, other_f)
    *sent_f, send_rest = dispatch(
        metas, own_f, other_f, plan, row_f, 0, False, passing=(send_rest,)
    )
    rows_f = to_experts(sent_f, relative)
    other_rest = exchange(send_rest, "dp", 1)
    sent_x = dispatch(metas, own_x, other_rest, plan, row_b, 0, False)
    rows_b = to_experts(sent_x, relative)
    gate_w, up_w, down_w = load(
        [in_hbm(weight[0, 0]) for weight in (w_gate, w_up, w_down)], after=sent_x[:1]
    )
    sent_dy = dispatch(
        metas, own_dy, other_rest, plan, row_b, tokens, True, after=(in_vmem(down_w),)
    )
    cots_b = to_experts(sent_dy, relative)

    part_f = gate_up(rows_f, gate_w, up_w, after=sent_dy[:1])
    part_f_other = exchange(part_f, "dp", 1)
    part_b = gate_up(rows_b, gate_w, up_w, planes=3, after=(part_f,), weight=3000)
    down_blocks = down(part_f, part_f_other, down_w, plan, after=(in_vmem(part_b),))
    own_back_f = to_experts(down_blocks[:n_expert], relative)
    other_back_f = to_experts(down_blocks[n_expert:], relative)
    turned = turn(rows_b, after=down_blocks[:1])
    cots, part_b = d_hidden(cots_b, down_w, part_b, after=(in_vmem(turned),), weight=1000)
    part_b_other = exchange(part_b, "dp", 1)
    own_sum = combine(
        metas, own_back_f, plan, row_f, True, False, after=(in_vmem(part_b),), weight=2000
    )
    y_mine = section_shift(own_sum, 0)
    hidden, d_gate, d_up, *back_blocks = back(
        part_b, part_b_other, gate_w, up_w, plan, after=(own_sum,)
    )
    own_back_b = to_experts(back_blocks[:n_expert], relative)
    other_back_b = to_experts(back_blocks[n_expert:], relative)
    other_sum = combine(
        metas, other_back_f, plan, row_f, True, True, after=back_blocks[:1], weight=150
    )
    y_rest = section_shift(other_sum, 1)
    own_sum = combine(
        metas,
        own_back_b,
        plan,
        row_b,
        False,
        False,
        after=(other_sum, in_vmem(y_mine)),
        weight=150,
    )
    dx_mine = section_shift(own_sum, 0)
    grad_d = grad_down(hidden, cots, after=(own_sum,))
    other_sum = combine(
        metas,
        other_back_b,
        plan,
        row_b,
        False,
        True,
        after=(in_hbm(grad_d), in_vmem(y_rest)),
        weight=100,
    )
    dx_rest = section_shift(other_sum, 1)
    grad_g, grad_u = grad_in(
        d_gate, d_up, turned, after=(other_sum, in_vmem(dx_mine)), weight=100
    )
    y_next, dx_next = finish(y_mine, y_rest, dx_mine, dx_rest, after=(in_hbm(grad_g),))
    return (
        y_next[None],
        dx_next[None],
        grad_g[None, None],
        grad_u[None, None],
        grad_d[None, None],
    )


def solution(mesh):
    rows = P("section", ("expert", "dp"), None)
    by_feature = P("section", "expert", "dp", None)
    down_spec = P("section", "expert", None, "dp")
    return jax.shard_map(
        local,
        mesh=mesh,
        in_specs=(rows,) * 7 + (by_feature, by_feature, down_spec),
        out_specs=(rows, rows, by_feature, by_feature, down_spec),
        check_vma=False,
    )
```

```python
import functools

import jax
import jax.numpy as jnp
from jax import lax
from jax.experimental import pallas as pl
from jax.experimental.pallas import tpu as pltpu
from jax.sharding import PartitionSpec as P

FF = 1024
TOP = 2
TILE = 256
VMEM_LIMIT = 20 * 1024 * 1024
META = 16
COST = 10**7
F32 = jnp.float32
BF16 = jnp.bfloat16


def exchange(value, axis, mask):
    count = lax.axis_size(axis)
    return lax.ppermute(value, axis, [(source, source ^ mask) for source in range(count)])


def section_shift(value, flip):
    sections, cores = lax.axis_size("section"), lax.axis_size("dp")
    pairs = []
    for section in range(sections):
        for core in range(cores):
            target = ((section + 1) % sections) * cores + (core ^ flip)
            pairs.append((section * cores + core, target))
    return lax.ppermute(value, ("section", "dp"), pairs)


def dot(left, right, left_dim, right_dim):
    return lax.dot_general(
        left, right, (((left_dim,), (right_dim,)), ((), ())), preferred_element_type=F32
    )


VMEM = pl.BlockSpec(memory_space=pltpu.VMEM)
HBM = pl.BlockSpec(memory_space=pltpu.HBM)
AFTER = pl.BlockSpec(memory_space=pl.ANY)


def call(kernel, out_shape, in_specs, out_specs, scratch, grid=(), weight=1, aliases={}):
    return pl.pallas_call(
        kernel,
        out_shape=out_shape,
        grid=grid,
        in_specs=in_specs,
        out_specs=out_specs,
        scratch_shapes=scratch,
        input_output_aliases=aliases,
        compiler_params=pltpu.CompilerParams(vmem_limit_bytes=VMEM_LIMIT),
        cost_estimate=pl.CostEstimate(
            flops=weight * COST, bytes_accessed=1, transcendentals=0
        ),
    )


def array(*shape):
    return jax.ShapeDtypeStruct(shape, BF16)


def in_vmem(value):
    return pltpu.with_memory_space_constraint(value, pltpu.VMEM)


def in_hbm(value):
    return pltpu.with_memory_space_constraint(value, pltpu.HBM)


def halves(value_ref, own_ref, other_ref, sems, first):
    tokens, width = value_ref.shape[0], value_ref.shape[1] // 2
    core = lax.axis_index("dp")
    copies = []
    for place, (half, target) in enumerate(((core, own_ref), (1 - core, other_ref))):
        columns = pl.ds(pl.multiple_of(half * width, 128), width)
        copies.append(
            pltpu.make_async_copy(
                value_ref.at[:, columns], target.at[0:tokens], sems.at[first + place]
            )
        )
    for copy in copies:
        copy.start()
    return copies


def pack_kernel(f_ref, *refs):
    sources, (own, other, packed, sems), held = refs[:4], refs[4:8], refs[8:]
    tokens = f_ref.shape[0]
    small = [
        pltpu.make_async_copy(source, target, sems.at[2 + place])
        for place, (source, target) in enumerate(zip(sources, held))
    ]
    for copy in small:
        copy.start()
    copies = halves(f_ref, own, other, sems, 0)
    packed[...] = jnp.zeros_like(packed)
    for copy in small:
        copy.wait()
    for start, ids, route in ((0, *held[:2]), (META // 2, *held[2:])):
        packed[start : start + 2, 0:tokens] = ids[...].astype(F32)
        rest = route[...]
        for piece in range(3):
            top = rest.astype(BF16).astype(F32)
            row = start + 2 + 2 * piece
            packed[row : row + 2, 0:tokens] = top
            rest = rest - top
    mine = packed[...]
    lanes = packed.shape[1]
    own[tokens : tokens + META, 0:lanes] = mine.astype(BF16)
    other[tokens : tokens + META, 0:lanes] = pltpu.roll(mine, tokens, 1).astype(BF16)
    for copy in copies:
        copy.wait()


def pack(f, *small):
    tokens, width = f.shape[0], f.shape[1] // 2
    return call(
        pack_kernel,
        [array(tokens + META, width)] * 2,
        [HBM] * 5,
        [VMEM] * 2,
        [pltpu.VMEM((META, 2 * tokens), F32), pltpu.SemaphoreType.DMA((6,))]
        + [pltpu.VMEM(value.shape, value.dtype) for value in small],
    )(f, *small)


def cut_kernel(x_ref, dy_ref, *refs):
    own_x, own_dy, other, sems = refs[-4:]
    tokens = x_ref.shape[0]
    copies = halves(x_ref, own_x, other.at[0:tokens], sems, 0)
    copies += halves(dy_ref, own_dy, other.at[tokens : 2 * tokens], sems, 2)
    for copy in copies:
        copy.wait()


def cut(x, dy, after):
    tokens, width = x.shape[0], x.shape[1] // 2
    return call(
        cut_kernel,
        [array(tokens, width)] * 2 + [array(2 * tokens, width)],
        [HBM] * 2 + [AFTER] * len(after),
        [VMEM] * 3,
        [pltpu.SemaphoreType.DMA((4,))],
    )(x, dy, *after)


def load_kernel(*refs, count):
    sources, targets, sems = refs[:count], refs[-count - 1 : -1], refs[-1]
    copies = [
        pltpu.make_async_copy(source, target, sems.at[place])
        for place, (source, target) in enumerate(zip(sources, targets))
    ]
    for copy in copies:
        copy.start()
    for copy in copies:
        copy.wait()


def load(weights, after):
    return call(
        functools.partial(load_kernel, count=len(weights)),
        [array(*weight.shape) for weight in weights],
        [HBM] * len(weights) + [AFTER] * len(after),
        [VMEM] * len(weights),
        [pltpu.SemaphoreType.DMA((len(weights),))],
    )(*weights, *after)


class Plan:
    def __init__(self, blocks, part, group, tokens, relative):
        self.blocks, self.part, self.group = blocks, part, group
        self.tokens, self.relative = tokens, relative


def slot_rows(own_meta, other_meta, plan, first_row):
    lanes = 2 * plan.tokens
    padded = max(8, plan.blocks)
    me = lax.axis_index("expert") if plan.relative else 0
    meta = own_meta[plan.tokens : plan.tokens + META, 0:lanes].astype(F32)
    meta = meta + other_meta[plan.tokens : plan.tokens + META, 0:lanes].astype(F32)
    meta = meta[first_row : first_row + META // 2]
    first, second = meta[0:1], meta[1:2]
    route = meta[2:4] + meta[4:6] + meta[6:8]
    row = lax.broadcasted_iota(jnp.int32, (padded, lanes), 0)
    expert = ((row ^ me) // plan.group).astype(F32)
    is_first, is_second = expert == first, expert == second
    named = jnp.where(is_first | is_second, 1.0, 0.0)
    before = lax.broadcasted_iota(jnp.int32, (lanes, lanes), 0)
    after = lax.broadcasted_iota(jnp.int32, (lanes, lanes), 1)
    earlier = (before < after) & ((before < plan.tokens) == (after < plan.tokens))
    position = dot(named.astype(BF16), jnp.where(earlier, 1.0, 0.0).astype(BF16), 1, 0)
    lane = lax.broadcasted_iota(jnp.int32, (padded, lanes), 1)
    slot = position + jnp.where(lane < plan.tokens, 0, plan.part).astype(F32)
    slot = jnp.where(named > 0.5, slot, -1.0)
    return slot, jnp.where(is_first, route[0:1], route[1:2])


def slot_table(slot, block, first, rows):
    index = lax.broadcasted_iota(jnp.int32, (rows, slot.shape[1]), 0) + first
    index = index.astype(F32)
    return jnp.where(index == slot[block : block + 1, :], 1.0, 0.0)


def dispatch_kernel(
    own_meta, other_meta, own_ref, other_ref, *refs, plan, first_row, other_row, weighted, passed
):
    outs = refs[len(refs) - plan.blocks - passed : len(refs) - passed]
    width, tokens = outs[0].shape[1], plan.tokens
    slot, route = slot_rows(own_meta, other_meta, plan, first_row)
    values = jnp.concatenate([own_ref[0:tokens, :], other_ref[other_row : other_row + tokens, :]], axis=0)
    for block in range(plan.blocks):
        table = slot_table(slot, block, 0, 2 * plan.part)
        if weighted:
            scale = jnp.sum(table * route[block : block + 1, :], axis=1, keepdims=True)
        table = table.astype(BF16)
        for start in range(0, width, TILE):
            picked = dot(table, values[:, start : start + TILE], 1, 0)
            if weighted:
                picked = picked * scale
            outs[block][:, start : start + TILE] = picked.astype(BF16)


def dispatch(metas, own, other, plan, first_row, other_row, weighted, after=(), passing=()):
    width = own.shape[1]
    return call(
        functools.partial(
            dispatch_kernel,
            plan=plan,
            first_row=first_row,
            other_row=other_row,
            weighted=weighted,
            passed=len(passing),
        ),
        [array(2 * plan.part, width)] * plan.blocks + [array(*value.shape) for value in passing],
        [VMEM] * (4 + len(passing)) + [AFTER] * len(after),
        [VMEM] * (plan.blocks + len(passing)),
        [],
        aliases={4 + place: plan.blocks + place for place in range(len(passing))},
    )(*metas, own, other, *passing, *after)


def combine_kernel(own_meta, other_meta, *refs, plan, first_row, weighted, other):
    returned, out = refs[: plan.blocks], refs[-1]
    width, tokens = out.shape[1], plan.tokens
    slot, route = slot_rows(own_meta, other_meta, plan, first_row)
    table = []
    for block in range(plan.blocks):
        table.append(slot_table(slot, block, plan.part if other else 0, plan.part))
        if weighted:
            table[block] = table[block] * route[block : block + 1, :]
    table = jnp.concatenate(table, axis=0)
    high = table.astype(BF16)
    low = (table - high.astype(F32)).astype(BF16)
    for start in range(0, width, TILE):
        part = slice(start, start + TILE)
        values = jnp.concatenate([ref[:, part].astype(F32) for ref in returned], axis=0)
        values = values.astype(BF16)
        total = dot(high, values, 0, 0)
        if weighted:
            total += dot(low, values, 0, 0)
        out[:, part] = total[tokens if other else 0 :][:tokens].astype(BF16)


def combine(metas, returned, plan, first_row, weighted, other, after=(), weight=1):
    return call(
        functools.partial(
            combine_kernel, plan=plan, first_row=first_row, weighted=weighted, other=other
        ),
        array(plan.tokens, returned[0].shape[1]),
        [VMEM] * (2 + plan.blocks) + [AFTER] * len(after),
        VMEM,
        [],
        weight=weight,
    )(*metas, *returned, *after)


def joined(refs):
    return jnp.concatenate([ref[...] for ref in refs], axis=0)


def gate_up_kernel(*refs, blocks):
    gate_w, up_w = refs[blocks : blocks + 2]
    out, rows = refs[-2:]
    rows[...] = joined(refs[:blocks])
    for start in range(0, out.shape[2], TILE):
        part = slice(start, start + TILE)
        out[0, :, part] = dot(rows[...], gate_w[:, part], 1, 0).astype(BF16)
        out[1, :, part] = dot(rows[...], up_w[:, part], 1, 0).astype(BF16)


def gate_up(inputs, gate_w, up_w, planes=2, after=(), weight=1):
    blocks, (rows, width) = len(inputs), inputs[0].shape
    units, total = gate_w.shape[1], blocks * rows
    return call(
        functools.partial(gate_up_kernel, blocks=blocks),
        array(planes, total, units),
        [VMEM] * (blocks + 2) + [AFTER] * len(after),
        VMEM,
        [pltpu.VMEM((total, width), BF16)],
        weight=weight,
    )(*inputs, gate_w, up_w, *after)


def d_hidden_kernel(*refs, blocks):
    down_w = refs[blocks]
    rows, out = refs[-2:]
    rows[...] = joined(refs[:blocks])
    for start in range(0, out.shape[2], TILE):
        part = slice(start, start + TILE)
        out[2, :, part] = dot(rows[...], down_w[part, :], 1, 1).astype(BF16)


def d_hidden(inputs, down_w, partial, after=(), weight=1):
    blocks, (rows, width) = len(inputs), inputs[0].shape
    return call(
        functools.partial(d_hidden_kernel, blocks=blocks),
        [array(blocks * rows, width), array(*partial.shape)],
        [VMEM] * (blocks + 2) + [AFTER] * len(after),
        [VMEM] * 2,
        [],
        weight=weight,
        aliases={blocks + 1: 1},
    )(*inputs, down_w, partial, *after)


def scatter_tile(value, outs, columns):
    blocks, part = len(outs) // 2, outs[0].shape[0]
    for place, out in enumerate(outs):
        first = (2 * (place % blocks) + place // blocks) * part
        out[:, columns] = value[first : first + part].astype(BF16)


def total_of(own, other, part):
    own, other = own.astype(F32), other.astype(F32)
    rows = own.shape[0]
    turned = []
    for first in range(0, rows, 2 * part):
        turned += [other[first + part : first + 2 * part], other[first : first + part]]
    return own + jnp.concatenate(turned, axis=0)


def down_kernel(own_ref, other_ref, down_w, *refs, blocks):
    outs, hidden = refs[-1 - 2 * blocks : -1], refs[-1]
    part = outs[0].shape[0]
    for start in range(0, hidden.shape[1], TILE):
        columns = slice(start, start + TILE)
        gate = total_of(own_ref[0, :, columns], other_ref[0, :, columns], part)
        up = total_of(own_ref[1, :, columns], other_ref[1, :, columns], part)
        hidden[:, columns] = (gate * jax.nn.sigmoid(gate) * up).astype(BF16)
    for start in range(0, outs[0].shape[1], TILE):
        columns = slice(start, start + TILE)
        scatter_tile(dot(hidden[...], down_w[:, columns], 1, 0), outs, columns)


def down(own, other, down_w, plan, after=()):
    _, total, units = own.shape
    return call(
        functools.partial(down_kernel, blocks=plan.blocks),
        [array(plan.part, down_w.shape[1])] * (2 * plan.blocks),
        [VMEM] * 3 + [AFTER] * len(after),
        [VMEM] * (2 * plan.blocks),
        [pltpu.VMEM((total, units), BF16)],
    )(own, other, down_w, *after)


def back_kernel(own_ref, other_ref, gate_w, up_w, *refs, blocks):
    hidden, d_gate, d_up, *outs = refs[-3 - 2 * blocks :]
    part = outs[0].shape[0]
    for start in range(0, hidden.shape[1], TILE):
        columns = slice(start, start + TILE)
        gate = total_of(own_ref[0, :, columns], other_ref[0, :, columns], part)
        up = total_of(own_ref[1, :, columns], other_ref[1, :, columns], part)
        d_hid = total_of(own_ref[2, :, columns], other_ref[2, :, columns], part)
        sigmoid = jax.nn.sigmoid(gate)
        activated = gate * sigmoid
        hidden[:, columns] = (activated * up).astype(BF16)
        d_up[:, columns] = (d_hid * activated).astype(BF16)
        d_gate[:, columns] = (
            d_hid * up * sigmoid * (1.0 + gate * (1.0 - sigmoid))
        ).astype(BF16)
    for start in range(0, outs[0].shape[1], TILE):
        columns = slice(start, start + TILE)
        total = dot(d_gate[...], gate_w[columns, :], 1, 1)
        total += dot(d_up[...], up_w[columns, :], 1, 1)
        scatter_tile(total, outs, columns)


def back(own, other, gate_w, up_w, plan, after=()):
    _, total, units = own.shape
    return call(
        functools.partial(back_kernel, blocks=plan.blocks),
        [array(total, units)] * 3 + [array(plan.part, gate_w.shape[0])] * (2 * plan.blocks),
        [VMEM] * 4 + [AFTER] * len(after),
        [VMEM] * (3 + 2 * plan.blocks),
        [],
    )(own, other, gate_w, up_w, *after)


def turn_kernel(*refs, blocks):
    inputs, turned = refs[:blocks], refs[-1]
    for start in range(0, turned.shape[0], TILE):
        part = slice(start, start + TILE)
        turned[part, :] = jnp.concatenate([ref[:, part] for ref in inputs], axis=0).T


def turn(inputs, after=()):
    blocks, (rows, width) = len(inputs), inputs[0].shape
    return call(
        functools.partial(turn_kernel, blocks=blocks),
        array(width, blocks * rows),
        [VMEM] * blocks + [AFTER] * len(after),
        VMEM,
        [],
    )(*inputs, *after)


def grad_kernel(hidden, d_gate, d_up, turned, cots, *refs):
    grad_gate, grad_up, grad_down = refs[-3:]
    part = pl.ds(pl.multiple_of(pl.program_id(0) * TILE, TILE), TILE)
    grad_gate[...] = dot(turned[...], d_gate[:, part], 1, 0).astype(BF16)
    grad_up[...] = dot(turned[...], d_up[:, part], 1, 0).astype(BF16)
    grad_down[...] = dot(hidden[:, part], cots[...], 0, 0).astype(BF16)


def grads(hidden, d_gate, d_up, turned, cots, after=(), weight=1):
    width, units = turned.shape[0], d_gate.shape[1]
    by_column = pl.BlockSpec((width, TILE), lambda i: (0, i))
    return call(
        grad_kernel,
        [pltpu.HBM((width, units), BF16)] * 2 + [pltpu.HBM((units, width), BF16)],
        [VMEM] * 5 + [AFTER] * len(after),
        [by_column, by_column, pl.BlockSpec((TILE, width), lambda i: (i, 0))],
        [],
        grid=(units // TILE,),
        weight=weight,
    )(hidden, d_gate, d_up, turned, cots, *after)


def to_experts(blocks, relative):
    if not relative:
        stacked = lax.all_to_all(jnp.stack(blocks), "expert", split_axis=0, concat_axis=0)
        return [stacked[block] for block in range(len(blocks))]
    return [blocks[0]] + [
        exchange(block, "expert", mask) for mask, block in enumerate(blocks) if mask > 0
    ]


def finish_kernel(*refs):
    sources, outs, sems = refs[:4], refs[-3:-1], refs[-1]
    width = sources[0].shape[1]
    core = lax.axis_index("dp")
    copies = []
    for place, source in enumerate(sources):
        half = core if place % 2 == 0 else 1 - core
        columns = pl.ds(pl.multiple_of(half * width, 128), width)
        copies.append(
            pltpu.make_async_copy(source, outs[place // 2].at[:, columns], sems.at[place])
        )
    for copy in copies:
        copy.start()
    for copy in copies:
        copy.wait()


def finish(y_mine, y_rest, dx_mine, dx_rest, after):
    tokens, width = y_mine.shape
    return call(
        finish_kernel,
        [pltpu.HBM((tokens, 2 * width), BF16)] * 2,
        [VMEM] * 4 + [AFTER] * len(after),
        [HBM] * 2,
        [pltpu.SemaphoreType.DMA((4,))],
    )(y_mine, y_rest, dx_mine, dx_rest, *after)


def local(x_fwd, ids_fwd, route_fwd, x_bwd, ids_bwd, route_bwd, dy_bwd, w_gate, w_up, w_down):
    n_expert = lax.axis_size("expert")
    slab_width = w_gate.shape[-1]
    group = FF // slab_width
    experts = n_expert // group
    tokens = x_fwd.shape[1]
    spread = 4 * experts * group
    capacity = group * ((5 * tokens * TOP + spread - 1) // spread)
    relative = n_expert <= 8
    plan = Plan(n_expert, (capacity + 7) // 8 * 8, group, tokens, relative)
    row_b, row_f = 0, META // 2

    own_f, send_f = pack(
        in_hbm(x_fwd[0]),
        *[in_hbm(value[0].T) for value in (ids_bwd, route_bwd, ids_fwd, route_fwd)],
    )
    other_f = exchange(send_f, "dp", 1)
    own_x, own_dy, send_rest = cut(in_hbm(x_bwd[0]), in_hbm(dy_bwd[0]), after=(own_f,))
    metas = (own_f, other_f)
    *sent_f, send_rest = dispatch(
        metas, own_f, other_f, plan, row_f, 0, False, passing=(send_rest,)
    )
    rows_f = to_experts(sent_f, relative)
    other_rest = exchange(send_rest, "dp", 1)
    sent_x = dispatch(metas, own_x, other_rest, plan, row_b, 0, False)
    rows_b = to_experts(sent_x, relative)
    gate_w, up_w, down_w = load(
        [in_hbm(weight[0, 0]) for weight in (w_gate, w_up, w_down)], after=sent_x[:1]
    )
    sent_dy = dispatch(
        metas, own_dy, other_rest, plan, row_b, tokens, True, after=(in_vmem(down_w),)
    )
    cots_b = to_experts(sent_dy, relative)

    part_f = gate_up(rows_f, gate_w, up_w, after=sent_dy[:1])
    part_f_other = exchange(part_f, "dp", 1)
    part_b = gate_up(rows_b, gate_w, up_w, planes=3, after=(part_f,), weight=3000)
    down_blocks = down(part_f, part_f_other, down_w, plan, after=(in_vmem(part_b),))
    own_back_f = to_experts(down_blocks[:n_expert], relative)
    other_back_f = to_experts(down_blocks[n_expert:], relative)
    turned = turn(rows_b, after=down_blocks[:1])
    cots, part_b = d_hidden(cots_b, down_w, part_b, after=(in_vmem(turned),), weight=1000)
    part_b_other = exchange(part_b, "dp", 1)
    own_sum = combine(
        metas, own_back_f, plan, row_f, True, False, after=(in_vmem(part_b),), weight=2000
    )
    y_mine = section_shift(own_sum, 0)
    hidden, d_gate, d_up, *back_blocks = back(
        part_b, part_b_other, gate_w, up_w, plan, after=(own_sum,)
    )
    own_back_b = to_experts(back_blocks[:n_expert], relative)
    other_back_b = to_experts(back_blocks[n_expert:], relative)
    other_sum = combine(
        metas, other_back_f, plan, row_f, True, True, after=back_blocks[:1], weight=150
    )
    y_rest = section_shift(other_sum, 1)
    own_sum = combine(
        metas,
        own_back_b,
        plan,
        row_b,
        False,
        False,
        after=(other_sum,),
        weight=300,
    )
    dx_mine = section_shift(own_sum, 0)
    other_sum = combine(
        metas,
        other_back_b,
        plan,
        row_b,
        False,
        True,
        after=(own_sum, in_vmem(y_rest), in_vmem(y_mine)),
        weight=100,
    )
    dx_rest = section_shift(other_sum, 1)
    grad_g, grad_u, grad_d = grads(
        hidden, d_gate, d_up, turned, cots, after=(other_sum, in_vmem(dx_mine)), weight=100
    )
    y_next, dx_next = finish(y_mine, y_rest, dx_mine, dx_rest, after=(in_hbm(grad_g),))
    return (
        y_next[None],
        dx_next[None],
        grad_g[None, None],
        grad_u[None, None],
        grad_d[None, None],
    )


def solution(mesh):
    rows = P("section", ("expert", "dp"), None)
    by_feature = P("section", "expert", "dp", None)
    down_spec = P("section", "expert", None, "dp")
    return jax.shard_map(
        local,
        mesh=mesh,
        in_specs=(rows,) * 7 + (by_feature, by_feature, down_spec),
        out_specs=(rows, rows, by_feature, by_feature, down_spec),
        check_vma=False,
    )
```

```python
import functools

import jax
import jax.numpy as jnp
from jax import lax
from jax.experimental import pallas as pl
from jax.experimental.pallas import tpu as pltpu
from jax.sharding import PartitionSpec as P

FF = 1024
TOP = 2
TILE = 256
VMEM_LIMIT = 20 * 1024 * 1024
META = 16
COST = 10**7
F32 = jnp.float32
BF16 = jnp.bfloat16


def exchange(value, axis, mask):
    count = lax.axis_size(axis)
    return lax.ppermute(value, axis, [(source, source ^ mask) for source in range(count)])


def section_shift(value, flip):
    sections, cores = lax.axis_size("section"), lax.axis_size("dp")
    pairs = []
    for section in range(sections):
        for core in range(cores):
            target = ((section + 1) % sections) * cores + (core ^ flip)
            pairs.append((section * cores + core, target))
    return lax.ppermute(value, ("section", "dp"), pairs)


def dot(left, right, left_dim, right_dim):
    return lax.dot_general(
        left, right, (((left_dim,), (right_dim,)), ((), ())), preferred_element_type=F32
    )


VMEM = pl.BlockSpec(memory_space=pltpu.VMEM)
HBM = pl.BlockSpec(memory_space=pltpu.HBM)
AFTER = pl.BlockSpec(memory_space=pl.ANY)


def call(kernel, out_shape, in_specs, out_specs, scratch, grid=(), weight=1, aliases={}):
    return pl.pallas_call(
        kernel,
        out_shape=out_shape,
        grid=grid,
        in_specs=in_specs,
        out_specs=out_specs,
        scratch_shapes=scratch,
        input_output_aliases=aliases,
        compiler_params=pltpu.CompilerParams(vmem_limit_bytes=VMEM_LIMIT),
        cost_estimate=pl.CostEstimate(
            flops=weight * COST, bytes_accessed=1, transcendentals=0
        ),
    )


def array(*shape):
    return jax.ShapeDtypeStruct(shape, BF16)


def in_vmem(value):
    return pltpu.with_memory_space_constraint(value, pltpu.VMEM)


def in_hbm(value):
    return pltpu.with_memory_space_constraint(value, pltpu.HBM)


def halves(value_ref, own_ref, other_ref, sems, first):
    tokens, width = value_ref.shape[0], value_ref.shape[1] // 2
    core = lax.axis_index("dp")
    copies = []
    for place, (half, target) in enumerate(((core, own_ref), (1 - core, other_ref))):
        columns = pl.ds(pl.multiple_of(half * width, 128), width)
        copies.append(
            pltpu.make_async_copy(
                value_ref.at[:, columns], target.at[0:tokens], sems.at[first + place]
            )
        )
    for copy in copies:
        copy.start()
    return copies


def pack_kernel(f_ref, *refs):
    sources, (own, other, packed, sems), held = refs[:4], refs[4:8], refs[8:]
    tokens = f_ref.shape[0]
    small = [
        pltpu.make_async_copy(source, target, sems.at[2 + place])
        for place, (source, target) in enumerate(zip(sources, held))
    ]
    for copy in small:
        copy.start()
    copies = halves(f_ref, own, other, sems, 0)
    packed[...] = jnp.zeros_like(packed)
    for copy in small:
        copy.wait()
    for start, ids, route in ((0, *held[:2]), (META // 2, *held[2:])):
        packed[start : start + 2, 0:tokens] = ids[...].astype(F32)
        rest = route[...]
        for piece in range(3):
            top = rest.astype(BF16).astype(F32)
            row = start + 2 + 2 * piece
            packed[row : row + 2, 0:tokens] = top
            rest = rest - top
    mine = packed[...]
    lanes = packed.shape[1]
    own[tokens : tokens + META, 0:lanes] = mine.astype(BF16)
    other[tokens : tokens + META, 0:lanes] = pltpu.roll(mine, tokens, 1).astype(BF16)
    for copy in copies:
        copy.wait()


def pack(f, *small):
    tokens, width = f.shape[0], f.shape[1] // 2
    return call(
        pack_kernel,
        [array(tokens + META, width)] * 2,
        [HBM] * 5,
        [VMEM] * 2,
        [pltpu.VMEM((META, 2 * tokens), F32), pltpu.SemaphoreType.DMA((6,))]
        + [pltpu.VMEM(value.shape, value.dtype) for value in small],
    )(f, *small)


def cut_kernel(x_ref, dy_ref, *refs):
    own_x, own_dy, other, sems = refs[-4:]
    tokens = x_ref.shape[0]
    copies = halves(x_ref, own_x, other.at[0:tokens], sems, 0)
    copies += halves(dy_ref, own_dy, other.at[tokens : 2 * tokens], sems, 2)
    for copy in copies:
        copy.wait()


def cut(x, dy, after):
    tokens, width = x.shape[0], x.shape[1] // 2
    return call(
        cut_kernel,
        [array(tokens, width)] * 2 + [array(2 * tokens, width)],
        [HBM] * 2 + [AFTER] * len(after),
        [VMEM] * 3,
        [pltpu.SemaphoreType.DMA((4,))],
    )(x, dy, *after)


def load_kernel(*refs, count):
    sources, targets, sems = refs[:count], refs[-count - 1 : -1], refs[-1]
    copies = [
        pltpu.make_async_copy(source, target, sems.at[place])
        for place, (source, target) in enumerate(zip(sources, targets))
    ]
    for copy in copies:
        copy.start()
    for copy in copies:
        copy.wait()


def load(weights, after):
    return call(
        functools.partial(load_kernel, count=len(weights)),
        [array(*weight.shape) for weight in weights],
        [HBM] * len(weights) + [AFTER] * len(after),
        [VMEM] * len(weights),
        [pltpu.SemaphoreType.DMA((len(weights),))],
    )(*weights, *after)


class Plan:
    def __init__(self, blocks, part, group, tokens, relative):
        self.blocks, self.part, self.group = blocks, part, group
        self.tokens, self.relative = tokens, relative


def slot_rows(own_meta, other_meta, plan, first_row):
    lanes = 2 * plan.tokens
    padded = max(8, plan.blocks)
    me = lax.axis_index("expert") if plan.relative else 0
    meta = own_meta[plan.tokens : plan.tokens + META, 0:lanes].astype(F32)
    meta = meta + other_meta[plan.tokens : plan.tokens + META, 0:lanes].astype(F32)
    meta = meta[first_row : first_row + META // 2]
    first, second = meta[0:1], meta[1:2]
    route = meta[2:4] + meta[4:6] + meta[6:8]
    row = lax.broadcasted_iota(jnp.int32, (padded, lanes), 0)
    expert = ((row ^ me) // plan.group).astype(F32)
    is_first, is_second = expert == first, expert == second
    named = jnp.where(is_first | is_second, 1.0, 0.0)
    before = lax.broadcasted_iota(jnp.int32, (lanes, lanes), 0)
    after = lax.broadcasted_iota(jnp.int32, (lanes, lanes), 1)
    earlier = (before < after) & ((before < plan.tokens) == (after < plan.tokens))
    position = dot(named.astype(BF16), jnp.where(earlier, 1.0, 0.0).astype(BF16), 1, 0)
    lane = lax.broadcasted_iota(jnp.int32, (padded, lanes), 1)
    slot = position + jnp.where(lane < plan.tokens, 0, plan.part).astype(F32)
    slot = jnp.where(named > 0.5, slot, -1.0)
    return slot, jnp.where(is_first, route[0:1], route[1:2])


def slot_table(slot, block, first, rows):
    index = lax.broadcasted_iota(jnp.int32, (rows, slot.shape[1]), 0) + first
    index = index.astype(F32)
    return jnp.where(index == slot[block : block + 1, :], 1.0, 0.0)


def dispatch_kernel(
    own_meta, other_meta, own_ref, other_ref, *refs, plan, first_row, other_row, weighted, passed
):
    outs = refs[len(refs) - plan.blocks - passed : len(refs) - passed]
    width, tokens = outs[0].shape[1], plan.tokens
    slot, route = slot_rows(own_meta, other_meta, plan, first_row)
    values = jnp.concatenate([own_ref[0:tokens, :], other_ref[other_row : other_row + tokens, :]], axis=0)
    for block in range(plan.blocks):
        table = slot_table(slot, block, 0, 2 * plan.part)
        if weighted:
            scale = jnp.sum(table * route[block : block + 1, :], axis=1, keepdims=True)
        table = table.astype(BF16)
        for start in range(0, width, TILE):
            picked = dot(table, values[:, start : start + TILE], 1, 0)
            if weighted:
                picked = picked * scale
            outs[block][:, start : start + TILE] = picked.astype(BF16)


def dispatch(metas, own, other, plan, first_row, other_row, weighted, after=(), passing=()):
    width = own.shape[1]
    return call(
        functools.partial(
            dispatch_kernel,
            plan=plan,
            first_row=first_row,
            other_row=other_row,
            weighted=weighted,
            passed=len(passing),
        ),
        [array(2 * plan.part, width)] * plan.blocks + [array(*value.shape) for value in passing],
        [VMEM] * (4 + len(passing)) + [AFTER] * len(after),
        [VMEM] * (plan.blocks + len(passing)),
        [],
        aliases={4 + place: plan.blocks + place for place in range(len(passing))},
    )(*metas, own, other, *passing, *after)


def combine_kernel(own_meta, other_meta, *refs, plan, first_row, weighted, other):
    returned, out = refs[: plan.blocks], refs[-1]
    width, tokens = out.shape[1], plan.tokens
    slot, route = slot_rows(own_meta, other_meta, plan, first_row)
    table = []
    for block in range(plan.blocks):
        table.append(slot_table(slot, block, plan.part if other else 0, plan.part))
        if weighted:
            table[block] = table[block] * route[block : block + 1, :]
    table = jnp.concatenate(table, axis=0)
    high = table.astype(BF16)
    low = (table - high.astype(F32)).astype(BF16)
    for start in range(0, width, TILE):
        part = slice(start, start + TILE)
        values = jnp.concatenate([ref[:, part].astype(F32) for ref in returned], axis=0)
        values = values.astype(BF16)
        total = dot(high, values, 0, 0)
        if weighted:
            total += dot(low, values, 0, 0)
        out[:, part] = total[tokens if other else 0 :][:tokens].astype(BF16)


def combine(metas, returned, plan, first_row, weighted, other, after=(), weight=1):
    return call(
        functools.partial(
            combine_kernel, plan=plan, first_row=first_row, weighted=weighted, other=other
        ),
        array(plan.tokens, returned[0].shape[1]),
        [VMEM] * (2 + plan.blocks) + [AFTER] * len(after),
        VMEM,
        [],
        weight=weight,
    )(*metas, *returned, *after)


def joined(refs):
    return jnp.concatenate([ref[...] for ref in refs], axis=0)


def gate_up_kernel(*refs, blocks):
    gate_w, up_w = refs[blocks : blocks + 2]
    out, rows = refs[-2:]
    rows[...] = joined(refs[:blocks])
    for start in range(0, out.shape[2], TILE):
        part = slice(start, start + TILE)
        out[0, :, part] = dot(rows[...], gate_w[:, part], 1, 0).astype(BF16)
        out[1, :, part] = dot(rows[...], up_w[:, part], 1, 0).astype(BF16)


def gate_up(inputs, gate_w, up_w, planes=2, after=(), weight=1):
    blocks, (rows, width) = len(inputs), inputs[0].shape
    units, total = gate_w.shape[1], blocks * rows
    return call(
        functools.partial(gate_up_kernel, blocks=blocks),
        array(planes, total, units),
        [VMEM] * (blocks + 2) + [AFTER] * len(after),
        VMEM,
        [pltpu.VMEM((total, width), BF16)],
        weight=weight,
    )(*inputs, gate_w, up_w, *after)


def d_hidden_kernel(*refs, blocks):
    down_w = refs[blocks]
    rows, out = refs[-2:]
    rows[...] = joined(refs[:blocks])
    for start in range(0, out.shape[2], TILE):
        part = slice(start, start + TILE)
        out[2, :, part] = dot(rows[...], down_w[part, :], 1, 1).astype(BF16)


def d_hidden(inputs, down_w, partial, after=(), weight=1):
    blocks, (rows, width) = len(inputs), inputs[0].shape
    return call(
        functools.partial(d_hidden_kernel, blocks=blocks),
        [array(blocks * rows, width), array(*partial.shape)],
        [VMEM] * (blocks + 2) + [AFTER] * len(after),
        [VMEM] * 2,
        [],
        weight=weight,
        aliases={blocks + 1: 1},
    )(*inputs, down_w, partial, *after)


def scatter_tile(value, outs, columns):
    blocks, part = len(outs) // 2, outs[0].shape[0]
    for place, out in enumerate(outs):
        first = (2 * (place % blocks) + place // blocks) * part
        out[:, columns] = value[first : first + part].astype(BF16)


def total_of(own, other, part):
    own, other = own.astype(F32), other.astype(F32)
    rows = own.shape[0]
    turned = []
    for first in range(0, rows, 2 * part):
        turned += [other[first + part : first + 2 * part], other[first : first + part]]
    return own + jnp.concatenate(turned, axis=0)


def down_kernel(own_ref, other_ref, down_w, *refs, blocks):
    outs, hidden = refs[-1 - 2 * blocks : -1], refs[-1]
    part = outs[0].shape[0]
    for start in range(0, hidden.shape[1], TILE):
        columns = slice(start, start + TILE)
        gate = total_of(own_ref[0, :, columns], other_ref[0, :, columns], part)
        up = total_of(own_ref[1, :, columns], other_ref[1, :, columns], part)
        hidden[:, columns] = (gate * jax.nn.sigmoid(gate) * up).astype(BF16)
    for start in range(0, outs[0].shape[1], TILE):
        columns = slice(start, start + TILE)
        scatter_tile(dot(hidden[...], down_w[:, columns], 1, 0), outs, columns)


def down(own, other, down_w, plan, after=()):
    _, total, units = own.shape
    return call(
        functools.partial(down_kernel, blocks=plan.blocks),
        [array(plan.part, down_w.shape[1])] * (2 * plan.blocks),
        [VMEM] * 3 + [AFTER] * len(after),
        [VMEM] * (2 * plan.blocks),
        [pltpu.VMEM((total, units), BF16)],
    )(own, other, down_w, *after)


def back_kernel(own_ref, other_ref, gate_w, up_w, *refs, blocks):
    hidden, d_gate, d_up, *outs = refs[-3 - 2 * blocks :]
    part = outs[0].shape[0]
    for start in range(0, hidden.shape[1], TILE):
        columns = slice(start, start + TILE)
        gate = total_of(own_ref[0, :, columns], other_ref[0, :, columns], part)
        up = total_of(own_ref[1, :, columns], other_ref[1, :, columns], part)
        d_hid = total_of(own_ref[2, :, columns], other_ref[2, :, columns], part)
        sigmoid = jax.nn.sigmoid(gate)
        activated = gate * sigmoid
        hidden[:, columns] = (activated * up).astype(BF16)
        d_up[:, columns] = (d_hid * activated).astype(BF16)
        d_gate[:, columns] = (
            d_hid * up * sigmoid * (1.0 + gate * (1.0 - sigmoid))
        ).astype(BF16)
    for start in range(0, outs[0].shape[1], TILE):
        columns = slice(start, start + TILE)
        total = dot(d_gate[...], gate_w[columns, :], 1, 1)
        total += dot(d_up[...], up_w[columns, :], 1, 1)
        scatter_tile(total, outs, columns)


def back(own, other, gate_w, up_w, plan, after=()):
    _, total, units = own.shape
    return call(
        functools.partial(back_kernel, blocks=plan.blocks),
        [array(total, units)] * 3 + [array(plan.part, gate_w.shape[0])] * (2 * plan.blocks),
        [VMEM] * 4 + [AFTER] * len(after),
        [VMEM] * (3 + 2 * plan.blocks),
        [],
    )(own, other, gate_w, up_w, *after)


def turn_kernel(*refs, blocks):
    inputs, turned = refs[:blocks], refs[-1]
    for start in range(0, turned.shape[0], TILE):
        part = slice(start, start + TILE)
        turned[part, :] = jnp.concatenate([ref[:, part] for ref in inputs], axis=0).T


def turn(inputs, after=()):
    blocks, (rows, width) = len(inputs), inputs[0].shape
    return call(
        functools.partial(turn_kernel, blocks=blocks),
        array(width, blocks * rows),
        [VMEM] * blocks + [AFTER] * len(after),
        VMEM,
        [],
    )(*inputs, *after)


def grad_in_kernel(d_gate, d_up, turned, *refs):
    grad_gate, grad_up = refs[-2:]
    part = pl.ds(pl.multiple_of(pl.program_id(0) * TILE, TILE), TILE)
    grad_gate[...] = dot(turned[...], d_gate[:, part], 1, 0).astype(BF16)
    grad_up[...] = dot(turned[...], d_up[:, part], 1, 0).astype(BF16)


def grad_in(d_gate, d_up, turned, after=(), weight=1):
    width, units = turned.shape[0], d_gate.shape[1]
    return call(
        grad_in_kernel,
        [pltpu.HBM((width, units), BF16)] * 2,
        [VMEM] * 3 + [AFTER] * len(after),
        [pl.BlockSpec((width, TILE), lambda i: (0, i))] * 2,
        [],
        grid=(units // TILE,),
        weight=weight,
    )(d_gate, d_up, turned, *after)


def grad_down_kernel(hidden, cots, *refs):
    part = pl.ds(pl.multiple_of(pl.program_id(0) * TILE, TILE), TILE)
    refs[-1][...] = dot(hidden[:, part], cots[...], 0, 0).astype(BF16)


def grad_down(hidden, cots, after=(), weight=1):
    units, width = hidden.shape[1], cots.shape[1]
    return call(
        grad_down_kernel,
        pltpu.HBM((units, width), BF16),
        [VMEM] * 2 + [AFTER] * len(after),
        pl.BlockSpec((TILE, width), lambda i: (i, 0)),
        [],
        grid=(units // TILE,),
        weight=weight,
    )(hidden, cots, *after)


def to_experts(blocks, relative):
    if not relative:
        stacked = lax.all_to_all(jnp.stack(blocks), "expert", split_axis=0, concat_axis=0)
        return [stacked[block] for block in range(len(blocks))]
    return [blocks[0]] + [
        exchange(block, "expert", mask) for mask, block in enumerate(blocks) if mask > 0
    ]


def place_kernel(*refs, halves_of, count):
    outs, sems = refs[-1 - count : -1], refs[-1]
    width = refs[0].shape[1]
    core = lax.axis_index("dp")
    copies = []
    for place, (out, own) in enumerate(halves_of):
        half = core if own else 1 - core
        columns = pl.ds(pl.multiple_of(half * width, 128), width)
        copies.append(
            pltpu.make_async_copy(refs[place], outs[out].at[:, columns], sems.at[place])
        )
    for copy in copies:
        copy.start()
    for copy in copies:
        copy.wait()


def placed(sources, halves_of, count, into=(), after=()):
    tokens, width = sources[0].shape
    return call(
        functools.partial(place_kernel, halves_of=halves_of, count=count),
        [pltpu.HBM((tokens, 2 * width), BF16)] * count,
        [VMEM] * len(sources) + [HBM] * len(into) + [AFTER] * len(after),
        [HBM] * count,
        [pltpu.SemaphoreType.DMA((len(sources),))],
        aliases={len(sources) + place: place for place in range(len(into))},
    )(*sources, *[in_hbm(value) for value in into], *after)


def local(x_fwd, ids_fwd, route_fwd, x_bwd, ids_bwd, route_bwd, dy_bwd, w_gate, w_up, w_down):
    n_expert = lax.axis_size("expert")
    slab_width = w_gate.shape[-1]
    group = FF // slab_width
    experts = n_expert // group
    tokens = x_fwd.shape[1]
    spread = 4 * experts * group
    capacity = group * ((5 * tokens * TOP + spread - 1) // spread)
    relative = n_expert <= 8
    plan = Plan(n_expert, (capacity + 7) // 8 * 8, group, tokens, relative)
    row_b, row_f = 0, META // 2

    own_f, send_f = pack(
        in_hbm(x_fwd[0]),
        *[in_hbm(value[0].T) for value in (ids_bwd, route_bwd, ids_fwd, route_fwd)],
    )
    other_f = exchange(send_f, "dp", 1)
    own_x, own_dy, send_rest = cut(in_hbm(x_bwd[0]), in_hbm(dy_bwd[0]), after=(own_f,))
    metas = (own_f, other_f)
    *sent_f, send_rest = dispatch(
        metas, own_f, other_f, plan, row_f, 0, False, passing=(send_rest,)
    )
    rows_f = to_experts(sent_f, relative)
    other_rest = exchange(send_rest, "dp", 1)
    sent_x = dispatch(metas, own_x, other_rest, plan, row_b, 0, False)
    rows_b = to_experts(sent_x, relative)
    gate_w, up_w, down_w = load(
        [in_hbm(weight[0, 0]) for weight in (w_gate, w_up, w_down)], after=sent_x[:1]
    )
    sent_dy = dispatch(
        metas, own_dy, other_rest, plan, row_b, tokens, True, after=(in_vmem(down_w),)
    )
    cots_b = to_experts(sent_dy, relative)

    part_f = gate_up(rows_f, gate_w, up_w, after=sent_dy[:1])
    part_f_other = exchange(part_f, "dp", 1)
    part_b = gate_up(rows_b, gate_w, up_w, planes=3, after=(part_f,), weight=3000)
    down_blocks = down(part_f, part_f_other, down_w, plan, after=(in_vmem(part_b),))
    own_back_f = to_experts(down_blocks[:n_expert], relative)
    other_back_f = to_experts(down_blocks[n_expert:], relative)
    turned = turn(rows_b, after=down_blocks[:1])
    cots, part_b = d_hidden(cots_b, down_w, part_b, after=(in_vmem(turned),), weight=1000)
    part_b_other = exchange(part_b, "dp", 1)
    own_sum = combine(
        metas, own_back_f, plan, row_f, True, False, after=(in_vmem(part_b),), weight=2000
    )
    y_mine = section_shift(own_sum, 0)
    hidden, d_gate, d_up, *back_blocks = back(
        part_b, part_b_other, gate_w, up_w, plan, after=(own_sum,)
    )
    own_back_b = to_experts(back_blocks[:n_expert], relative)
    other_back_b = to_experts(back_blocks[n_expert:], relative)
    other_sum = combine(
        metas, other_back_f, plan, row_f, True, True, after=back_blocks[:1], weight=150
    )
    y_rest = section_shift(other_sum, 1)
    own_sum = combine(
        metas,
        own_back_b,
        plan,
        row_b,
        False,
        False,
        after=(other_sum, in_vmem(y_mine)),
        weight=150,
    )
    dx_mine = section_shift(own_sum, 0)
    grad_d = grad_down(hidden, cots, after=(own_sum,))
    other_sum = combine(
        metas,
        other_back_b,
        plan,
        row_b,
        False,
        True,
        after=(in_hbm(grad_d), in_vmem(y_rest)),
        weight=100,
    )
    dx_rest = section_shift(other_sum, 1)
    grad_g, grad_u = grad_in(
        d_gate, d_up, turned, after=(other_sum, in_vmem(dx_mine)), weight=100
    )
    y_next, dx_next = placed(
        [y_mine, y_rest, dx_mine],
        ((0, True), (0, False), (1, True)),
        2,
        after=(in_hbm(grad_g),),
    )
    (dx_next,) = placed([dx_rest], ((0, False),), 1, into=(dx_next,))
    return (
        y_next[None],
        dx_next[None],
        grad_g[None, None],
        grad_u[None, None],
        grad_d[None, None],
    )


def solution(mesh):
    rows = P("section", ("expert", "dp"), None)
    by_feature = P("section", "expert", "dp", None)
    down_spec = P("section", "expert", None, "dp")
    return jax.shard_map(
        local,
        mesh=mesh,
        in_specs=(rows,) * 7 + (by_feature, by_feature, down_spec),
        out_specs=(rows, rows, by_feature, by_feature, down_spec),
        check_vma=False,
    )
```
